32 devices in a mesh: section: 2 (over x), dp: 16 (over z, y, core).
Axes of the slice: x: 2, y: 2, z: 4, core: 2. Of those that a mesh axis runs over, the one named last changes fastest.
Arguments:
- tokens: bfloat16 [8192, 1024], P('dp'), may hold values from -6 to 6
- qkv_weight: bfloat16 [2, 1024, 3072], P('section', 'dp'), may hold values from -0.1875 to 0.1875
- qkv_bias: bfloat16 [2, 3072], P('section', 'dp'), may hold values from -1.1953125 to 1.1953125
- out_weight: bfloat16 [2, 1024, 1024], P('section', 'dp'), may hold values from -0.5 to 0.5
- out_bias: bfloat16 [2, 1024], P('section', 'dp'), may hold values from -1.1953125 to 1.1953125
- norm1_gain: bfloat16 [2, 1024], P('section', 'dp'), may hold values from 0.5 to 1.5
- norm1_bias: bfloat16 [2, 1024], P('section', 'dp'), may hold values from -1.1953125 to 1.1953125
- up_weight: bfloat16 [2, 1024, 4096], P('section', 'dp'), may hold values from -0.1875 to 0.1875
- up_bias: bfloat16 [2, 4096], P('section', 'dp'), may hold values from -1.1953125 to 1.1953125
- down_weight: bfloat16 [2, 4096, 1024], P('section', 'dp'), may hold values from -0.09375 to 0.09375
- down_bias: bfloat16 [2, 1024], P('section', 'dp'), may hold values from -1.1953125 to 1.1953125
- norm2_gain: bfloat16 [2, 1024], P('section', 'dp'), may hold values from 0.5 to 1.5
- norm2_bias: bfloat16 [2, 1024], P('section', 'dp'), may hold values from -1.1953125 to 1.1953125
- proj_weight: bfloat16 [1024, 128], P('dp'), may hold values from -0.1875 to 0.1875
- doc_lengths: int32 [32, 3], P('dp'), may hold values from 1 to 96, 192 in all within a row
- pair_docs: int32 [64, 8], replicated, may hold values from 0 to 47
Outputs:
- query_losses: float32 [64], P('dp')
- activations: bfloat16 [2, 8192, 1024], P('section', 'dp')
- grad_inputs: float32 [2, 8192, 1024], P('section', 'dp')
- grad_qkv_weight: float32 [2, 1024, 3072], P('section', 'dp')
- grad_qkv_bias: float32 [2, 3072], P('section', 'dp')
- grad_out_weight: float32 [2, 1024, 1024], P('section', 'dp')
- grad_out_bias: float32 [2, 1024], P('section', 'dp')
- grad_norm1_gain: float32 [2, 1024], P('section', 'dp')
- grad_norm1_bias: float32 [2, 1024], P('section', 'dp')
- grad_up_weight: float32 [2, 1024, 4096], P('section', 'dp')
- grad_up_bias: float32 [2, 4096], P('section', 'dp')
- grad_down_weight: float32 [2, 4096, 1024], P('section', 'dp')
- grad_down_bias: float32 [2, 1024], P('section', 'dp')
- grad_norm2_gain: float32 [2, 1024], P('section', 'dp')
- grad_norm2_bias: float32 [2, 1024], P('section', 'dp')
- grad_proj_weight: float32 [1024, 128], P(('section', 'dp'))
The draws below stay inside these ranges and needn't reach their ends.
Inputs may be any that keep to these rules, and one draw needn't show every extreme that they name: `doc_lengths`: each row fills the 192 document rows of a block; its longest document has exactly 96 tokens.
All inputs are finite; a program needn't handle non-finite values.
Results may differ from the reference program's by a relative error of at most 0.019.
Values may be sent and summed in bfloat16 or wider, within the bound.
No kernel may reach another device: no remote copies, remote signals or barrier semaphores. Data moves between devices by JAX's collectives and lax.ppermute only.
A program may use at most 320 MiB of HBM per device.

```python
import math
import jax
import jax.numpy as jnp
import numpy as np
from jax import lax

D = 1024
HEADS = 16
HEAD = 64
FF = 4096
PROJ = 128
QLEN = 32
DOC_ROWS = 192
QRY_DEV = 2
DOCS_DEV = 3
MICRO = 2
CANDS = 8
ROWS = 256
BLOCKS = 32
TOKENS = 8192
QUERIES = 64
N_SECTION = 2
N_DP = 16


def touch_ends(drawn, rng, low, largest):
    shape = drawn.shape
    index_at = [jax.random.randint(jax.random.fold_in(rng, axis), (), 0, shape[axis]) for axis in range(len(shape))]
    drawn = drawn.at[tuple(index_at)].set(low)
    longest = shape.index(max(shape))
    index_at[longest] = (index_at[longest] + 1) % shape[longest]
    return drawn.at[tuple(index_at)].set(largest)


def block_scale(own_key, extent, cuts, least, largest):
    factor_of, own = 1.0, jax.random.fold_in(own_key, 6)
    for dim, blocks in cuts:
        draws = jnp.exp(jax.random.uniform(jax.random.fold_in(own, dim), (blocks,), jnp.float32, least / len(cuts), largest / len(cuts)))
        factor_of = factor_of * jnp.repeat(draws, extent[dim] // blocks).reshape([-1 if axis == dim else 1 for axis in range(len(extent))])
    return factor_of


def length_profile(count, total, most, slope):
    weights = [(1 << 20) // math.isqrt(grade ** slope) + 1 for grade in range(2, count + 1)]
    spare, holding = total - most - (count - 1), [1] * (count - 1)
    while spare > 0:
        free = [i for i in range(count - 1) if holding[i] < most]
        mass, left = sum([weights[i] for i in free]), spare
        for i in free:
            more = min(most - holding[i], max(1, left * weights[i] // mass), spare)
            holding[i] = holding[i] + more
            spare = spare - more
    return np.array([most] + holding)


def uneven(rng, count, total, bound, lean):
    if count == 2:
        one = jax.random.randint(rng, (), max(1, total - bound), min(bound, total - 1) + 1)
        return jnp.stack([one, total - one])
    lengths = jnp.asarray(length_profile(count, total, bound, lean), jnp.int32)
    pairs = (count - 1) // 2
    giver, taker = lengths[1:1 + 2 * pairs:2], lengths[2:2 + 2 * pairs:2]
    room = jnp.minimum(giver - 1, bound - taker)
    shifted = jax.random.randint(jax.random.fold_in(rng, 1), (pairs,), 0, 1 << 20) % (room + 1)
    lengths = lengths.at[1:1 + 2 * pairs:2].set(giver - shifted).at[2:2 + 2 * pairs:2].set(taker + shifted)
    return lengths[jax.random.permutation(jax.random.fold_in(rng, 2), count)]


def scatter_about(rng, shape, scale, most, shards=(), kind=jnp.bfloat16):
    values = scale * jax.random.normal(rng, shape, jnp.float32)
    if shards:
        values = values * block_scale(rng, shape, shards, -0.22, 0.18)
    return jnp.clip(values, -most, most).astype(kind)


def setup_inputs(seed: int = 0) -> dict:
    splits = jax.random.split(jax.random.key(seed), 17)
    return {
        "tokens": scatter_about(splits[0], (TOKENS, D), 1.0, 6.0, ((0, 16),)),
        "qkv_weight": scatter_about(splits[1], (N_SECTION, D, 3 * D), D ** -0.5, 0.1875, ((0, 2), (1, 16))),
        "qkv_bias": scatter_about(splits[2], (N_SECTION, 3 * D), 0.2, 1.1953125, ((0, 2), (1, 16))),
        "out_weight": scatter_about(splits[3], (N_SECTION, D, D), (D // 8) ** -0.5, 0.5, ((0, 2), (1, 16))),
        "out_bias": scatter_about(splits[4], (N_SECTION, D), 0.2, 1.1953125, ((0, 2), (1, 16))),
        "norm1_gain": jnp.clip(1.0 + 0.1 * jax.random.normal(splits[5], (N_SECTION, D), jnp.float32), 0.5, 1.5).astype(jnp.bfloat16),
        "norm1_bias": scatter_about(splits[6], (N_SECTION, D), 0.2, 1.1953125, ((0, 2), (1, 16))),
        "up_weight": scatter_about(splits[7], (N_SECTION, D, FF), D ** -0.5, 0.1875, ((0, 2), (1, 16))),
        "up_bias": scatter_about(splits[8], (N_SECTION, FF), 0.2, 1.1953125, ((0, 2), (1, 16))),
        "down_weight": scatter_about(splits[9], (N_SECTION, FF, D), FF ** -0.5, 0.09375, ((0, 2), (1, 16))),
        "down_bias": scatter_about(splits[10], (N_SECTION, D), 0.2, 1.1953125, ((0, 2), (1, 16))),
        "norm2_gain": jnp.clip(1.0 + 0.1 * jax.random.normal(splits[11], (N_SECTION, D), jnp.float32), 0.5, 1.5).astype(jnp.bfloat16),
        "norm2_bias": scatter_about(splits[12], (N_SECTION, D), 0.2, 1.1953125, ((0, 2), (1, 16))),
        "proj_weight": scatter_about(splits[13], (D, PROJ), D ** -0.5, 0.1875, ((0, 16),)),
        "doc_lengths": jax.vmap(lambda own: uneven(own, DOCS_DEV, DOC_ROWS, DOC_ROWS // 2, 2))(jax.random.split(splits[14], BLOCKS)).reshape((BLOCKS, DOCS_DEV)).astype(jnp.int32),
        "pair_docs": touch_ends(jax.random.randint(splits[15], (QUERIES, CANDS), 0, N_DP * DOCS_DEV), jax.random.fold_in(splits[15], 1), 0, (N_DP * DOCS_DEV) - 1).astype(jnp.int32),
    }


@jax.custom_vjp
def low(v):
    return lax.optimization_barrier(v.astype(jnp.bfloat16)).astype(jnp.float32)

@jax.custom_vjp
def low_back(v):
    return v

def low_keep(v):
    return (low(v), None)

def low_pass(kept, grad):
    return (grad,)

def back_keep(v):
    return (v, None)

def back_low(kept, grad):
    return (low(grad),)
low.defvjp(low_keep, low_pass)
low_back.defvjp(back_keep, back_low)
norm_eps = 1e-05
unit_eps = 1e-06
sharpness = 20.0
score_scale = 0.125
masked_score = -1000000000.0

def highest(left_side, right_side):
    return jnp.dot(left_side, right_side, precision=lax.Precision.HIGHEST)

def layer_norm(values, scales, offset):
    center = values - lax.optimization_barrier(jnp.mean(values, axis=-1, keepdims=True))
    spread = lax.optimization_barrier(jnp.mean(center * center, axis=-1, keepdims=True))
    return center * lax.rsqrt(spread + norm_eps) * scales + offset

def doc_layout(doc_lens):
    row_ids = jnp.arange(ROWS, dtype=jnp.int32)
    ends_at = jnp.cumsum(doc_lens.astype(jnp.int32)).astype(jnp.int32)
    starts_at = ends_at - doc_lens.astype(jnp.int32)
    doc_of = lax.optimization_barrier(jnp.sum((row_ids[:, None] >= ends_at[None, :]).astype(jnp.int32), axis=1)).astype(jnp.int32)
    doc_index = jnp.arange(DOCS_DEV, dtype=jnp.int32)
    begins = lax.optimization_barrier(jnp.sum(jnp.where(doc_of[:, None] == doc_index[None, :], starts_at[None, :], 0), axis=1)).astype(jnp.int32)
    in_docs = row_ids < DOC_ROWS
    query_rows = jnp.maximum(row_ids - DOC_ROWS, 0)
    segment = jnp.where(in_docs, doc_of, DOCS_DEV + query_rows // QLEN).astype(jnp.int32)
    position = jnp.where(in_docs, row_ids - begins, query_rows % QLEN).astype(jnp.int32)
    return (segment, position)

def membership(doc_lens):
    segment, position = doc_layout(doc_lens)
    doc_index = jnp.arange(DOCS_DEV, dtype=jnp.int32)
    return (segment[:DOC_ROWS, None] == doc_index[None, :]).astype(jnp.float32)

def rotary(position):
    step_ids = jnp.arange(HEAD // 2, dtype=jnp.int32).astype(jnp.float32)
    frequency = jnp.exp(step_ids * (-2.0 * math.log(10000.0) / HEAD))
    angles = position.astype(jnp.float32)[:, None] * frequency[None, :]
    return (jnp.cos(angles), jnp.sin(angles))

def rotate(tensor, cosine, sine_tab):
    halfway = tensor.shape[-1] // 2
    first_half = tensor[..., :halfway]
    second_half = tensor[..., halfway:]
    cos_wide = cosine[:, None, :]
    sin_wide = sine_tab[:, None, :]
    return jnp.concatenate([first_half * cos_wide - second_half * sin_wide, second_half * cos_wide + first_half * sin_wide], axis=-1)

def layer_apply(source, params, segment, position):
    qkv_w, qkv_b, out_w, out_b, gain_one, bias_one, up_w, up_b, down_w, down_b, gain_two, bias_two = params
    row_count = source.shape[0]
    mixed = low_back(highest(source, qkv_w) + qkv_b)
    cosine, sine_tab = rotary(position)
    queries = low(rotate(mixed[:, :D].reshape(row_count, HEADS, HEAD), cosine, sine_tab))
    keys_rot = low(rotate(mixed[:, D:2 * D].reshape(row_count, HEADS, HEAD), cosine, sine_tab))
    values = low(mixed[:, 2 * D:].reshape(row_count, HEADS, HEAD))
    scores = low_back(jnp.einsum('qhd,khd->hqk', queries, keys_rot, precision=lax.Precision.HIGHEST) * score_scale)
    allowed = segment[:, None] == segment[None, :]
    scores = jnp.where(allowed[None], scores, masked_score)
    attention = low(jax.nn.softmax(scores, axis=-1))
    mixture = low(low_back(jnp.einsum('hqk,khd->qhd', attention, values, precision=lax.Precision.HIGHEST))).reshape(row_count, D)
    attended = low_back(highest(mixture, out_w) + out_b)
    first_norm = low(layer_norm(source + attended, gain_one, bias_one))
    gate_in = low_back(highest(first_norm, up_w) + up_b)
    activated = low(jax.nn.gelu(gate_in, approximate=False))
    branch = low_back(highest(activated, down_w) + down_b)
    return layer_norm(first_norm + branch, gain_two, bias_two)

def run_layer(blocks, params, segments, positions):
    apply_one = jax.checkpoint(lambda operands: layer_apply(operands[0], params, operands[1], operands[2]))
    return lax.map(apply_one, (blocks, segments, positions))

def score_block(queries, documents, member):
    results = []
    for prefix in (PROJ // 2, 3 * PROJ // 4, PROJ):
        query_part = queries[..., :prefix]
        doc_part = documents[:, :prefix]
        query_unit = query_part * lax.rsqrt(lax.optimization_barrier(jnp.sum(query_part * query_part, axis=-1, keepdims=True)) + unit_eps)
        doc_unit = doc_part * lax.rsqrt(lax.optimization_barrier(jnp.sum(doc_part * doc_part, axis=-1, keepdims=True)) + unit_eps)
        similar = jnp.einsum('qtp,rp->qtr', query_unit, doc_unit, precision=lax.Precision.HIGHEST)
        masses = jnp.einsum('qtr,rj->qtj', jnp.exp(sharpness * similar), member, precision=lax.Precision.HIGHEST)
        results.append(lax.optimization_barrier(jnp.sum(jnp.log(masses), axis=1)) / sharpness)
    return jnp.stack(results)

def cross_entropy(scores, pair_ids):
    total_docs = scores.shape[2]
    chosen = (pair_ids[:, :, None] == jnp.arange(total_docs, dtype=jnp.int32)[None, None, :]).astype(jnp.float32)
    logits = jnp.einsum('kqa,qca->kqc', scores, chosen, precision=lax.Precision.HIGHEST)
    return lax.optimization_barrier(jnp.sum(jax.nn.logsumexp(logits, axis=-1) - logits[:, :, 0], axis=0))

def reference(tokens, qkv_weight, qkv_bias, out_weight, out_bias, norm1_gain, norm1_bias, up_weight, up_bias, down_weight, down_bias, norm2_gain, norm2_bias, proj_weight, doc_lengths, pair_docs):
    layer_args = (qkv_weight, qkv_bias, out_weight, out_bias, norm1_gain, norm1_bias, up_weight, up_bias, down_weight, down_bias, norm2_gain, norm2_bias)
    segments, positions = jax.vmap(doc_layout)(doc_lengths)
    members = jax.vmap(membership)(doc_lengths).reshape(N_DP, MICRO, DOC_ROWS, DOCS_DEV)
    pair_grid = pair_docs.reshape(N_DP, MICRO, QRY_DEV, CANDS)

    def objective(token_vals, params, projection, probe_input):
        blocks = token_vals.reshape(BLOCKS, ROWS, D)
        first_out = low(run_layer(blocks, tuple((weight_pair[0] for weight_pair in params)), segments, positions))
        second_in = low_back(first_out) + probe_input
        second_out = low(run_layer(second_in, tuple((weight_pair[1] for weight_pair in params)), segments, positions))
        embedded = low(low_back(jnp.einsum('brd,dp->brp', second_out, projection, precision=lax.Precision.HIGHEST)))
        embedded = embedded.reshape(N_DP, MICRO, ROWS, PROJ)
        losses = []
        for micro_step in range(MICRO):
            queries = embedded[:, micro_step, DOC_ROWS:].reshape(N_DP * QRY_DEV, QLEN, PROJ)
            scorer = jax.checkpoint(lambda operands: score_block(queries, operands[0], operands[1]))
            per_device = lax.map(scorer, (embedded[:, micro_step, :DOC_ROWS], members[:, micro_step]))
            score_table = jnp.transpose(per_device, (1, 2, 0, 3)).reshape(3, N_DP * QRY_DEV, N_DP * DOCS_DEV)
            pair_rows = pair_grid[:, micro_step].reshape(N_DP * QRY_DEV, CANDS)
            losses.append(cross_entropy(score_table, pair_rows).reshape(N_DP, QRY_DEV))
        return (jnp.stack(losses, axis=1).reshape(QUERIES), (first_out, second_out))
    params = tuple((argument.astype(jnp.float32) for argument in layer_args))
    probe_input = jnp.zeros((BLOCKS, ROWS, D), jnp.float32)
    losses, pullback, sections_out = jax.vjp(objective, tokens.astype(jnp.float32), params, proj_weight.astype(jnp.float32), probe_input, has_aux=True)
    grad_tokens, grad_params, grad_proj, grad_probe = pullback(jnp.ones_like(losses))
    activations = jnp.stack([sections_out[0], sections_out[1]]).reshape(2, TOKENS, D).astype(jnp.bfloat16)
    grad_inputs = jnp.stack([grad_tokens, grad_probe.reshape(TOKENS, D)])
    return (losses, activations, grad_inputs, grad_params[0], grad_params[1], grad_params[2], grad_params[3], grad_params[4], grad_params[5], grad_params[6], grad_params[7], grad_params[8], grad_params[9], grad_params[10], grad_params[11], grad_proj)
```

```python
from functools import partial
import math

import jax
import jax.numpy as jnp
from jax import lax
from jax.experimental import pallas as pl
from jax.experimental.pallas import tpu as pltpu
from jax.sharding import PartitionSpec as P

HEAD = 64
PROJ = 128
QLEN = 32
DOC_ROWS = 192
QRY_DEV = 2
DOCS_DEV = 3
MICRO = 2
CANDS = 8
ROWS = 256
PREFIXES = (PROJ // 2, 3 * PROJ // 4, PROJ)


norm_eps = 1e-05
unit_eps = 1e-06
sharpness = 20.0
score_scale = 0.125
masked_score = -1000000000.0


def from_behind(value, axis, steps):
    count = lax.axis_size(axis)
    first, last = (max(0, -steps), min(count, count - steps))
    return lax.ppermute(value, axis, [(source, source + steps) for source in range(first, last)])


def product(left_side, right_side):
    return jnp.dot(left_side, right_side, preferred_element_type=jnp.float32)


def product_tn(left_side, right_side):
    return lax.dot_general(
        left_side, right_side, (((0,), (0,)), ((), ())), preferred_element_type=jnp.float32
    )


def product_nt(left_side, right_side):
    return lax.dot_general(
        left_side, right_side, (((1,), (1,)), ((), ())), preferred_element_type=jnp.float32
    )


def layer_norm(values, scales, offset):
    center = values - jnp.mean(values, axis=-1, keepdims=True)
    spread = jnp.mean(center * center, axis=-1, keepdims=True)
    return center * lax.rsqrt(spread + norm_eps) * scales + offset


def doc_layout(doc_lens):
    row_ids = jnp.arange(ROWS, dtype=jnp.int32)
    ends_at = jnp.cumsum(doc_lens)
    starts_at = ends_at - doc_lens
    doc_of = jnp.sum((row_ids[:, None] >= ends_at[None, :]).astype(jnp.int32), axis=1)
    doc_index = jnp.arange(DOCS_DEV, dtype=jnp.int32)
    begins = jnp.sum(
        jnp.where(doc_of[:, None] == doc_index[None, :], starts_at[None, :], 0), axis=1
    )
    in_docs = row_ids < DOC_ROWS
    query_rows = jnp.maximum(row_ids - DOC_ROWS, 0)
    segment = jnp.where(in_docs, doc_of, DOCS_DEV + query_rows // QLEN)
    position = jnp.where(in_docs, row_ids - begins, query_rows % QLEN)
    return (segment, position)


def rotary(position):
    step_ids = jnp.arange(HEAD // 2, dtype=jnp.int32).astype(jnp.float32)
    frequency = jnp.exp(step_ids * (-2.0 * math.log(10000.0) / HEAD))
    angles = position.astype(jnp.float32)[:, None] * frequency[None, :]
    return (jnp.cos(angles), jnp.sin(angles))


def rotate(tensor, cosine, sine_tab):
    halfway = tensor.shape[-1] // 2
    first_half = tensor[..., :halfway]
    second_half = tensor[..., halfway:]
    cos_wide = cosine[:, None, :]
    sin_wide = sine_tab[:, None, :]
    return jnp.concatenate(
        [
            first_half * cos_wide - second_half * sin_wide,
            second_half * cos_wide + first_half * sin_wide,
        ],
        axis=-1,
    )


def layer_forward(source, weights, segment, position):
    (
        qkv_w,
        qkv_b,
        out_w,
        out_b,
        gain_one,
        bias_one,
        up_w,
        up_b,
        down_w,
        down_b,
        gain_two,
        bias_two,
    ) = weights
    row_count = source.shape[0]
    model_width = out_w.shape[0]
    mixed = product(source, qkv_w) + qkv_b.astype(jnp.float32)
    cosine, sine_tab = rotary(position)
    queries = rotate(mixed[:, :model_width].reshape(row_count, -1, HEAD), cosine, sine_tab).astype(
        jnp.bfloat16
    )
    keys_rot = rotate(
        mixed[:, model_width : 2 * model_width].reshape(row_count, -1, HEAD), cosine, sine_tab
    ).astype(jnp.bfloat16)
    values = mixed[:, 2 * model_width :].reshape(row_count, -1, HEAD).astype(jnp.bfloat16)
    scores = (
        jnp.einsum("qhd,khd->hqk", queries, keys_rot, preferred_element_type=jnp.float32)
        * score_scale
    )
    allowed = segment[:, None] == segment[None, :]
    scores = jnp.where(allowed[None], scores, masked_score)
    attention = jax.nn.softmax(scores, axis=-1)
    attention_low = attention.astype(jnp.bfloat16)
    mixture = jnp.einsum("hqk,khd->qhd", attention_low, values, preferred_element_type=jnp.float32)
    mixture = mixture.reshape(row_count, model_width).astype(jnp.bfloat16)
    first_sum = source.astype(jnp.float32) + (product(mixture, out_w) + out_b.astype(jnp.float32))
    first_norm = layer_norm(
        first_sum, gain_one.astype(jnp.float32), bias_one.astype(jnp.float32)
    ).astype(jnp.bfloat16)
    gate_in = product(first_norm, up_w) + up_b.astype(jnp.float32)
    activated = jax.nn.gelu(gate_in, approximate=False).astype(jnp.bfloat16)
    second_sum = first_norm.astype(jnp.float32) + (
        product(activated, down_w) + down_b.astype(jnp.float32)
    )
    result = layer_norm(
        second_sum, gain_two.astype(jnp.float32), bias_two.astype(jnp.float32)
    ).astype(jnp.bfloat16)
    return (
        source,
        cosine,
        sine_tab,
        queries,
        keys_rot,
        values,
        attention,
        attention_low,
        mixture,
        first_sum,
        first_norm,
        gate_in,
        activated,
        second_sum,
        result,
    )


def layer_backward(saved_state, upstream, weights):
    (
        qkv_w,
        qkv_b,
        out_w,
        out_b,
        gain_one,
        bias_one,
        up_w,
        up_b,
        down_w,
        down_b,
        gain_two,
        bias_two,
    ) = weights
    (
        source,
        cosine,
        sine_tab,
        queries,
        keys_rot,
        values,
        attention,
        attention_low,
        mixture,
        first_sum,
        first_norm,
        gate_in,
        activated,
        second_sum,
        result,
    ) = saved_state
    row_count = source.shape[0]
    unused, second_back = jax.vjp(
        layer_norm, second_sum, gain_two.astype(jnp.float32), bias_two.astype(jnp.float32)
    )
    grad_sum_two, grad_gain_two, grad_bias_two = second_back(upstream)
    grad_branch = grad_sum_two.astype(jnp.bfloat16)
    grad_down_b = jnp.sum(grad_branch.astype(jnp.float32), axis=0)
    unused, gelu_back = jax.vjp(partial(jax.nn.gelu, approximate=False), gate_in)
    (grad_gate,) = gelu_back(product_nt(grad_branch, down_w))
    grad_gate_low = grad_gate.astype(jnp.bfloat16)
    grad_up_b = jnp.sum(grad_gate_low.astype(jnp.float32), axis=0)
    grad_first = grad_sum_two + product_nt(grad_gate_low, up_w)
    unused, first_back = jax.vjp(
        layer_norm, first_sum, gain_one.astype(jnp.float32), bias_one.astype(jnp.float32)
    )
    grad_sum_one, grad_gain_one, grad_bias_one = first_back(grad_first)
    grad_attended = grad_sum_one.astype(jnp.bfloat16)
    grad_out_b = jnp.sum(grad_attended.astype(jnp.float32), axis=0)
    grad_mixture = (
        product_nt(grad_attended, out_w).astype(jnp.bfloat16).reshape(row_count, -1, HEAD)
    )
    grad_attention = jnp.einsum(
        "qhd,khd->hqk", grad_mixture, values, preferred_element_type=jnp.float32
    )
    grad_values = jnp.einsum(
        "hqk,qhd->khd", attention_low, grad_mixture, preferred_element_type=jnp.float32
    )
    grad_scores = attention * (
        grad_attention - jnp.sum(grad_attention * attention, axis=-1, keepdims=True)
    )
    grad_scores = grad_scores.astype(jnp.bfloat16)
    grad_queries = (
        jnp.einsum("hqk,khd->qhd", grad_scores, keys_rot, preferred_element_type=jnp.float32)
        * score_scale
    )
    grad_keys = (
        jnp.einsum("hqk,qhd->khd", grad_scores, queries, preferred_element_type=jnp.float32)
        * score_scale
    )
    grad_queries = rotate(grad_queries, cosine, -sine_tab)
    grad_keys = rotate(grad_keys, cosine, -sine_tab)
    grad_mixed = jnp.concatenate(
        [
            grad_queries.reshape(row_count, -1),
            grad_keys.reshape(row_count, -1),
            grad_values.reshape(row_count, -1),
        ],
        axis=1,
    ).astype(jnp.bfloat16)
    grad_qkv_b = jnp.sum(grad_mixed.astype(jnp.float32), axis=0)
    grad_source = grad_sum_one + product_nt(grad_mixed, qkv_w)
    pairs = (
        (activated, grad_branch),
        (first_norm, grad_gate_low),
        (mixture, grad_attended),
        (source, grad_mixed),
    )
    vectors = (
        grad_qkv_b,
        grad_out_b,
        grad_gain_one,
        grad_bias_one,
        grad_up_b,
        grad_down_b,
        grad_gain_two,
        grad_bias_two,
    )
    return (pairs, vectors, grad_source)


def grid_of(count):
    dims, rest = [], count // 2
    while rest % 4 == 0:
        dims.append(4)
        rest //= 4
    if rest > 1:
        dims.append(rest)
    return dims + [2]


def coordinates(dims, number):
    at = []
    for size in reversed(dims):
        at.append(number % size)
        number = number // size
    return at[::-1]


def shifted(value, dims, dim, steps):
    count = math.prod(dims)
    stride = math.prod(dims[dim + 1 :])
    pairs = []
    for source in range(count):
        place = (source // stride) % dims[dim]
        pairs.append((source, source + ((place + steps) % dims[dim] - place) * stride))
    return lax.ppermute(value, "dp", pairs)


def after(value, *earlier):
    return lax.optimization_barrier((value, *earlier))[0]


def place_kernel(count, rows, places, *refs):
    pieces, out, sems = refs[:-2], refs[-2], refs[-1]
    copies = []
    for number in range(count):
        group, inner = divmod(number, pieces[0].shape[0])
        copies.append(
            pltpu.make_async_copy(
                pieces[group].at[inner], out.at[places[number]], sems.at[number]
            )
        )
    for copy in copies:
        copy.start()
    for copy in copies:
        copy.wait()


def placed(pieces, places):
    count = sum(piece.shape[0] for piece in pieces)
    rows, columns = pieces[0].shape[1:]
    if rows % 16:
        stacked = jnp.concatenate(pieces, axis=0)
        order = jnp.zeros((count,), jnp.int32).at[places].set(jnp.arange(count, dtype=jnp.int32))
        return jnp.take(stacked, order, axis=0).reshape(count * rows, columns)
    return pl.pallas_call(
        partial(place_kernel, count, rows),
        out_shape=jax.ShapeDtypeStruct((count, rows, columns), pieces[0].dtype),
        in_specs=[pl.BlockSpec(memory_space=pltpu.SMEM)]
        + [pl.BlockSpec(memory_space=pl.ANY)] * len(pieces),
        out_specs=pl.BlockSpec(memory_space=pltpu.VMEM),
        scratch_shapes=[pltpu.SemaphoreType.DMA((count,))],
        compiler_params=pltpu.CompilerParams(vmem_limit_bytes=24 << 20),
        name="place",
    )(places, *pieces).reshape(count * rows, columns)


def gather_rows(shards_in_order, dims, dp_index):
    at = [
        (dp_index // math.prod(dims[dim + 1 :])) % dims[dim] for dim in range(len(dims))
    ]
    owners = jnp.zeros((1,), jnp.int32)
    for dim in range(len(dims)):
        steps = jnp.arange(dims[dim], dtype=jnp.int32)
        own = ((at[dim] - steps) % dims[dim]) * math.prod(dims[dim + 1 :])
        owners = (own[:, None] + owners[None, :]).reshape(-1)
    first_done = []
    whole = []
    for number, shard in enumerate(shards_in_order):
        if number >= 2:
            shard = after(shard, first_done[number - 2])
        stack = jnp.stack(
            [shard] + [shifted(shard, dims, 0, steps) for steps in range(1, dims[0])]
        )
        first_done.append(stack)
        groups = [stack]
        for dim in range(1, len(dims)):
            groups = groups + [
                shifted(group, dims, dim, steps)
                for steps in range(1, dims[dim])
                for group in groups
            ]
        whole.append(placed(groups, owners))
    return whole


def scatter_rows(left, right, dims, dp_index):
    count = math.prod(dims)
    at = [
        (dp_index // math.prod(dims[dim + 1 :])) % dims[dim] for dim in range(len(dims))
    ]
    samples, height = left.shape
    rows, columns = height // count, right.shape[1]
    split = left.reshape(samples, count // 2, 2, rows)
    for_other = lax.dynamic_index_in_dim(split, 1 - at[-1], 2, False).reshape(samples, -1)
    for_self = lax.dynamic_index_in_dim(split, at[-1], 2, False).reshape(samples, -1)
    sent = product_tn(for_other, right).astype(jnp.bfloat16)
    total = product_tn(for_self, right) + shifted(sent, dims, len(dims) - 1, 1).astype(jnp.float32)
    for dim in reversed(range(len(dims) - 1)):
        low = total.astype(jnp.bfloat16).reshape(-1, dims[dim], rows, columns)
        total = lax.dynamic_index_in_dim(low, at[dim], 1, False).astype(jnp.float32)
        for steps in range(1, dims[dim]):
            part = lax.dynamic_index_in_dim(low, (at[dim] + steps) % dims[dim], 1, False)
            total = total + shifted(part, dims, dim, steps).astype(jnp.float32)
    return total.reshape(rows, columns)


def spread(value, count):
    return lax.all_to_all(
        jnp.broadcast_to(value[None], (count, *value.shape)), "dp", 0, 0, tiled=True
    )


def summed(parts):
    return jnp.sum(lax.all_to_all(parts, "dp", 0, 0, tiled=True).astype(jnp.float32), axis=0)


def halves(value):
    high = value.astype(jnp.bfloat16)
    return high, (value - high.astype(jnp.float32)).astype(jnp.bfloat16)


def exact_product(left_side, right_side):
    high, low = halves(right_side)
    return product(left_side, high) + product(left_side, low)


def product_by_ones(left_side, right_side):
    high, low = halves(left_side)
    return product(high, right_side) + product(low, right_side)


def prefix_masks(length):
    places = lax.broadcasted_iota(jnp.int32, (1, length), 1)
    return [places < width for width in PREFIXES]


def similar_parts(documents, queries_t):
    docs_f32 = documents.astype(jnp.float32)
    squares = docs_f32 * docs_f32
    query_squares = queries_t * queries_t
    queries_low = queries_t.astype(jnp.bfloat16)
    parts = []
    for width, mask in zip(PREFIXES, prefix_masks(PROJ)):
        cut = jnp.where(mask, docs_f32, 0.0)
        doc_scale = lax.rsqrt(
            jnp.sum(jnp.where(mask, squares, 0.0), axis=1, keepdims=True) + unit_eps
        )
        query_scale = lax.rsqrt(
            jnp.sum(query_squares[:width], axis=0, keepdims=True) + unit_eps
        )
        cut = cut.astype(jnp.bfloat16)
        similar = product(cut, queries_low) * doc_scale * query_scale
        parts.append((cut, doc_scale, query_scale, similar))
    return parts


def members_of(ends_ref, micro_step, by_row):
    shape = (DOC_ROWS, 8) if by_row else (8, DOC_ROWS)
    rows = lax.broadcasted_iota(jnp.int32, shape, 0 if by_row else 1)
    docs = lax.broadcasted_iota(jnp.int32, shape, 1 if by_row else 0)
    inside = jnp.zeros(shape, jnp.float32)
    for number in range(DOCS_DEV):
        begin = ends_ref[micro_step, number - 1] if number else 0
        held = (docs == number) & (rows >= begin) & (rows < ends_ref[micro_step, number])
        inside = jnp.where(held, 1.0, inside)
    return inside.astype(jnp.bfloat16)


def query_of_token(tokens, by_token):
    shape = (tokens, 128) if by_token else (128, tokens)
    token = lax.broadcasted_iota(jnp.int32, shape, 0 if by_token else 1)
    query = lax.broadcasted_iota(jnp.int32, shape, 1 if by_token else 0)
    held = (token >= query * QLEN) & (token < query * QLEN + QLEN)
    return jnp.where(held, 1.0, 0.0).astype(jnp.bfloat16)


def score_kernel(ends_ref, queries_ref, docs_ref, out_ref):
    micro_step = pl.program_id(0)
    tokens = queries_ref.shape[0] * queries_ref.shape[2]
    queries_t = queries_ref[:, 0].astype(jnp.float32).reshape(tokens, PROJ).T
    members = members_of(ends_ref, micro_step, False)
    by_query = query_of_token(tokens, True)
    for number, (_, _, _, similar) in enumerate(similar_parts(docs_ref[0], queries_t)):
        masses = exact_product(members, jnp.exp(sharpness * similar))
        held = lax.broadcasted_iota(jnp.int32, masses.shape, 0) < DOCS_DEV
        logs = jnp.log(jnp.where(held, masses, 1.0))
        out_ref[0, 0, number] = product_by_ones(logs, by_query) / sharpness


def loss_kernel(
    ends_ref, queries_ref, docs_ref, table_ref, own_ref, times_ref, first_ref, own_times_ref,
    own_first_ref, loss_ref, grad_queries_ref, grad_docs_ref
):
    micro_step = pl.program_id(0)
    step = pl.program_id(1)
    devices, width = queries_ref.shape[0], queries_ref.shape[2]
    tokens = devices * width
    queries_t = queries_ref[:, 0].astype(jnp.float32).reshape(tokens, PROJ).T
    queries_low = queries_t.astype(jnp.bfloat16)
    members = members_of(ends_ref, micro_step, False)
    members_by_row = members_of(ends_ref, micro_step, True)
    spread_out = query_of_token(tokens, False)
    places = lax.broadcasted_iota(jnp.int32, (PROJ, 1), 0)
    grad_queries = jnp.zeros((PROJ, tokens), jnp.float32)
    grad_docs = jnp.zeros((DOC_ROWS, PROJ), jnp.float32)
    losses = jnp.zeros((1, 128), jnp.float32)
    docs_f32 = docs_ref[0].astype(jnp.float32)
    times, first = times_ref[0, 0], first_ref[0, 0]
    for number, (cut, doc_scale, query_scale, similar) in enumerate(
        similar_parts(docs_ref[0], queries_t)
    ):
        table = table_ref[0, 0, number]
        top = jnp.max(jnp.where(times > 0, table, -1e30), axis=0, keepdims=True)
        top = jnp.where(top > -1e29, top, 0.0)
        normal = top + jnp.log(
            jnp.maximum(
                jnp.sum(times * jnp.exp(jnp.minimum(table - top, 0.0)), axis=0, keepdims=True),
                1e-30,
            )
        )
        losses = losses + normal - jnp.sum(first * table, axis=0, keepdims=True)
        own = own_ref[0, 0, number]
        own_times = own_times_ref[0, 0]
        grad_score = (
            own_times * jnp.exp(jnp.where(own_times > 0, own - normal, 0.0)) - own_first_ref[0, 0]
        )
        weights = jnp.exp(sharpness * similar)
        masses = exact_product(members, weights)
        by_token = product_by_ones(grad_score, spread_out)
        held = lax.broadcasted_iota(jnp.int32, masses.shape, 0) < DOCS_DEV
        by_token = jnp.where(held, by_token / jnp.where(held, masses, 1.0), 0.0)
        grad_similar = weights * exact_product(members_by_row, by_token)
        along = grad_similar * similar
        pulled = (grad_similar * doc_scale * query_scale).astype(jnp.bfloat16)
        mask = lax.broadcasted_iota(jnp.int32, (1, PROJ), 1) < PREFIXES[number]
        grad_docs = (
            grad_docs
            + jnp.where(mask, product_nt(pulled, queries_low), 0.0)
            - cut.astype(jnp.float32)
            * (doc_scale * doc_scale * jnp.sum(along, axis=1, keepdims=True))
        )
        toward = product_tn(cut, pulled)
        back = queries_t * (
            query_scale * query_scale * jnp.sum(along, axis=0, keepdims=True)
        )
        grad_queries = grad_queries + toward - jnp.where(places < PREFIXES[number], back, 0.0)
    loss_ref[0, 0] = losses
    grad_queries_ref[:, 0] = grad_queries.T.reshape(devices, width, PROJ).astype(jnp.bfloat16)

    @pl.when(step == 0)
    def _():
        grad_docs_ref[0] = grad_docs

    @pl.when(step > 0)
    def _():
        grad_docs_ref[0] += grad_docs


def loss_parts(hidden, projection, ends, pair_rows, dp_index, count):
    group = math.gcd(count, 16)
    steps = count // group
    queries_in_step = group * QRY_DEV
    total_docs = count * DOCS_DEV
    doc_rows = -(-total_docs // 8) * 8
    doc_ids = jnp.arange(doc_rows, dtype=jnp.int32)
    chosen = (pair_rows[:, None, :, :] == doc_ids[None, :, None, None]).astype(jnp.float32)
    by_doc = [jnp.sum(chosen, axis=3), chosen[..., 0]]

    def steps_of(value):
        value = value.reshape(*value.shape[:-1], steps, queries_in_step)
        value = jnp.pad(value, [(0, 0)] * (value.ndim - 1) + [(0, 128 - queries_in_step)])
        return jnp.moveaxis(value, -2, 1)

    times, first = [steps_of(value) for value in by_doc]
    own_times, own_first = [
        jnp.pad(
            lax.dynamic_slice_in_dim(value, dp_index * DOCS_DEV, DOCS_DEV, 2),
            [(0, 0), (0, 0), (0, 8 - DOCS_DEV), (0, 0)],
        )
        for value in (times, first)
    ]
    embedded = product(hidden.reshape(MICRO * ROWS, -1), projection).astype(jnp.bfloat16)
    embedded = embedded.reshape(MICRO, ROWS, -1)
    documents = embedded[:, :DOC_ROWS]
    all_queries = spread(embedded[:, DOC_ROWS:], count)
    in_smem = pl.BlockSpec(memory_space=pltpu.SMEM)
    queries_spec = pl.BlockSpec((group, 1, QRY_DEV * QLEN, PROJ), lambda m, b: (b, m, 0, 0))
    docs_spec = pl.BlockSpec((1, DOC_ROWS, PROJ), lambda m, b: (m, 0, 0))
    own_spec = pl.BlockSpec((1, 1, 3, 8, 128), lambda m, b: (m, b, 0, 0, 0))
    params = pltpu.CompilerParams(vmem_limit_bytes=48 << 20)
    own_scores = pl.pallas_call(
        score_kernel,
        grid=(MICRO, steps),
        out_shape=jax.ShapeDtypeStruct((MICRO, steps, 3, 8, 128), jnp.float32),
        in_specs=[in_smem, queries_spec, docs_spec],
        out_specs=own_spec,
        compiler_params=params,
        name="scores",
    )(ends, all_queries, documents)
    tables = spread(own_scores[:, :, :, :DOCS_DEV], count)
    table = jnp.transpose(tables, (1, 2, 3, 0, 4, 5)).reshape(MICRO, steps, 3, total_docs, 128)
    table = jnp.pad(table, [(0, 0)] * 3 + [(0, doc_rows - total_docs), (0, 0)])
    counts_spec = pl.BlockSpec((1, 1, doc_rows, 128), lambda m, b: (m, b, 0, 0))
    own_counts_spec = pl.BlockSpec((1, 1, 8, 128), lambda m, b: (m, b, 0, 0))
    losses, grad_queries, grad_docs = pl.pallas_call(
        loss_kernel,
        grid=(MICRO, steps),
        out_shape=(
            jax.ShapeDtypeStruct((MICRO, steps, 1, 128), jnp.float32),
            jax.ShapeDtypeStruct((count, MICRO, QRY_DEV * QLEN, PROJ), jnp.bfloat16),
            jax.ShapeDtypeStruct((MICRO, DOC_ROWS, PROJ), jnp.float32),
        ),
        in_specs=[
            in_smem,
            queries_spec,
            docs_spec,
            pl.BlockSpec((1, 1, 3, doc_rows, 128), lambda m, b: (m, b, 0, 0, 0)),
            own_spec,
            counts_spec,
            counts_spec,
            own_counts_spec,
            own_counts_spec,
        ],
        out_specs=(
            pl.BlockSpec((1, 1, 1, 128), lambda m, b: (m, b, 0, 0)),
            queries_spec,
            docs_spec,
        ),
        compiler_params=params,
        name="losses",
    )(ends, all_queries, documents, table, own_scores, times, first, own_times, own_first)
    losses = losses[:, :, 0, :queries_in_step].reshape(MICRO, count * QRY_DEV)
    own_losses = lax.dynamic_slice_in_dim(losses, dp_index * QRY_DEV, QRY_DEV, 1)
    grad_own = summed(grad_queries)
    grad_embedded = jnp.concatenate([grad_docs, grad_own], axis=1).astype(jnp.bfloat16)
    grad_projection = product_tn(
        hidden.reshape(MICRO * ROWS, -1), grad_embedded.reshape(MICRO * ROWS, -1)
    )
    grad_hidden = product_nt(grad_embedded.reshape(MICRO * ROWS, -1), projection)
    return (grad_hidden.reshape(MICRO, ROWS, -1), own_losses.reshape(-1), grad_projection)


def shards(
    tokens,
    qkv_weight,
    qkv_bias,
    out_weight,
    out_bias,
    norm1_gain,
    norm1_bias,
    up_weight,
    up_bias,
    down_weight,
    down_bias,
    norm2_gain,
    norm2_bias,
    proj_weight,
    doc_lengths,
    pair_docs,
):
    section_index = lax.axis_index("section")
    dp_index = lax.axis_index("dp")
    count = lax.axis_size("dp")
    dims = grid_of(count)
    is_first = section_index == 0
    last_scale = section_index.astype(jnp.float32)
    model_width = tokens.shape[1]
    small = (
        qkv_bias,
        out_bias,
        norm1_gain,
        norm1_bias,
        up_bias,
        down_bias,
        norm2_gain,
        norm2_bias,
        proj_weight.reshape(1, -1),
    )
    widths = [value.shape[1] for value in small]
    together = spread(jnp.concatenate(small, axis=1)[0], count)
    cuts, start = [], 0
    for width in widths:
        cuts.append(together[:, start : start + width].reshape(-1))
        start += width
    qkv_b, out_b, gain_one, bias_one, up_b, down_b, gain_two, bias_two, projection = cuts
    projection = projection.reshape(model_width, -1)
    qkv_w, out_w, up_w, down_w = gather_rows(
        [qkv_weight[0], out_weight[0], up_weight[0], down_weight[0]], dims, dp_index
    )
    weights = (
        qkv_w,
        qkv_b,
        out_w,
        out_b,
        gain_one,
        bias_one,
        up_w,
        up_b,
        down_w,
        down_b,
        gain_two,
        bias_two,
    )
    layouts = [doc_layout(doc_lengths[micro_step]) for micro_step in range(MICRO)]
    blank_rows = jnp.zeros((ROWS, model_width), jnp.bfloat16)
    arrived = blank_rows
    states = []
    for tick_step in range(MICRO + 1):
        first_micro = min(tick_step, MICRO - 1)
        second_micro = max(tick_step - 1, 0)
        own_rows = (
            tokens[tick_step * ROWS : (tick_step + 1) * ROWS] if tick_step < MICRO else blank_rows
        )
        source = jnp.where(is_first, own_rows, arrived)
        segment = jnp.where(is_first, layouts[first_micro][0], layouts[second_micro][0])
        position = jnp.where(is_first, layouts[first_micro][1], layouts[second_micro][1])
        states.append(layer_forward(source, weights, segment, position))
        if tick_step < MICRO:
            arrived = from_behind(states[-1][-1], "section", 1)
    results = [state[-1] for state in states]
    activations = jnp.concatenate(
        [
            jnp.where(is_first, results[micro_step], results[micro_step + 1])
            for micro_step in range(MICRO)
        ],
        axis=0,
    )[None]
    loss_grads, own_losses, proj_total = loss_parts(
        jnp.stack(results[1:]),
        projection,
        jnp.cumsum(doc_lengths, axis=1),
        jnp.moveaxis(pair_docs.reshape(count, MICRO, QRY_DEV, CANDS), 1, 0).reshape(
            MICRO, count * QRY_DEV, CANDS
        ),
        dp_index,
        count,
    )
    query_losses = jnp.where(is_first, from_behind(own_losses, "section", -1), own_losses)
    proj_total = proj_total * last_scale
    back_grad = jnp.zeros((ROWS, model_width), jnp.float32)
    input_grads, pairs, vectors = [], [], None
    for tick_step in range(MICRO + 1):
        second_micro = MICRO - 1 - tick_step
        upstream = jnp.where(
            is_first,
            back_grad,
            loss_grads[second_micro] if second_micro >= 0 else jnp.zeros_like(back_grad),
        )
        tick_pairs, tick_vectors, grad_source = layer_backward(
            states[MICRO - tick_step], upstream, weights
        )
        pairs.append(tick_pairs)
        vectors = (
            tick_vectors
            if vectors is None
            else tuple(total + extra for total, extra in zip(vectors, tick_vectors))
        )
        input_grads.append(grad_source)
        if second_micro >= 0:
            back_grad = from_behind(grad_source.astype(jnp.bfloat16), "section", -1).astype(
                jnp.float32
            )
    weight_grads = []
    for number in range(4):
        left, right = (
            jnp.concatenate(
                [pairs[1][number][side]]
                + [jnp.where(is_first, pairs[2][number][side], pairs[0][number][side])]
            )
            for side in range(2)
        )
        weight_grads.append(scatter_rows(left, right, dims, dp_index)[None])
    grad_down, grad_up, grad_out, grad_qkv = weight_grads
    own = summed(jnp.concatenate([value.reshape(count, -1) for value in vectors], axis=1))
    small_grads, start = [], 0
    for width in widths[:-1]:
        small_grads.append(own[None, start : start + width])
        start += width
    proj_parts = proj_total.reshape(2, count, -1, proj_total.shape[1])
    proj_own = summed(jnp.swapaxes(proj_parts, 0, 1))
    proj_grad = jnp.where(is_first, from_behind(proj_own[0], "section", -1), proj_own[1])
    grad_inputs = jnp.concatenate(
        [
            jnp.where(
                is_first, input_grads[MICRO - micro_step], input_grads[MICRO - 1 - micro_step]
            )
            for micro_step in range(MICRO)
        ],
        axis=0,
    )[None]
    return (
        query_losses,
        activations,
        grad_inputs,
        grad_qkv,
        small_grads[0],
        grad_out,
        small_grads[1],
        small_grads[2],
        small_grads[3],
        grad_up,
        small_grads[4],
        grad_down,
        small_grads[5],
        small_grads[6],
        small_grads[7],
        proj_grad,
    )


def solution(mesh):
    in_specs = (
        P("dp", None),
        P("section", "dp", None),
        P("section", "dp"),
        P("section", "dp", None),
        P("section", "dp"),
        P("section", "dp"),
        P("section", "dp"),
        P("section", "dp", None),
        P("section", "dp"),
        P("section", "dp", None),
        P("section", "dp"),
        P("section", "dp"),
        P("section", "dp"),
        P("dp", None),
        P("dp", None),
        P(),
    )
    out_specs = (
        P("dp"),
        P("section", "dp", None),
        P("section", "dp", None),
        P("section", "dp", None),
        P("section", "dp"),
        P("section", "dp", None),
        P("section", "dp"),
        P("section", "dp"),
        P("section", "dp"),
        P("section", "dp", None),
        P("section", "dp"),
        P("section", "dp", None),
        P("section", "dp"),
        P("section", "dp"),
        P("section", "dp"),
        P(("section", "dp"), None),
    )
    return jax.shard_map(shards, mesh=mesh, in_specs=in_specs, out_specs=out_specs, check_vma=False)
```

```python
from functools import partial
import math

import jax
import jax.numpy as jnp
from jax import lax
from jax.experimental import pallas as pl
from jax.experimental.pallas import tpu as pltpu
from jax.sharding import PartitionSpec as P

HEAD = 64
PROJ = 128
QLEN = 32
DOC_ROWS = 192
QRY_DEV = 2
DOCS_DEV = 3
MICRO = 2
CANDS = 8
ROWS = 256
PREFIXES = (PROJ // 2, 3 * PROJ // 4, PROJ)


norm_eps = 1e-05
unit_eps = 1e-06
sharpness = 20.0
score_scale = 0.125
masked_score = -1000000000.0


def from_behind(value, axis, steps):
    count = lax.axis_size(axis)
    first, last = (max(0, -steps), min(count, count - steps))
    return lax.ppermute(value, axis, [(source, source + steps) for source in range(first, last)])


def product(left_side, right_side):
    return jnp.dot(left_side, right_side, preferred_element_type=jnp.float32)


def product_tn(left_side, right_side):
    return lax.dot_general(
        left_side, right_side, (((0,), (0,)), ((), ())), preferred_element_type=jnp.float32
    )


def product_nt(left_side, right_side):
    return lax.dot_general(
        left_side, right_side, (((1,), (1,)), ((), ())), preferred_element_type=jnp.float32
    )


def doc_layout(doc_lens):
    row_ids = jnp.arange(ROWS, dtype=jnp.int32)
    ends_at = jnp.cumsum(doc_lens)
    starts_at = ends_at - doc_lens
    doc_of = jnp.sum((row_ids[:, None] >= ends_at[None, :]).astype(jnp.int32), axis=1)
    doc_index = jnp.arange(DOCS_DEV, dtype=jnp.int32)
    begins = jnp.sum(
        jnp.where(doc_of[:, None] == doc_index[None, :], starts_at[None, :], 0), axis=1
    )
    in_docs = row_ids < DOC_ROWS
    query_rows = jnp.maximum(row_ids - DOC_ROWS, 0)
    segment = jnp.where(in_docs, doc_of, DOCS_DEV + query_rows // QLEN)
    position = jnp.where(in_docs, row_ids - begins, query_rows % QLEN)
    return (segment, position)


def rotary(position):
    step_ids = jnp.arange(HEAD // 2, dtype=jnp.int32).astype(jnp.float32)
    frequency = jnp.exp(step_ids * (-2.0 * math.log(10000.0) / HEAD))
    angles = position.astype(jnp.float32)[..., None] * frequency
    cosine, sine = jnp.cos(angles), jnp.sin(angles)
    return (
        jnp.concatenate([cosine] * 4, axis=-1),
        jnp.concatenate([-sine, sine] * 2, axis=-1),
    )


def lane_ids():
    return lax.broadcasted_iota(jnp.int32, (1, 2 * HEAD), 1)


def turned(value, cosine, sine):
    in_first = lane_ids() % HEAD < HEAD // 2
    ahead = pltpu.roll(value, 2 * HEAD - HEAD // 2, 1)
    behind = pltpu.roll(value, HEAD // 2, 1)
    return value * cosine + jnp.where(in_first, ahead, behind) * sine


def statistics(values):
    center = values - jnp.mean(values, axis=1, keepdims=True)
    spread = jnp.mean(center * center, axis=1, keepdims=True)
    scale = lax.rsqrt(spread + norm_eps)
    return center * scale, scale


def norm_back(grad, unit, scale, gain):
    inner = grad * gain
    along = jnp.mean(inner * unit, axis=1, keepdims=True)
    grad_in = scale * (inner - jnp.mean(inner, axis=1, keepdims=True) - unit * along)
    return grad_in, jnp.sum(grad * unit, axis=0, keepdims=True), jnp.sum(grad, axis=0, keepdims=True)


def gelu_parts(value):
    bell = jnp.exp(-0.5 * value * value)
    part = 1.0 / (1.0 + (0.3275911 * math.sqrt(0.5)) * jnp.abs(value))
    tail = 0.5 * 1.061405429 * part - 0.5 * 1.453152027
    tail = tail * part + 0.5 * 1.421413741
    tail = tail * part - 0.5 * 0.284496736
    tail = tail * part + 0.5 * 0.254829592
    tail = tail * part * bell
    below = jnp.where(value >= 0, 1.0 - tail, tail)
    return value * below, below + value * bell * (1.0 / math.sqrt(2.0 * math.pi))


def probabilities(queries, keys, allowed, held):
    scores = product_nt(jnp.where(held, queries, jnp.zeros_like(queries)), keys)
    scores = jnp.where(allowed, scores, masked_score)
    scores = jnp.exp(scores - jnp.max(scores, axis=1, keepdims=True))
    return scores * (1.0 / jnp.sum(scores, axis=1, keepdims=True))


LOW, WIDE = jnp.bfloat16, jnp.float32
VMEM_LIMIT = 52 << 20
BLOCK = 512
NO_COST = pl.CostEstimate(flops=1, bytes_accessed=1, transcendentals=0)
FULL_COST = pl.CostEstimate(flops=40 * 10**9, bytes_accessed=10**8, transcendentals=0)


class Weight:
    def __init__(self, places, rows, columns, width, parts):
        self.places, self.rows, self.columns, self.width = places, rows, columns, width
        self.count = places.shape[0]
        self.height = self.count * rows
        self.arrays = [group for _, _, groups in parts for group in groups]
        self.plan = [
            (start, width, [group.shape[0] for group in groups]) for start, width, groups in parts
        ]

    def scratch(self):
        return [
            pltpu.VMEM((self.height, self.columns), LOW),
            pltpu.SemaphoreType.DMA((self.columns // self.width, self.count)),
        ]


class Fetch:
    def __init__(self, weight, places_ref, refs, buffer, sems):
        self.weight, self.places_ref = weight, places_ref
        self.refs, self.buffer, self.sems = refs, buffer, sems
        self.waited = set()

    def copies(self, number):
        weight, begin = self.weight, number * self.weight.width
        passed = 0
        for start, width, lengths in weight.plan:
            if start <= begin < start + width:
                break
            passed += len(lengths)
        columns = pl.ds(begin - start, weight.width)
        block = 0
        for group, length in enumerate(lengths):
            for inner in range(length):
                place = pl.multiple_of(self.places_ref[block] * weight.rows, weight.rows)
                yield pltpu.make_async_copy(
                    self.refs[passed + group].at[inner, pl.ds(0, weight.rows), columns],
                    self.buffer.at[pl.ds(place, weight.rows), pl.ds(begin, weight.width)],
                    self.sems.at[number, block],
                )
                block += 1

    def start(self):
        for number in range(self.weight.columns // self.weight.width):
            for copy in self.copies(number):
                copy.start()

    def ready(self, until=None):
        until = self.weight.columns if until is None else until
        for number in range(-(-until // self.weight.width)):
            if number not in self.waited:
                self.waited.add(number)
                for copy in self.copies(number):
                    copy.wait()
        return self.buffer


class Parts:
    def __init__(self, refs, loads, weights, outs, scratch):
        self.pick, self.places, *refs = refs
        loaded, refs = refs[: len(loads)], refs[len(loads) :]
        fetched = {}
        for name, weight in weights.items():
            fetched[name], refs = refs[: len(weight.arrays)], refs[len(weight.arrays) :]
        stored, refs = refs[: len(outs)], refs[len(outs) :]
        self.buffers, refs = dict(zip(loads, refs)), refs[len(loads) :]
        self.weights = {}
        for name, weight in weights.items():
            buffer, sems, *refs = refs
            self.weights[name] = Fetch(weight, self.places, fetched[name], buffer, sems)
        self.outs, refs = dict(zip(outs, refs)), refs[len(outs) :]
        self.scratch, refs = dict(zip(scratch, refs)), refs[len(scratch) :]
        load_sems, out_sems = refs
        self.loads = {
            name: pltpu.make_async_copy(ref, self.buffers[name], load_sems.at[number])
            for number, (name, ref) in enumerate(zip(loads, loaded))
        }
        self.stores = {
            name: pltpu.make_async_copy(self.outs[name], ref, out_sems.at[number])
            for number, (name, ref) in enumerate(zip(outs, stored))
        }
        self.waited = set()

    def start(self, order):
        for name in order:
            (self.loads[name] if name in self.loads else self.weights[name]).start()

    def ref(self, name):
        if name in self.outs:
            return self.outs[name]
        if name in self.scratch:
            return self.scratch[name]
        if name not in self.waited:
            self.waited.add(name)
            self.loads[name].wait()
        return self.buffers[name]

    def refs(self, *names):
        return [self.ref(name) for name in names]

    def leave(self, *names):
        for name in names:
            self.stores[name].start()

    def finish(self):
        for name in self.stores:
            self.stores[name].wait()


def run_parts(name, bodies, pick, places, loads, weights, outs, scratch, order, cost):
    def kernel(*refs):
        parts = Parts(refs, list(loads), weights, list(outs), list(scratch))
        parts.start(order)
        for body in bodies:
            body(parts)
        parts.finish()

    arrays = [*loads.values(), *(array for weight in weights.values() for array in weight.arrays)]
    results = pl.pallas_call(
        kernel,
        in_specs=[pl.BlockSpec(memory_space=pltpu.SMEM)] * 2
        + [pl.BlockSpec(memory_space=pl.ANY)] * len(arrays),
        out_specs=[pl.BlockSpec(memory_space=pltpu.HBM)] * len(outs),
        out_shape=[pltpu.HBM(*out) for out in outs.values()],
        scratch_shapes=[pltpu.VMEM(array.shape, array.dtype) for array in loads.values()]
        + [entry for weight in weights.values() for entry in weight.scratch()]
        + [pltpu.VMEM(*out) for out in outs.values()]
        + list(scratch.values())
        + [pltpu.SemaphoreType.DMA((len(loads),)), pltpu.SemaphoreType.DMA((len(outs),))],
        compiler_params=pltpu.CompilerParams(vmem_limit_bytes=VMEM_LIMIT),
        cost_estimate=cost,
        name=name,
    )(pick, places, *arrays)
    return dict(zip(outs, results))


def attend_part(parts):
    micro_step = parts.pick[1]
    source = parts.ref("x")
    cos_ref, sin_ref, column_ref, row_ref, bias_ref = parts.refs(
        "cosine", "sine", "column", "row", "qkv_bias"
    )
    cosine, sine = cos_ref[micro_step], sin_ref[micro_step]
    outs = parts.refs("q", "k", "v")
    width = source.shape[1]
    for part, ref in enumerate(outs):
        qkv = parts.weights["qkv"].ready((part + 1) * width)
        for start in range(0, width, BLOCK):
            at = slice(part * width + start, part * width + start + BLOCK)
            value = product(source[...], qkv[:, at])
            value = value + bias_ref[part : part + 1, start : start + BLOCK]
            for pair in range(0, BLOCK, 2 * HEAD):
                two = value[:, pair : pair + 2 * HEAD]
                if part < 2:
                    two = turned(two, cosine, sine)
                ref[:, start + pair : start + pair + 2 * HEAD] = two.astype(LOW)
    parts.leave("q", "k", "v")
    allowed = column_ref[micro_step] == row_ref[micro_step]
    q_ref, k_ref, v_ref = outs
    mixture_ref, sum_ref, norm_ref, small_ref = parts.refs("mixture", "sum_one", "norm", "small")
    for start in range(0, width, 2 * HEAD):
        at = slice(start, start + 2 * HEAD)
        queries = q_ref[:, at] * LOW(score_scale)
        keys, values = k_ref[:, at], v_ref[:, at]
        mixed = []
        for head in range(2):
            held = lane_ids() // HEAD == head
            attention = probabilities(queries, keys, allowed, held)
            mixed.append(product(attention.astype(LOW), values))
        mixture_ref[:, at] = jnp.where(lane_ids() < HEAD, mixed[0], mixed[1]).astype(LOW)
    out = parts.weights["out"].ready()
    for start in range(0, width, BLOCK):
        at = slice(start, start + BLOCK)
        sum_ref[:, at] = (
            source[:, at].astype(WIDE)
            + small_ref[0:1, at]
            + product(mixture_ref[...], out[:, at])
        )
    unit, _ = statistics(sum_ref[...])
    norm_ref[...] = (unit * small_ref[1:2] + small_ref[2:3]).astype(LOW)
    parts.leave("mixture", "sum_one", "norm")


def up_part(parts):
    norm_ref, bias_ref, active_ref, slope_ref = parts.refs("norm", "up_bias", "active", "slope")
    for start in range(0, active_ref.shape[1], BLOCK):
        up = parts.weights["up"].ready(start + BLOCK)
        at = slice(start, start + BLOCK)
        active, slope = gelu_parts(product(norm_ref[...], up[:, at]) + bias_ref[:, at])
        active_ref[:, at] = active.astype(LOW)
        slope_ref[:, at] = slope.astype(LOW)
    parts.leave("active", "slope")


def down_part(parts):
    active_ref, norm_ref, small_ref = parts.refs("active", "norm", "small")
    sum_ref, result_ref = parts.refs("sum_two", "result")
    for start in range(0, sum_ref.shape[1], BLOCK):
        at = slice(start, start + BLOCK)
        down = parts.weights["down"].ready(start + BLOCK)
        sum_ref[:, at] = (
            norm_ref[:, at].astype(WIDE)
            + small_ref[3:4, at]
            + product(active_ref[...], down[:, at])
        )
    unit, _ = statistics(sum_ref[...])
    result = (unit * small_ref[4:5] + small_ref[5:6]).astype(LOW)
    result_ref[...] = result
    parts.leave("result", "sum_two")
    if "embedded" in parts.outs:
        parts.ref("embedded")[...] = product(result, parts.ref("projection")[...]).astype(LOW)
        parts.leave("embedded")
    if "activations" in parts.outs:
        early, late, own, both = parts.refs("early", "late", "own", "activations")

        @pl.when(parts.pick[0] == 1)
        def _():
            both[:ROWS] = early[...]
            both[ROWS:] = late[...]

        @pl.when(parts.pick[0] == 0)
        def _():
            both[:ROWS] = own[...]
            both[ROWS:] = result

        parts.leave("activations")


def feed_back_part(parts):
    if "docs" in parts.loads:
        own = jnp.sum(parts.ref("own_parts")[...].astype(WIDE), axis=0)
        embedded = jnp.concatenate([parts.ref("docs")[...], own], axis=0).astype(LOW)
        parts.ref("grad_embedded")[...] = embedded
        parts.leave("grad_embedded")
        upstream = product_nt(embedded, parts.ref("projection")[...])
        upstream = upstream * (1 - parts.pick[0]).astype(WIDE)
    else:
        upstream = parts.ref("back")[...].astype(WIDE)
    branch_ref, gate_ref, attended_ref = parts.refs("branch", "gate", "attended")
    vector_ref, up_bias_ref, total, small_ref = parts.refs("vectors", "grad_up_bias", "total", "small")
    unit, scale = statistics(parts.ref("sum_two")[...])
    grad, gain, bias = norm_back(upstream, unit, scale, small_ref[4:5])
    low = grad.astype(LOW)
    branch_ref[...] = low
    vector_ref[...] = jnp.zeros_like(vector_ref)
    vector_ref[3:4] = jnp.sum(low.astype(WIDE), axis=0, keepdims=True)
    vector_ref[4:5] = gain
    vector_ref[5:6] = bias
    total[...] = grad
    parts.leave("branch")
    slope_ref = parts.ref("slope")
    down = parts.weights["down"].ready()
    for start in range(0, gate_ref.shape[1], BLOCK):
        at = slice(start, start + BLOCK)
        gate = product_nt(branch_ref[...], down[at]) * slope_ref[:, at].astype(WIDE)
        gate = gate.astype(LOW)
        gate_ref[:, at] = gate
        up_bias_ref[:, at] = jnp.sum(gate.astype(WIDE), axis=0, keepdims=True)
    parts.leave("gate", "grad_up_bias")
    up = parts.weights["up"].ready()
    for start in range(0, total.shape[1], BLOCK):
        at = slice(start, start + BLOCK)
        total[:, at] += product_nt(gate_ref[...], up[at])
    unit, scale = statistics(parts.ref("sum_one")[...])
    grad, gain, bias = norm_back(total[...], unit, scale, small_ref[1:2])
    total[...] = grad
    low = grad.astype(LOW)
    attended_ref[...] = low
    vector_ref[0:1] = jnp.sum(low.astype(WIDE), axis=0, keepdims=True)
    vector_ref[1:2] = gain
    vector_ref[2:3] = bias
    parts.leave("attended", "vectors")
    if "grad_one" in parts.outs:
        parts.ref("grad_one")[...] = grad
        parts.leave("grad_one")


def attend_back_part(parts):
    micro_step = parts.pick[1]
    attended_ref, mixed_ref, vector_ref, mixture, total = parts.refs(
        "attended", "mixed", "qkv_vectors", "mixture", "total"
    )
    cos_ref, sin_ref, column_ref, row_ref = parts.refs("cosine", "sine", "column", "row")
    cosine, sine = cos_ref[micro_step], sin_ref[micro_step]
    allowed = column_ref[micro_step] == row_ref[micro_step]
    width = mixture.shape[1]
    if "grad_one" in parts.loads:
        total[...] = parts.ref("grad_one")[...]
    out = parts.weights["out"].ready()
    for start in range(0, width, BLOCK):
        at = slice(start, start + BLOCK)
        mixture[:, at] = product_nt(attended_ref[...], out[at]).astype(LOW)
    q_ref, k_ref, v_ref = parts.refs("q", "k", "v")
    for start in range(0, width, 2 * HEAD):
        at = slice(start, start + 2 * HEAD)
        queries, keys, values = q_ref[:, at], k_ref[:, at], v_ref[:, at]
        scaled = queries * LOW(score_scale)
        grad_mixture = mixture[:, at]
        grads = []
        for head in range(2):
            held = lane_ids() // HEAD == head
            attention = probabilities(scaled, keys, allowed, held)
            own = jnp.where(held, grad_mixture, jnp.zeros_like(grad_mixture))
            grad_attention = product_nt(own, values)
            grad_values = product_tn(attention.astype(LOW), own)
            along = jnp.sum(grad_attention * attention, axis=1, keepdims=True)
            grad_scores = (attention * (grad_attention - along)).astype(LOW)
            grads.append((product(grad_scores, keys), product_tn(grad_scores, queries), grad_values))
        first_head = lane_ids() < HEAD
        for part in range(2):
            value = jnp.where(first_head, grads[0][part], grads[1][part]) * score_scale
            mixed_ref[part, :, at] = turned(value, cosine, -sine).astype(LOW)
        mixed_ref[2, :, at] = (grads[0][2] + grads[1][2]).astype(LOW)
    parts.leave("mixed")
    vector_ref[...] = jnp.zeros_like(vector_ref)
    for part in range(3):
        vector_ref[part : part + 1] = jnp.sum(
            mixed_ref[part].astype(WIDE), axis=0, keepdims=True
        )
    parts.leave("qkv_vectors")
    qkv = parts.weights["qkv"].ready()
    for start in range(0, width, BLOCK):
        at = slice(start, start + BLOCK)
        value = total[:, at]
        for part in range(3):
            value = value + product_nt(mixed_ref[part], qkv[at, part * width : (part + 1) * width])
        total[:, at] = value
    if "grad_low" in parts.outs:
        parts.ref("grad_low")[...] = total[...].astype(LOW)
        parts.leave("grad_low")
        parts.ref("grad_source")[...] = total[...]
    else:
        late, early, own, source_ref = parts.refs("late", "early", "own", "grad_source")

        @pl.when(parts.pick[0] == 1)
        def _():
            source_ref[:ROWS] = total[...]
            source_ref[ROWS:] = own[...]

        @pl.when(parts.pick[0] == 0)
        def _():
            source_ref[:ROWS] = early[...]
            source_ref[ROWS:] = late[...]

    parts.leave("grad_source")


class Layer:
    def __init__(self, places, layout):
        self.places = places
        self.layout = dict(zip(("cosine", "sine", "column", "row"), layout))

    def attend_set(self, source):
        rows = source.shape
        return (
            {"x": source, **self.layout, "qkv_bias": self.qkv_bias, "small": self.small},
            {"qkv": self.qkv, "out": self.out},
            {
                "q": (rows, LOW),
                "k": (rows, LOW),
                "v": (rows, LOW),
                "mixture": (rows, LOW),
                "sum_one": (rows, WIDE),
                "norm": (rows, LOW),
            },
            {},
        )

    def up_set(self):
        rows = (ROWS, self.up.columns)
        return (
            {"up_bias": self.up_bias},
            {"up": self.up},
            {"active": (rows, LOW), "slope": (rows, LOW)},
            {},
        )

    def down_set(self, projection, earlier):
        rows = (ROWS, self.down.columns)
        loads = {"small": self.small}
        outs = {"sum_two": (rows, WIDE), "result": (rows, LOW)}
        if projection is not None:
            loads["projection"] = projection
            outs["embedded"] = ((ROWS, PROJ), LOW)
        if earlier:
            loads |= dict(zip(("early", "late", "own"), earlier))
            outs["activations"] = ((MICRO * ROWS, self.down.columns), LOW)
        return loads, {"down": self.down}, outs, {}

    def run(self, name, bodies, sets, pick, more=None, cost=NO_COST):
        loads, weights, outs, scratch = dict(more or {}), {}, {}, {}
        order = list(loads)
        for one in sets:
            order += [key for key in (*one[0], *one[1]) if key not in order]
            loads, weights = loads | one[0], weights | one[1]
            outs, scratch = outs | one[2], scratch | one[3]
        return run_parts(
            name, bodies, pick, self.places, loads, weights, outs, scratch, order, cost
        )

    def attend(self, source, pick):
        return self.run("attend", [attend_part], [self.attend_set(source)], pick)

    def rise(self, norm, pick):
        return self.run("up", [up_part], [self.up_set()], pick, {"norm": norm})

    def fall(self, active, norm, pick):
        return self.run(
            "down", [down_part], [self.down_set(None, ())], pick, {"active": active, "norm": norm}
        )

    def forward(self, source, pick, projection, earlier):
        return self.run(
            "forward",
            [attend_part, up_part, down_part],
            [self.attend_set(source), self.up_set(), self.down_set(projection, earlier)],
            pick,
            cost=FULL_COST,
        )

    def feed_back_set(self, state, loss_grads, back_grad):
        rows, hidden = (ROWS, self.down.columns), self.up.columns
        loads, outs = {}, {}
        if loss_grads is not None:
            loads |= dict(zip(("docs", "own_parts", "projection"), loss_grads))
            outs["grad_embedded"] = ((ROWS, PROJ), LOW)
        if back_grad is not None:
            loads["back"] = back_grad
        loads |= {"sum_two": state["sum_two"], "small": self.small, "slope": state["slope"]}
        outs |= {
            "branch": (rows, LOW),
            "gate": ((ROWS, hidden), LOW),
            "attended": (rows, LOW),
            "vectors": ((8, rows[1]), WIDE),
            "grad_up_bias": ((1, hidden), WIDE),
        }
        return (
            loads,
            {"down": self.down, "up": self.up},
            outs,
            {"total": pltpu.VMEM(rows, WIDE)},
        )

    def attend_back_set(self, state, earlier):
        rows = (ROWS, self.out.columns)
        outs = {"mixed": ((3, *rows), LOW), "qkv_vectors": ((8, rows[1]), WIDE)}
        loads = {"q": state["q"], "k": state["k"], "v": state["v"], **self.layout}
        if earlier:
            loads |= dict(zip(("late", "early", "own"), earlier))
            outs["grad_source"] = ((MICRO * ROWS, rows[1]), WIDE)
        else:
            outs |= {"grad_source": (rows, WIDE), "grad_low": (rows, LOW)}
        return (
            loads,
            {"out": self.out, "qkv": self.qkv},
            outs,
            {"mixture": pltpu.VMEM(rows, LOW), "total": pltpu.VMEM(rows, WIDE)},
        )

    def backward(self, state, loss_grads, back_grad, pick):
        return self.run(
            "backward",
            [feed_back_part, attend_back_part],
            [
                self.feed_back_set(state, loss_grads, back_grad),
                ({"sum_one": state["sum_one"]}, {}, {}, {}),
                self.attend_back_set(state, ()),
            ],
            pick,
            cost=FULL_COST,
        )

    def feed_back(self, state, back_grad, pick):
        rows = (ROWS, self.down.columns)
        return self.run(
            "feed_back",
            [feed_back_part],
            [
                self.feed_back_set(state, None, back_grad),
                ({"sum_one": state["sum_one"]}, {}, {"grad_one": (rows, WIDE)}, {}),
            ],
            pick,
        )

    def attend_back(self, state, attended, grad_one, earlier, pick):
        return self.run(
            "attend_back",
            [attend_back_part],
            [self.attend_back_set(state, earlier)],
            pick,
            {"attended": attended, "grad_one": grad_one},
        )


def grid_of(count):
    dims = []
    while count % 2 == 0:
        dims.append(2)
        count //= 2
    return ([count] if count > 1 else []) + dims


def coordinates(dims, number):
    at = []
    for size in reversed(dims):
        at.append(number % size)
        number = number // size
    return at[::-1]


def shifted(value, dims, dim, steps):
    count = math.prod(dims)
    stride = math.prod(dims[dim + 1 :])
    pairs = []
    for source in range(count):
        place = (source // stride) % dims[dim]
        pairs.append((source, source + ((place + steps) % dims[dim] - place) * stride))
    return lax.ppermute(value, "dp", pairs)


def after(value, *earlier):
    return lax.optimization_barrier((value, *earlier))[0]


def stage(sends, dims, earlier):
    values = lax.optimization_barrier((*(value for value, _, _ in sends), *earlier))
    arrived = [
        shifted(value, dims, dim, steps) for value, (_, dim, steps) in zip(values, sends)
    ]
    return list(lax.optimization_barrier(tuple(arrived)))


def rows_kernel(top, places, *refs):
    pieces, out, sems = refs[:-2], refs[-2], refs[-1]
    copies = []
    for group in pieces:
        for inner in range(group.shape[0]):
            number = len(copies)
            copies.append(
                pltpu.make_async_copy(
                    group.at[inner, pl.ds(top, out.shape[1])],
                    out.at[places[number]],
                    sems.at[number],
                )
            )
    for copy in copies:
        copy.start()
    for copy in copies:
        copy.wait()


def placed_rows(groups, places, top, rows):
    count, columns = places.shape[0], groups[0].shape[2]
    return pl.pallas_call(
        partial(rows_kernel, top),
        out_shape=jax.ShapeDtypeStruct((count, rows, columns), groups[0].dtype),
        in_specs=[pl.BlockSpec(memory_space=pltpu.SMEM)]
        + [pl.BlockSpec(memory_space=pl.ANY)] * len(groups),
        out_specs=pl.BlockSpec(memory_space=pltpu.VMEM),
        scratch_shapes=[pltpu.SemaphoreType.DMA((count,))],
        name="place",
    )(places, *groups)


class Gather:
    def __init__(self, chunks, dims, at):
        self.dims, self.chunks = dims, chunks
        self.held = [[value[None]] for value in chunks]
        self.arrived, self.step = [], 0
        owners = jnp.zeros((1,), jnp.int32)
        for dim in range(len(dims)):
            steps = jnp.arange(dims[dim], dtype=jnp.int32)
            own = ((at[dim] - steps) % dims[dim]) * math.prod(dims[dim + 1 :])
            owners = (own[:, None] + owners[None, :]).reshape(-1)
        self.owners = owners

    def until(self, number):
        while self.step < number + len(self.dims):
            self.advance()
        return self.held[number]

    def advance(self, *earlier):
        sends, takers = [], []
        for dim in range(len(self.dims)):
            number = self.step - dim
            if 0 <= number < len(self.chunks):
                for steps in range(1, self.dims[dim]):
                    for group in self.held[number]:
                        sends.append((group, dim, steps))
                        takers.append(number)
        self.arrived = stage(sends, self.dims, [*self.arrived, *earlier])
        for number in sorted(set(takers)):
            got = [value for value, taker in zip(self.arrived, takers) if taker == number]
            if self.step - number < len(self.dims) - 2:
                self.held[number] = [jnp.concatenate(self.held[number] + got)]
            else:
                self.held[number] = self.held[number] + got
        self.step += 1


def scatter_rows_plain(left, right, dims, dp_index):
    count = math.prod(dims)
    at = [
        (dp_index // math.prod(dims[dim + 1 :])) % dims[dim] for dim in range(len(dims))
    ]
    samples, height = left.shape
    rows, columns = height // count, right.shape[1]
    split = left.reshape(samples, count // 2, 2, rows)
    for_other = lax.dynamic_index_in_dim(split, 1 - at[-1], 2, False).reshape(samples, -1)
    for_self = lax.dynamic_index_in_dim(split, at[-1], 2, False).reshape(samples, -1)
    sent = product_tn(for_other, right).astype(jnp.bfloat16)
    total = product_tn(for_self, right) + shifted(sent, dims, len(dims) - 1, 1).astype(jnp.float32)
    for dim in reversed(range(len(dims) - 1)):
        low = total.astype(jnp.bfloat16).reshape(-1, dims[dim], rows, columns)
        total = lax.dynamic_index_in_dim(low, at[dim], 1, False).astype(jnp.float32)
        for steps in range(1, dims[dim]):
            part = lax.dynamic_index_in_dim(low, (at[dim] + steps) % dims[dim], 1, False)
            total = total + shifted(part, dims, dim, steps).astype(jnp.float32)
    return total.reshape(rows, columns)


def fetch_chosen(pick_ref, pair, place, target, sem):
    for wanted, ref in ((1, pair[0]), (0, pair[1])):

        @pl.when(pick_ref[0] == wanted)
        def _(ref=ref):
            pltpu.make_async_copy(ref.at[place], target, sem).start()

    return pltpu.make_async_copy(pair[0].at[place], target, sem)


def grad_kernel(pick_ref, *refs, rows, slots, outer, start, sends):
    lefts, rights, refs = (refs[0:2], refs[2:4]), (refs[4:6], refs[6:8]), refs[8:]
    if not sends:
        other_ref, *refs = refs
    out_refs, refs = refs[: 1 if sends else slots], refs[1 if sends else slots :]
    if sends:
        left, right, out, left_sems, right_sems, out_sems = refs
    else:
        left, right, other, out, left_sems, right_sems, other_sems, out_sems = refs
    chips, width = outer * slots, right.shape[1]
    samples = lefts[0][0].shape[0]
    side = 1 - pick_ref[1] if sends else pick_ref[1]
    thin = rows % 128 != 0
    block = min(BLOCK, width) if thin else width
    blocks = width // block
    wide_part = rights[0][0].shape[-1]

    def left_copies(number):
        if thin:
            place, target = (slice(None), slice(None)), slice(None)
        else:
            chip = number if sends else chip_of(number)
            place = (slice(None), pl.ds(pl.multiple_of((2 * chip + side) * rows, rows), rows))
            target = slice(number * rows, (number + 1) * rows)
        return [
            fetch_chosen(
                pick_ref,
                lefts[half],
                place,
                left.at[half * samples : (half + 1) * samples, target],
                left_sems.at[number, half],
            )
            for half in range(2)
        ]

    def right_copies(number):
        begin = start + number * block
        columns = pl.ds(begin % wide_part, block)
        place = (slice(None), columns)
        if len(rights[0][0].shape) == 3:
            place = (begin // wide_part, *place)
        at = slice(number * block, (number + 1) * block)
        return [
            fetch_chosen(
                pick_ref,
                rights[half],
                place,
                right.at[half * samples : (half + 1) * samples, at],
                right_sems.at[number, half],
            )
            for half in range(2)
        ]

    def chip_of(number):
        return (number % outer) * slots + lax.rem(pick_ref[2] + number // outer, slots)

    def other_copy(number):
        if thin:
            return pltpu.make_async_copy(
                other_ref.at[pl.ds(0, chips * rows), pl.ds(start + number * block, block)],
                other.at[:, number * block : (number + 1) * block],
                other_sems.at[number],
            )
        return pltpu.make_async_copy(
            other_ref.at[
                pl.ds(pl.multiple_of(chip_of(number) * rows, rows), rows), pl.ds(start, width)
            ],
            other.at[number * rows : (number + 1) * rows],
            other_sems.at[number],
        )

    def wait(copies):
        for copy in copies:
            copy.wait()

    leaving = []
    if thin:
        halves_of_left = left_copies(0)
        arriving = [right_copies(number) for number in range(blocks)]
        if not sends:
            others = [other_copy(number) for number in range(blocks)]
            for copy in others:
                copy.start()
        wait(halves_of_left)
        flipped = left[...].T
        turned = jnp.concatenate(
            [
                jnp.where(
                    side == 0,
                    flipped[2 * rows * chip : 2 * rows * chip + rows],
                    flipped[2 * rows * chip + rows : 2 * rows * (chip + 1)],
                )
                for chip in range(chips)
            ]
        )
        for number in range(blocks):
            at = slice(number * block, (number + 1) * block)
            wait(arriving[number])
            result = product(turned, right[:, at])
            if sends:
                out[:, at] = result.astype(LOW)
                leaving.append(
                    pltpu.make_async_copy(out.at[:, at], out_refs[0].at[:, at], out_sems.at[number])
                )
                leaving[-1].start()
                continue
            others[number].wait()
            out[:, at] = (result + other[:, at].astype(WIDE)).astype(LOW)
            for place in range(chips):
                leaving.append(
                    pltpu.make_async_copy(
                        out.at[pl.ds(pl.multiple_of(chip_of(place) * rows, rows), rows), at],
                        out_refs[place // outer].at[place % outer, :, at],
                        out_sems.at[number * chips + place],
                    )
                )
                leaving[-1].start()
    else:
        arriving = right_copies(0)
        pieces = [left_copies(number) for number in range(chips)]
        if not sends:
            others = [other_copy(number) for number in range(chips)]
            for copy in others:
                copy.start()
        wait(arriving)
        for number in range(chips):
            at = slice(number * rows, (number + 1) * rows)
            wait(pieces[number])
            result = product_tn(left[:, at], right[...])
            if sends:
                out[at] = result.astype(LOW)
                target = out_refs[0].at[at]
            else:
                others[number].wait()
                out[at] = (result + other[at].astype(WIDE)).astype(LOW)
                target = out_refs[number // outer].at[number % outer]
            leaving.append(pltpu.make_async_copy(out.at[at], target, out_sems.at[number]))
            leaving[-1].start()
    wait(leaving)


def fold_kernel(pick_ref, held_ref, other_ref, out_ref, *send_refs, slots, thin_rows):
    for slot in range(slots):
        place = lax.rem(pick_ref[0] + slot, slots)
        for number in range(out_ref.shape[0]):
            index = number * slots + place
            value = held_ref[index].astype(WIDE) + other_ref[index].astype(WIDE)
            if slot == 0:
                out_ref[number] = value
                continue
            send_refs[slot - 1][number] = value.astype(LOW)
            if thin_rows:
                pair = value[thin_rows : thin_rows + 1] + value[thin_rows + 1 : thin_rows + 2]
                high, low = halves(pair)
                ids = lax.broadcasted_iota(jnp.int32, (16, value.shape[1]), 0)
                send_refs[slot - 1][number, thin_rows:] = jnp.where(
                    ids == 0, high.astype(WIDE), jnp.where(ids == 1, low.astype(WIDE), 0.0)
                ).astype(LOW)


def terms(value):
    high = lax.reduce_precision(value, 8, 7)
    return high.astype(LOW), (value - high).astype(LOW)


class Scatter:
    def __init__(self, name, lefts, rights, dims, at, first):
        self.name, self.lefts, self.rights, self.dims, self.at = name, lefts, rights, dims, at
        self.count = math.prod(dims)
        self.height = lefts[0][0].shape[1]
        self.rows = self.height // self.count
        sample = rights[0][0]
        self.columns = sample.shape[-1] * (3 if sample.ndim == 3 else 1)
        self.pick = jnp.stack([first, at[-1], at[-2]])

    def product(self, start, width, other, quick=False):
        samples = self.lefts[0][0].shape[0]
        half, rows, slots = self.height // 2, self.rows, self.dims[-2]
        chips = self.count // 2
        outer = chips // slots
        sends = other is None
        thin = rows % 128 != 0
        blocks = width // min(BLOCK, width) if thin else 1
        pieces = 1 if thin else chips
        anywhere = pl.BlockSpec(memory_space=pl.ANY)
        args = [*self.lefts[0], *self.lefts[1], *self.rights[0], *self.rights[1]]
        args += [] if sends else [other]
        out_sems = blocks * (1 if sends else chips) if thin else chips
        other_scratch = [] if sends else [pltpu.VMEM((half, width), LOW)]
        other_sems = [] if sends else [pltpu.SemaphoreType.DMA((blocks if thin else chips,))]
        outs = [(half, width)] if sends else [(outer, rows, width)] * slots
        return pl.pallas_call(
            partial(
                grad_kernel, rows=rows, slots=slots, outer=outer, start=start, sends=sends
            ),
            in_specs=[pl.BlockSpec(memory_space=pltpu.SMEM)] + [anywhere] * len(args),
            out_specs=[anywhere] * len(outs),
            out_shape=[jax.ShapeDtypeStruct(out, LOW) for out in outs],
            scratch_shapes=[
                pltpu.VMEM((2 * samples, self.height if thin else half), LOW),
                pltpu.VMEM((2 * samples, width), LOW),
                *other_scratch,
                pltpu.VMEM((half, width), LOW),
                pltpu.SemaphoreType.DMA((pieces, 2)),
                pltpu.SemaphoreType.DMA((blocks, 2)),
                *other_sems,
                pltpu.SemaphoreType.DMA((out_sems,)),
            ],
            compiler_params=pltpu.CompilerParams(vmem_limit_bytes=VMEM_LIMIT),
            cost_estimate=NO_COST if sends or quick else FULL_COST,
            name=self.name + ("_send" if sends else "_keep"),
        )(self.pick, *args)

    def send(self, extra=None):
        sent = self.product(0, self.columns, None)[0]
        self.extra = None
        if extra is not None:
            split = extra.reshape(-1, 2, extra.shape[1])
            sent = jnp.concatenate(
                [sent, *terms(lax.dynamic_index_in_dim(split, 1 - self.at[-1], 1, False))]
            )
        self.other = shifted(sent, self.dims, len(self.dims) - 1, 1)
        if extra is not None:
            held = lax.dynamic_index_in_dim(split, self.at[-1], 1, False)
            arrived = self.other[self.height // 2 :].astype(WIDE)
            held = held + arrived[: held.shape[0]] + arrived[held.shape[0] :]
            rows = jnp.stack(terms(held), axis=1)
            rows = jnp.pad(rows, [(0, 0), (0, 14), (0, 0)])
            self.extra = rows.reshape(-1, self.dims[-2], 16, extra.shape[1])

    def keep(self, start, width, quick=False):
        pieces = self.product(start, width, self.other, quick)
        if self.extra is not None:
            pieces = [
                jnp.concatenate(
                    [
                        piece,
                        lax.dynamic_index_in_dim(
                            self.extra, (self.at[-2] + slot) % self.dims[-2], 1, False
                        ),
                    ],
                    axis=1,
                )
                for slot, piece in enumerate(pieces)
            ]
        return pieces


def folded(held, moved, dims, dim, at, thin_rows):
    outer, rows, columns = held.shape
    slots = dims[dim]
    if rows % 16 == 0 and len(moved) == 1:
        whole = pl.BlockSpec(memory_space=pltpu.VMEM)
        shape = (outer // slots, rows, columns)
        total, *sends = pl.pallas_call(
            partial(fold_kernel, slots=slots, thin_rows=thin_rows),
            out_shape=[jax.ShapeDtypeStruct(shape, WIDE)]
            + [jax.ShapeDtypeStruct(shape, LOW)] * (slots - 1),
            in_specs=[pl.BlockSpec(memory_space=pltpu.SMEM), whole, whole],
            out_specs=[whole] * slots,
            compiler_params=pltpu.CompilerParams(vmem_limit_bytes=24 << 20),
            cost_estimate=NO_COST,
            name="fold",
        )(at[dim][None], held, moved[0])
        return total, sends
    total = held.astype(WIDE)
    for piece in moved:
        total = total + piece.astype(WIDE)
    split = total.reshape(outer // slots, slots, rows, columns)
    blocks = [
        lax.dynamic_index_in_dim(split, (at[dim] + steps) % slots, 1, False)
        for steps in range(slots)
    ]
    return blocks[0], [block.astype(LOW) for block in blocks[1:]]


def travels(makers, dims, at, own_rows, before):
    chip_dims = list(reversed(range(len(dims) - 1)))
    held, sends, sums = {}, {}, {}
    arrived = []
    for step in range(len(makers) + len(chip_dims) - 1):
        if step < len(makers):
            held[step], *sends[step] = makers[step](arrived)
        outgoing, takers = [], []
        for phase, dim in enumerate(chip_dims):
            number = step - phase
            if 0 <= number < len(makers):
                outgoing += [(value, dim, k) for k, value in enumerate(sends[number], start=1)]
                takers += [number] * len(sends[number])
        arrived = stage(outgoing, dims, [*arrived, *before.get(step, lambda _: ())(arrived)])
        for phase, dim in enumerate(chip_dims):
            number = step - phase
            if 0 <= number < len(makers):
                moved = [value for value, taker in zip(arrived, takers) if taker == number]
                if dim:
                    rows = held[number].shape[1]
                    held[number], sends[number] = folded(
                        held[number], moved, dims, dim - 1, at, own_rows if rows == own_rows + 16 else 0
                    )
                else:
                    total = held[number].astype(WIDE)
                    for piece in moved:
                        total = total + piece.astype(WIDE)
                    sums[number] = total.reshape(total.shape[-2:])
    return [sums[number] for number in range(len(makers))]


def spread(value, count):
    return lax.all_to_all(
        jnp.broadcast_to(value[None], (count, *value.shape)), "dp", 0, 0, tiled=True
    )


def summed(parts):
    return jnp.sum(lax.all_to_all(parts, "dp", 0, 0, tiled=True).astype(jnp.float32), axis=0)


def halves(value):
    high = value.astype(jnp.bfloat16)
    return high, (value - high.astype(jnp.float32)).astype(jnp.bfloat16)


def exact_product(left_side, right_side):
    high, low = halves(right_side)
    return product(left_side, high) + product(left_side, low)


def product_by_ones(left_side, right_side):
    high, low = halves(left_side)
    return product(high, right_side) + product(low, right_side)


def prefix_masks(length):
    places = lax.broadcasted_iota(jnp.int32, (1, length), 1)
    return [places < width for width in PREFIXES]


def similar_parts(documents, queries_t):
    docs_f32 = documents.astype(jnp.float32)
    squares = docs_f32 * docs_f32
    query_squares = queries_t * queries_t
    queries_low = queries_t.astype(jnp.bfloat16)
    parts = []
    for width, mask in zip(PREFIXES, prefix_masks(PROJ)):
        cut = jnp.where(mask, docs_f32, 0.0)
        doc_scale = lax.rsqrt(
            jnp.sum(jnp.where(mask, squares, 0.0), axis=1, keepdims=True) + unit_eps
        )
        query_scale = lax.rsqrt(
            jnp.sum(query_squares[:width], axis=0, keepdims=True) + unit_eps
        )
        cut = cut.astype(jnp.bfloat16)
        similar = product(cut, queries_low) * doc_scale * query_scale
        parts.append((cut, doc_scale, query_scale, similar))
    return parts


def members_of(ends_ref, micro_step, by_row):
    shape = (DOC_ROWS, 8) if by_row else (8, DOC_ROWS)
    rows = lax.broadcasted_iota(jnp.int32, shape, 0 if by_row else 1)
    docs = lax.broadcasted_iota(jnp.int32, shape, 1 if by_row else 0)
    inside = jnp.zeros(shape, jnp.float32)
    for number in range(DOCS_DEV):
        begin = ends_ref[micro_step, number - 1] if number else 0
        held = (docs == number) & (rows >= begin) & (rows < ends_ref[micro_step, number])
        inside = jnp.where(held, 1.0, inside)
    return inside.astype(jnp.bfloat16)


def query_of_token(tokens, by_token):
    shape = (tokens, 128) if by_token else (128, tokens)
    token = lax.broadcasted_iota(jnp.int32, shape, 0 if by_token else 1)
    query = lax.broadcasted_iota(jnp.int32, shape, 1 if by_token else 0)
    held = (token >= query * QLEN) & (token < query * QLEN + QLEN)
    return jnp.where(held, 1.0, 0.0).astype(jnp.bfloat16)


def score_kernel(ends_ref, queries_ref, docs_ref, out_ref, *, micro_step):
    tokens = queries_ref.shape[0] * queries_ref.shape[1]
    queries_t = queries_ref[...].astype(WIDE).reshape(tokens, PROJ).T
    members = members_of(ends_ref, micro_step, False)
    by_query = query_of_token(tokens, True)
    for number, (_, _, _, similar) in enumerate(similar_parts(docs_ref[:DOC_ROWS], queries_t)):
        masses = exact_product(members, jnp.exp(sharpness * similar))
        held = lax.broadcasted_iota(jnp.int32, masses.shape, 0) < DOCS_DEV
        logs = jnp.log(jnp.where(held, masses, 1.0))
        out_ref[0, number] = product_by_ones(logs, by_query) / sharpness


def loss_kernel(
    ends_ref, where_ref, queries_ref, docs_ref, tables_ref, times_ref, first_ref,
    loss_ref, grad_queries_ref, grad_docs_ref, table, *, micro_step
):
    step = pl.program_id(0)
    devices, width = queries_ref.shape[:2]
    tokens = devices * width
    queries_t = queries_ref[...].astype(WIDE).reshape(tokens, PROJ).T
    queries_low = queries_t.astype(LOW)
    members = members_of(ends_ref, micro_step, False)
    members_by_row = members_of(ends_ref, micro_step, True)
    spread_out = query_of_token(tokens, False)
    places = lax.broadcasted_iota(jnp.int32, (PROJ, 1), 0)
    grad_queries = jnp.zeros((PROJ, tokens), WIDE)
    grad_docs = jnp.zeros((DOC_ROWS, PROJ), WIDE)
    losses = jnp.zeros((1, 128), WIDE)
    times, first = times_ref[0], first_ref[0]
    own_rows = pl.ds(pl.multiple_of(where_ref[0] * 8, 8), 8)
    own_times, own_first = times_ref[0, own_rows], first_ref[0, own_rows]
    table[...] = jnp.zeros_like(table)
    for number, (cut, doc_scale, query_scale, similar) in enumerate(
        similar_parts(docs_ref[:DOC_ROWS], queries_t)
    ):
        for device in range(table.shape[0] // 8):
            table[8 * device : 8 * device + DOCS_DEV] = tables_ref[device, 0, number]
        scores = table[...]
        top = jnp.max(jnp.where(times > 0, scores, -1e30), axis=0, keepdims=True)
        top = jnp.where(top > -1e29, top, 0.0)
        normal = top + jnp.log(
            jnp.maximum(
                jnp.sum(times * jnp.exp(jnp.minimum(scores - top, 0.0)), axis=0, keepdims=True),
                1e-30,
            )
        )
        losses = losses + normal - jnp.sum(first * scores, axis=0, keepdims=True)
        own = table[own_rows]
        grad_score = own_times * jnp.exp(jnp.where(own_times > 0, own - normal, 0.0)) - own_first
        weights = jnp.exp(sharpness * similar)
        masses = exact_product(members, weights)
        by_token = product_by_ones(grad_score, spread_out)
        held = lax.broadcasted_iota(jnp.int32, masses.shape, 0) < DOCS_DEV
        by_token = jnp.where(held, by_token / jnp.where(held, masses, 1.0), 0.0)
        grad_similar = weights * exact_product(members_by_row, by_token)
        along = grad_similar * similar
        pulled = (grad_similar * doc_scale * query_scale).astype(LOW)
        mask = lax.broadcasted_iota(jnp.int32, (1, PROJ), 1) < PREFIXES[number]
        grad_docs = (
            grad_docs
            + jnp.where(mask, product_nt(pulled, queries_low), 0.0)
            - cut.astype(WIDE) * (doc_scale * doc_scale * jnp.sum(along, axis=1, keepdims=True))
        )
        toward = product_tn(cut, pulled)
        back = queries_t * (query_scale * query_scale * jnp.sum(along, axis=0, keepdims=True))
        grad_queries = grad_queries + toward - jnp.where(places < PREFIXES[number], back, 0.0)
    loss_ref[0] = losses
    grad_queries_ref[...] = grad_queries.T.reshape(devices, width, PROJ).astype(LOW)

    @pl.when(step == 0)
    def _():
        grad_docs_ref[...] = grad_docs

    @pl.when(step > 0)
    def _():
        grad_docs_ref[...] += grad_docs


class Loss:
    def __init__(self, micro_step, ends, pair_rows, dp_index, count):
        self.micro_step, self.ends, self.dp_index, self.count = micro_step, ends, dp_index, count
        self.group = math.gcd(count, 16)
        self.steps = count // self.group
        place = jnp.arange(8 * count, dtype=jnp.int32)
        doc_ids = jnp.where(place % 8 < DOCS_DEV, place // 8 * DOCS_DEV + place % 8, -1)
        picked = (pair_rows[None, :, :] == doc_ids[:, None, None]).astype(WIDE)
        self.times, self.first = [
            jnp.pad(
                jnp.swapaxes(value.reshape(8 * count, self.steps, -1), 0, 1),
                [(0, 0), (0, 0), (0, 128 - self.group * QRY_DEV)],
            )
            for value in (jnp.sum(picked, axis=2), picked[..., 0])
        ]
        self.params = dict(
            grid=(self.steps,), compiler_params=pltpu.CompilerParams(vmem_limit_bytes=VMEM_LIMIT)
        )
        self.queries_spec = pl.BlockSpec((self.group, QRY_DEV * QLEN, PROJ), lambda i: (i, 0, 0))
        self.smem = pl.BlockSpec(memory_space=pltpu.SMEM)

    def scores(self, embedded):
        self.embedded = embedded
        self.queries = spread(embedded[DOC_ROWS:], self.count)
        return pl.pallas_call(
            partial(score_kernel, micro_step=self.micro_step),
            out_shape=jax.ShapeDtypeStruct((self.steps, 3, 8, 128), WIDE),
            in_specs=[
                self.smem,
                self.queries_spec,
                pl.BlockSpec((ROWS, PROJ), lambda i: (0, 0)),
            ],
            out_specs=pl.BlockSpec((1, 3, 8, 128), lambda i: (i, 0, 0, 0)),
            name="scores",
            cost_estimate=NO_COST,
            **self.params,
        )(self.ends, self.queries, embedded)[:, :, :DOCS_DEV]

    def grads(self, tables, *earlier):
        losses, grad_queries, grad_docs = pl.pallas_call(
            partial(loss_kernel, micro_step=self.micro_step),
            out_shape=(
                jax.ShapeDtypeStruct((self.steps, 1, 128), WIDE),
                jax.ShapeDtypeStruct(self.queries.shape, LOW),
                jax.ShapeDtypeStruct((DOC_ROWS, PROJ), WIDE),
            ),
            in_specs=[
                self.smem,
                self.smem,
                self.queries_spec,
                pl.BlockSpec((ROWS, PROJ), lambda i: (0, 0)),
                pl.BlockSpec((self.count, 1, 3, DOCS_DEV, 128), lambda i: (0, i, 0, 0, 0)),
                pl.BlockSpec((1, 8 * self.count, 128), lambda i: (i, 0, 0)),
                pl.BlockSpec((1, 8 * self.count, 128), lambda i: (i, 0, 0)),
            ],
            out_specs=(
                pl.BlockSpec((1, 1, 128), lambda i: (i, 0, 0)),
                self.queries_spec,
                pl.BlockSpec((DOC_ROWS, PROJ), lambda i: (0, 0)),
            ),
            scratch_shapes=[pltpu.VMEM((8 * self.count, 128), WIDE)],
            name="losses",
            cost_estimate=NO_COST,
            **self.params,
        )(
            self.ends,
            self.dp_index[None],
            self.queries,
            after(self.embedded, *earlier),
            tables,
            self.times,
            self.first,
        )
        losses = losses[:, 0, : self.group * QRY_DEV].reshape(self.count * QRY_DEV)
        own = lax.dynamic_slice_in_dim(losses, self.dp_index * QRY_DEV, QRY_DEV, 0)
        return own, grad_queries, grad_docs


def shards(
    tokens,
    qkv_weight,
    qkv_bias,
    out_weight,
    out_bias,
    norm1_gain,
    norm1_bias,
    up_weight,
    up_bias,
    down_weight,
    down_bias,
    norm2_gain,
    norm2_bias,
    proj_weight,
    doc_lengths,
    pair_docs,
):
    section_index = lax.axis_index("section")
    dp_index = lax.axis_index("dp")
    count = lax.axis_size("dp")
    dims = grid_of(count)
    at = coordinates(dims, dp_index)
    is_first = section_index == 0
    first = is_first.astype(jnp.int32)
    width, hidden = tokens.shape[1], up_weight.shape[2]
    own_height = width // count
    by_hand = own_height % 16 == 0

    segments, positions = [
        jnp.stack(value)
        for value in zip(*(doc_layout(doc_lengths[micro_step]) for micro_step in range(MICRO)))
    ]
    layout = (*rotary(positions), segments[:, :, None], segments[:, None, :])
    picks = [jnp.stack([first, jnp.int32(micro_step)]) for micro_step in range(MICRO)]
    own_rows = [tokens[micro_step * ROWS : (micro_step + 1) * ROWS] for micro_step in range(MICRO)]
    ends = jnp.cumsum(doc_lengths, axis=1)
    pair_rows = pair_docs.reshape(count, MICRO, QRY_DEV, CANDS)
    losses_of = [
        Loss(
            micro_step,
            ends,
            pair_rows[:, micro_step].reshape(count * QRY_DEV, CANDS),
            dp_index,
            count,
        )
        for micro_step in range(MICRO)
    ]

    vectors = (
        qkv_bias,
        out_bias,
        norm1_gain,
        norm1_bias,
        up_bias,
        down_bias,
        norm2_gain,
        norm2_bias,
    )
    lengths = [value.shape[1] for value in vectors]
    short = sum(lengths)
    shards_of = [out_weight[0], qkv_weight[0], up_weight[0], down_weight[0]]

    fetched = (width, width, hidden // 4, width // 2)

    def small_parameters(layer, rows, projection):
        cuts, start = [], 0
        for length in lengths:
            cuts.append(rows[:, start : start + length].astype(WIDE).reshape(-1))
            start += length
        qkv_b, out_b, gain_one, bias_one, up_b, down_b, gain_two, bias_two = cuts
        layer.qkv_bias = qkv_b.reshape(3, width)
        layer.up_bias = up_b[None]
        layer.small = jnp.concatenate(
            [
                jnp.stack([out_b, gain_one, bias_one, down_b, gain_two, bias_two]),
                jnp.zeros((2, width), WIDE),
            ]
        )
        return projection.reshape(width, -1)

    if by_hand:
        line = jnp.concatenate([*vectors, jnp.zeros((1, width - short), LOW)], axis=1)
        proj_lines = proj_weight.reshape(-1, width)
        filler = jnp.zeros((15 - proj_lines.shape[0], width), LOW)
        chunks = [jnp.concatenate([shards_of[0], line, proj_lines, filler])]
        cuts_of = ([1], [1, 2], [2, 2], [2, 2])
        for number in (1, 2, 3):
            parts, shard = cuts_of[number], shards_of[number]
            unit, start = shard.shape[1] // sum(parts), 0
            for part in parts:
                chunks.append(lax.slice_in_dim(shard, start, start + part * unit, axis=1))
                start += part * unit
        gather = Gather(chunks, dims, at)
        layer = Layer(gather.owners, layout)

        def whole(number, first_chunk):
            parts, start = [], 0
            unit = shards_of[number].shape[1] // sum(cuts_of[number])
            for offset, part in enumerate(cuts_of[number]):
                parts.append((start, part * unit, gather.until(first_chunk + offset)))
                start += part * unit
            return Weight(gather.owners, shards_of[number].shape[0], start, fetched[number], parts)

        layer.out = whole(0, 0)
        block = placed_rows(layer.out.arrays, gather.owners, own_height, 16)
        projection = small_parameters(
            layer, block[:, 0], block[:, 1 : 1 + proj_lines.shape[0]]
        )
        layer.qkv = whole(1, 1)
        states = [layer.attend(rows, pick) for rows, pick in zip(own_rows, picks)]
        gather.advance()
        gather.advance(states[0]["norm"])
        layer.up = whole(2, 3)
        for state, pick in zip(states, picks):
            state |= layer.rise(state["norm"], pick)
        gather.advance(states[1]["norm"])
        gather.advance(*(state["active"] for state in states))
        layer.down = whole(3, 5)
    else:
        layer = Layer(jnp.zeros((1,), jnp.int32), layout)
        wholes = [
            lax.all_gather(value, "dp", axis=0, tiled=True)[None] for value in shards_of
        ]
        layer.out, layer.qkv, layer.up, layer.down = [
            Weight(layer.places, *value.shape[1:], columns, [(0, value.shape[2], [value])])
            for value, columns in zip(wholes, fetched)
        ]
        together = spread(jnp.concatenate([*vectors, proj_weight.reshape(1, -1)], axis=1)[0], count)
        projection = small_parameters(layer, together[:, :short], together[:, short:])
        states = [layer.attend(rows, pick) for rows, pick in zip(own_rows, picks)]
        for state, pick in zip(states, picks):
            state |= layer.rise(state["norm"], pick)

    arrived = []
    for state, pick in zip(states, picks):
        active = after(state["active"], *(one["result"] for one in states if "result" in one))
        state |= layer.fall(active, state["norm"], pick)
        arrived.append(from_behind(state["result"], "section", 1))
    own_scores = []
    for micro_step in range(MICRO):
        last = micro_step == MICRO - 1
        states.append(
            layer.forward(
                arrived[micro_step],
                picks[micro_step],
                projection,
                [state["result"] for state in states] if last else (),
            )
        )
        own_scores.append(losses_of[micro_step].scores(states[-1]["embedded"]))
    activations = states[-1]["activations"][None]

    tables = spread(jnp.stack(own_scores), count)
    own_losses, loss_grads = [None] * MICRO, [None] * MICRO
    earlier = []
    for micro_step in reversed(range(MICRO)):
        own_losses[micro_step], grad_queries, grad_docs = losses_of[micro_step].grads(
            tables[:, micro_step], *earlier
        )
        earlier = [grad_queries]
        loss_grads[micro_step] = (
            grad_docs,
            lax.all_to_all(grad_queries, "dp", 0, 0, tiled=True),
            projection,
        )
    own_losses = jnp.concatenate(own_losses)

    back, back_grads = [], []
    for micro_step in reversed(range(MICRO)):
        back.append(
            layer.backward(states[MICRO + micro_step], loss_grads[micro_step], None, picks[micro_step])
        )
        back_grads.append(from_behind(back[-1]["grad_low"], "section", -1))
    def exchanged(earlier):
        proj_total = product_tn(
            jnp.concatenate([state["result"] for state in states[:1:-1]]),
            after(jnp.concatenate([grads["grad_embedded"] for grads in back[:MICRO]]), *earlier),
        ) * section_index.astype(WIDE)
        proj_parts = proj_total.reshape(2, count, -1, proj_total.shape[1])
        proj_own = summed(jnp.swapaxes(proj_parts, 0, 1))
        proj_other, loss_other = [
            from_behind(value, "section", -1) for value in (proj_own[0], after(own_losses, *earlier))
        ]
        return (
            jnp.where(is_first, proj_other, proj_own[1]),
            jnp.where(is_first, loss_other, own_losses),
        )

    back.append(layer.backward(states[1], None, back_grads[0], picks[1]))
    back_grad = after(back_grads[1], back[-1]["mixed"])
    grads = layer.feed_back(states[0], back_grad, picks[0])

    def pairs(values):
        return [values[1], values[3]], [values[0], values[2]]

    lefts = [
        pairs([state[name] for state in states]) for name in ("active", "norm", "mixture")
    ] + [pairs([*own_rows, *arrived])]

    def rights_of(name):
        return pairs([grads[name], *(back[number][name] for number in (2, 1, 0))])

    def scatter(name, number, right):
        return Scatter(name, lefts[number], rights_of(right), dims, at, first)

    attended = grads["attended"]
    if by_hand:
        of_down, of_up = scatter("down", 0, "branch"), scatter("up", 1, "gate")
        of_down.send()
        of_up.send()
        down_first = of_down.keep(0, width // 2)
        attended = after(attended, *down_first)
    grads |= layer.attend_back(
        states[0], attended, grads["grad_one"], [one["grad_source"] for one in back], picks[0]
    )
    grad_inputs = grads["grad_source"]
    grad_vectors = [
        (
            one["qkv_vectors"][:3].reshape(-1),
            *(one["vectors"][number] for number in range(3)),
            one["grad_up_bias"][0],
            *(one["vectors"][number] for number in range(3, 6)),
        )
        for one in (*back, grads)
    ]
    totals = [sum(values) for values in zip(*grad_vectors)]
    packed = jnp.concatenate([value.reshape(count, -1) for value in totals], axis=1)
    if by_hand:
        of_out, of_qkv = scatter("out", 2, "attended"), scatter("qkv", 3, "mixed")
        of_qkv.send()
        of_out.send(jnp.pad(packed, [(0, 0), (0, width - packed.shape[1])]))

        def maker(weight, start, columns, quick=False):
            return lambda arrived: weight.keep(start, columns, quick)

        shared = []

        def exchange(arrived):
            shared.extend(exchanged(arrived))
            return ()

        sums = travels(
            [
                lambda arrived: down_first,
                maker(of_down, width // 2, width // 2, True),
                maker(of_up, 0, hidden // 2, True),
                maker(of_up, hidden // 2, hidden // 2),
                maker(of_qkv, 0, 2 * width),
                maker(of_qkv, 2 * width, width),
                maker(of_out, 0, width),
            ],
            dims,
            at,
            own_height,
            {1: lambda _: [grads["mixed"]], 5: exchange, 7: lambda _: shared},
        )
        proj_grad, query_losses = shared
        grad_down, grad_up, grad_qkv = (
            jnp.concatenate(group, axis=1)[None] for group in (sums[0:2], sums[2:4], sums[4:6])
        )
        grad_out, own = sums[6][None, :own_height], sums[6][own_height] + sums[6][own_height + 1]
    else:
        weight_grads = []
        for number, name in enumerate(("branch", "gate", "attended", "mixed")):
            left = jnp.concatenate([jnp.where(is_first, *pair) for pair in lefts[number]])
            right = [jnp.where(is_first, *pair) for pair in rights_of(name)]
            if number == 3:
                right = [jnp.swapaxes(value, 0, 1).reshape(ROWS, -1) for value in right]
            weight_grads.append(
                scatter_rows_plain(left, jnp.concatenate(right), dims, dp_index)[None]
            )
        grad_down, grad_up, grad_out, grad_qkv = weight_grads
        own = summed(packed)
        proj_grad, query_losses = exchanged(())
    small_grads, start = [], 0
    for length in lengths:
        small_grads.append(own[None, start : start + length])
        start += length
    grad_qkv_b, grad_out_b, grad_gain1, grad_bias1, grad_up_b, grad_down_b, grad_gain2, grad_bias2 = (
        small_grads
    )
    return (
        query_losses,
        activations,
        grad_inputs[None],
        grad_qkv,
        grad_qkv_b,
        grad_out,
        grad_out_b,
        grad_gain1,
        grad_bias1,
        grad_up,
        grad_up_b,
        grad_down,
        grad_down_b,
        grad_gain2,
        grad_bias2,
        proj_grad,
    )


def solution(mesh):
    in_specs = (
        P("dp", None),
        P("section", "dp", None),
        P("section", "dp"),
        P("section", "dp", None),
        P("section", "dp"),
        P("section", "dp"),
        P("section", "dp"),
        P("section", "dp", None),
        P("section", "dp"),
        P("section", "dp", None),
        P("section", "dp"),
        P("section", "dp"),
        P("section", "dp"),
        P("dp", None),
        P("dp", None),
        P(),
    )
    out_specs = (
        P("dp"),
        P("section", "dp", None),
        P("section", "dp", None),
        P("section", "dp", None),
        P("section", "dp"),
        P("section", "dp", None),
        P("section", "dp"),
        P("section", "dp"),
        P("section", "dp"),
        P("section", "dp", None),
        P("section", "dp"),
        P("section", "dp", None),
        P("section", "dp"),
        P("section", "dp"),
        P("section", "dp"),
        P(("section", "dp"), None),
    )
    return jax.shard_map(shards, mesh=mesh, in_specs=in_specs, out_specs=out_specs, check_vma=False)
```

```python
from functools import partial
import math

import jax
import jax.numpy as jnp
from jax import lax
from jax.experimental import pallas as pl
from jax.experimental.pallas import tpu as pltpu
from jax.sharding import PartitionSpec as P

HEAD = 64
PROJ = 128
QLEN = 32
DOC_ROWS = 192
QRY_DEV = 2
DOCS_DEV = 3
MICRO = 2
CANDS = 8
ROWS = 256
PREFIXES = (PROJ // 2, 3 * PROJ // 4, PROJ)


norm_eps = 1e-05
unit_eps = 1e-06
sharpness = 20.0
score_scale = 0.125
masked_score = -1000000000.0


def from_behind(value, axis, steps):
    count = lax.axis_size(axis)
    first, last = (max(0, -steps), min(count, count - steps))
    return lax.ppermute(value, axis, [(source, source + steps) for source in range(first, last)])


def product(left_side, right_side):
    return jnp.dot(left_side, right_side, preferred_element_type=jnp.float32)


def product_tn(left_side, right_side):
    return lax.dot_general(
        left_side, right_side, (((0,), (0,)), ((), ())), preferred_element_type=jnp.float32
    )


def product_nt(left_side, right_side):
    return lax.dot_general(
        left_side, right_side, (((1,), (1,)), ((), ())), preferred_element_type=jnp.float32
    )


def doc_layout(doc_lens):
    row_ids = jnp.arange(ROWS, dtype=jnp.int32)
    ends_at = jnp.cumsum(doc_lens)
    starts_at = ends_at - doc_lens
    doc_of = jnp.sum((row_ids[:, None] >= ends_at[None, :]).astype(jnp.int32), axis=1)
    doc_index = jnp.arange(DOCS_DEV, dtype=jnp.int32)
    begins = jnp.sum(
        jnp.where(doc_of[:, None] == doc_index[None, :], starts_at[None, :], 0), axis=1
    )
    in_docs = row_ids < DOC_ROWS
    query_rows = jnp.maximum(row_ids - DOC_ROWS, 0)
    segment = jnp.where(in_docs, doc_of, DOCS_DEV + query_rows // QLEN)
    position = jnp.where(in_docs, row_ids - begins, query_rows % QLEN)
    return (segment, position)


def rotary(position):
    step_ids = jnp.arange(HEAD // 2, dtype=jnp.int32).astype(jnp.float32)
    frequency = jnp.exp(step_ids * (-2.0 * math.log(10000.0) / HEAD))
    angles = position.astype(jnp.float32)[..., None] * frequency
    cosine, sine = jnp.cos(angles), jnp.sin(angles)
    return (
        jnp.concatenate([cosine] * 4, axis=-1),
        jnp.concatenate([-sine, sine] * 2, axis=-1),
    )


def lane_ids():
    return lax.broadcasted_iota(jnp.int32, (1, 2 * HEAD), 1)


def turned(value, cosine, sine):
    in_first = lane_ids() % HEAD < HEAD // 2
    ahead = pltpu.roll(value, 2 * HEAD - HEAD // 2, 1)
    behind = pltpu.roll(value, HEAD // 2, 1)
    return value * cosine + jnp.where(in_first, ahead, behind) * sine


def statistics(values):
    center = values - jnp.mean(values, axis=1, keepdims=True)
    spread = jnp.mean(center * center, axis=1, keepdims=True)
    scale = lax.rsqrt(spread + norm_eps)
    return center * scale, scale


def norm_back(grad, unit, scale, gain):
    inner = grad * gain
    along = jnp.mean(inner * unit, axis=1, keepdims=True)
    grad_in = scale * (inner - jnp.mean(inner, axis=1, keepdims=True) - unit * along)
    return grad_in, jnp.sum(grad * unit, axis=0, keepdims=True), jnp.sum(grad, axis=0, keepdims=True)


def gelu_parts(value):
    bell = jnp.exp(-0.5 * value * value)
    part = 1.0 / (1.0 + (0.3275911 * math.sqrt(0.5)) * jnp.abs(value))
    tail = 0.5 * 1.061405429 * part - 0.5 * 1.453152027
    tail = tail * part + 0.5 * 1.421413741
    tail = tail * part - 0.5 * 0.284496736
    tail = tail * part + 0.5 * 0.254829592
    tail = tail * part * bell
    below = jnp.where(value >= 0, 1.0 - tail, tail)
    return value * below, below + value * bell * (1.0 / math.sqrt(2.0 * math.pi))


def probabilities(queries, keys, allowed, held):
    scores = product_nt(jnp.where(held, queries, jnp.zeros_like(queries)), keys)
    scores = jnp.where(allowed, scores, masked_score)
    scores = jnp.exp(scores - jnp.max(scores, axis=1, keepdims=True))
    return scores * (1.0 / jnp.sum(scores, axis=1, keepdims=True))


LOW, WIDE = jnp.bfloat16, jnp.float32
VMEM_LIMIT = 46 << 20


def in_hbm(array):
    if array.size < 1 << 17:
        return array
    return pltpu.with_memory_space_constraint(array, pltpu.HBM)


BLOCK = 512
NO_COST = pl.CostEstimate(flops=1, bytes_accessed=1, transcendentals=0)
SOME_COST = pl.CostEstimate(flops=10**8, bytes_accessed=2 * 10**6, transcendentals=0)
FULL_COST = pl.CostEstimate(flops=40 * 10**9, bytes_accessed=10**8, transcendentals=0)


class Weight:
    def __init__(self, count, rows, columns, width, parts):
        self.count, self.rows, self.columns, self.width = count, rows, columns, width
        self.height = self.count * rows
        self.arrays = [group for _, _, groups in parts for group in groups]
        self.plan = [
            (start, width, [group.shape[0] for group in groups]) for start, width, groups in parts
        ]

    def scratch(self):
        return [
            pltpu.VMEM((self.height, self.columns), LOW),
            pltpu.SemaphoreType.DMA((self.columns // self.width, self.count)),
        ]


class Fetch:
    def __init__(self, weight, places_ref, refs, buffer, sems):
        self.weight, self.places_ref = weight, places_ref
        self.refs, self.buffer, self.sems = refs, buffer, sems
        self.waited = set()

    def copies(self, number):
        weight, begin = self.weight, number * self.weight.width
        passed = 0
        for start, width, lengths in weight.plan:
            if start <= begin < start + width:
                break
            passed += len(lengths)
        columns = pl.ds(begin - start, weight.width)
        block = 0
        for group, length in enumerate(lengths):
            for inner in range(length):
                place = pl.multiple_of(self.places_ref[block] * weight.rows, weight.rows)
                yield pltpu.make_async_copy(
                    self.refs[passed + group].at[inner, pl.ds(0, weight.rows), columns],
                    self.buffer.at[pl.ds(place, weight.rows), pl.ds(begin, weight.width)],
                    self.sems.at[number, block],
                )
                block += 1

    def start(self):
        for number in range(self.weight.columns // self.weight.width):
            for copy in self.copies(number):
                copy.start()

    def ready(self, until=None):
        until = self.weight.columns if until is None else until
        for number in range(-(-until // self.weight.width)):
            if number not in self.waited:
                self.waited.add(number)
                for copy in self.copies(number):
                    copy.wait()
        return self.buffer


class Parts:
    def __init__(self, refs, loads, weights, outs, scratch):
        self.pick, self.places, *refs = refs
        loaded, refs = refs[: len(loads)], refs[len(loads) :]
        fetched = {}
        for name, weight in weights.items():
            fetched[name], refs = refs[: len(weight.arrays)], refs[len(weight.arrays) :]
        stored, refs = refs[: len(outs)], refs[len(outs) :]
        self.buffers, refs = dict(zip(loads, refs)), refs[len(loads) :]
        self.weights = {}
        for name, weight in weights.items():
            buffer, sems, *refs = refs
            self.weights[name] = Fetch(weight, self.places, fetched[name], buffer, sems)
        self.outs, refs = dict(zip(outs, refs)), refs[len(outs) :]
        self.scratch, refs = dict(zip(scratch, refs)), refs[len(scratch) :]
        load_sems, out_sems = refs
        self.loads = {
            name: pltpu.make_async_copy(ref, self.buffers[name], load_sems.at[number])
            for number, (name, ref) in enumerate(zip(loads, loaded))
        }
        self.stores = {
            name: pltpu.make_async_copy(self.outs[name], ref, out_sems.at[number])
            for number, (name, ref) in enumerate(zip(outs, stored))
        }
        self.waited, self.begun = set(), set()

    def start(self, order):
        for name in order:
            (self.loads[name] if name in self.loads else self.weights[name]).start()

    def ref(self, name):
        if name in self.outs:
            return self.outs[name]
        if name in self.scratch:
            return self.scratch[name]
        if name not in self.waited:
            self.waited.add(name)
            self.loads[name].wait()
        return self.buffers[name]

    def refs(self, *names):
        return [self.ref(name) for name in names]

    def leave(self, *names):
        for name in names:
            self.stores[name].start()

    def finish(self):
        for name in self.stores:
            self.stores[name].wait()


def run_parts(name, bodies, pick, places, loads, weights, outs, scratch, order, cost):
    def kernel(*refs):
        parts = Parts(refs, list(loads), weights, list(outs), list(scratch))
        parts.start(order)
        for body in bodies:
            body(parts)
        if "vectors" in outs:
            parts.leave("vectors")
        parts.finish()

    arrays = [*loads.values(), *(array for weight in weights.values() for array in weight.arrays)]
    scratch_shapes = [pltpu.VMEM(array.shape, array.dtype) for array in loads.values()]
    scratch_shapes += [entry for weight in weights.values() for entry in weight.scratch()]
    scratch_shapes += [pltpu.VMEM(*out) for out in outs.values()] + list(scratch.values())
    results = pl.pallas_call(
        kernel,
        in_specs=[pl.BlockSpec(memory_space=pltpu.SMEM)] * 2
        + [pl.BlockSpec(memory_space=pl.ANY)] * len(arrays),
        out_specs=[pl.BlockSpec(memory_space=pltpu.HBM)] * len(outs),
        out_shape=[pltpu.HBM(*out) for out in outs.values()],
        scratch_shapes=scratch_shapes
        + [pltpu.SemaphoreType.DMA((len(loads),)), pltpu.SemaphoreType.DMA((len(outs),))],
        compiler_params=pltpu.CompilerParams(vmem_limit_bytes=VMEM_LIMIT),
        cost_estimate=cost,
        name=name,
    )(pick, places, *(in_hbm(array) for array in arrays))
    return dict(zip(outs, results))


def attend_part(parts):
    micro_step = parts.pick[1]
    source = parts.ref("x")
    cos_ref, sin_ref, column_ref, row_ref, bias_ref = parts.refs(
        "cosine", "sine", "column", "row", "qkv_bias"
    )
    cosine, sine = cos_ref[micro_step], sin_ref[micro_step]
    outs = parts.refs("q", "k", "v")
    width = source.shape[1]
    for part, ref in enumerate(outs):
        qkv = parts.weights["qkv"].ready((part + 1) * width)
        for start in range(0, width, BLOCK):
            at = slice(part * width + start, part * width + start + BLOCK)
            value = product(source[...], qkv[:, at])
            value = value + bias_ref[part : part + 1, start : start + BLOCK]
            for pair in range(0, BLOCK, 2 * HEAD):
                two = value[:, pair : pair + 2 * HEAD]
                if part < 2:
                    two = turned(two, cosine, sine)
                ref[:, start + pair : start + pair + 2 * HEAD] = two.astype(LOW)
    parts.leave("q", "k", "v")
    allowed = jnp.concatenate([column_ref[micro_step]] * 2, axis=1) == row_ref[micro_step]
    q_ref, k_ref, v_ref = outs
    mixture_ref, sum_ref, norm_ref, small_ref = parts.refs("mixture", "sum_one", "norm", "small")
    for start in range(0, width, 2 * HEAD):
        at = slice(start, start + 2 * HEAD)
        queries = q_ref[:, at] * LOW(score_scale)
        keys, values = k_ref[:, at], v_ref[:, at]
        mixed = []
        for head in range(2):
            held = lane_ids() // HEAD == head
            attention = probabilities(queries, keys, allowed, held)
            mixed.append(product(attention.astype(LOW), values))
        mixture_ref[:, at] = jnp.where(lane_ids() < HEAD, mixed[0], mixed[1]).astype(LOW)
    out = parts.weights["out"].ready()
    for start in range(0, width, BLOCK):
        at = slice(start, start + BLOCK)
        sum_ref[:, at] = (
            source[:, at].astype(WIDE)
            + small_ref[0:1, at]
            + product(mixture_ref[...], out[:, at])
        )
    unit, _ = statistics(sum_ref[...])
    norm_ref[...] = (unit * small_ref[1:2] + small_ref[2:3]).astype(LOW)
    parts.leave("mixture", "sum_one", "norm")


def up_part(parts):
    norm_ref, bias_ref, active_ref, slope_ref = parts.refs("norm", "up_bias", "active", "slope")
    for start in range(0, active_ref.shape[1], BLOCK):
        up = parts.weights["up"].ready(start + BLOCK)
        at = slice(start, start + BLOCK)
        active, slope = gelu_parts(product(norm_ref[...], up[:, at]) + bias_ref[:, at])
        active_ref[:, at] = active.astype(LOW)
        slope_ref[:, at] = slope.astype(LOW)
    parts.leave("active", "slope")


def down_part(parts):
    active_ref, norm_ref, small_ref = parts.refs("active", "norm", "small")
    sum_ref, result_ref = parts.refs("sum_two", "result")
    for start in range(0, sum_ref.shape[1], BLOCK):
        at = slice(start, start + BLOCK)
        down = parts.weights["down"].ready(start + BLOCK)
        sum_ref[:, at] = (
            norm_ref[:, at].astype(WIDE)
            + small_ref[3:4, at]
            + product(active_ref[...], down[:, at])
        )
    unit, _ = statistics(sum_ref[...])
    result = (unit * small_ref[4:5] + small_ref[5:6]).astype(LOW)
    result_ref[...] = result
    parts.leave("result", "sum_two")
    if "embedded" in parts.outs:
        parts.ref("embedded")[...] = product(result, parts.ref("projection")[...]).astype(LOW)
        parts.leave("embedded")
    if "activations" in parts.outs:
        early, late, own, both = parts.refs("early", "late", "own", "activations")

        @pl.when(parts.pick[0] == 1)
        def _():
            both[:ROWS] = early[...]
            both[ROWS:] = late[...]

        @pl.when(parts.pick[0] == 0)
        def _():
            both[:ROWS] = own[...]
            both[ROWS:] = result

        parts.leave("activations")


def vector_rows(parts):
    vector_ref = parts.ref("vectors")
    if "vectors" not in parts.begun:
        parts.begun.add("vectors")
        vector_ref[...] = jnp.zeros_like(vector_ref)
    return vector_ref


def norm_back_part(parts):
    if "docs" in parts.loads:
        own = jnp.sum(parts.ref("own_parts")[...].astype(WIDE), axis=0)
        embedded = jnp.concatenate([parts.ref("docs")[...], own], axis=0).astype(LOW)
        parts.ref("grad_embedded")[...] = embedded
        parts.leave("grad_embedded")
        upstream = product_nt(embedded, parts.ref("projection")[...])
        upstream = upstream * (1 - parts.pick[0]).astype(WIDE)
    else:
        upstream = parts.ref("back")[...].astype(WIDE)
    branch_ref, total, small_ref = parts.refs("branch", "total", "small")
    vector_ref = vector_rows(parts)
    unit, scale = statistics(parts.ref("sum_two")[...])
    grad, gain, bias = norm_back(upstream, unit, scale, small_ref[4:5])
    low = grad.astype(LOW)
    branch_ref[...] = low
    total[...] = grad
    vector_ref[10:11] = jnp.sum(low.astype(WIDE), axis=0, keepdims=True)
    vector_ref[11:12] = gain
    vector_ref[12:13] = bias
    parts.leave("branch")
    if "total" in parts.outs:
        parts.leave("total")


def feed_back_part(parts):
    branch_ref, gate_ref, attended_ref = parts.refs("branch", "gate", "attended")
    small_ref, slope_ref = parts.refs("small", "slope")
    vector_ref = vector_rows(parts)
    width = attended_ref.shape[1]
    down = parts.weights["down"].ready()
    for start in range(0, gate_ref.shape[1], BLOCK):
        at = slice(start, start + BLOCK)
        gate = product_nt(branch_ref[...], down[at]) * slope_ref[:, at].astype(WIDE)
        gate = gate.astype(LOW)
        gate_ref[:, at] = gate
        row, column = 6 + start // width, start % width
        vector_ref[row : row + 1, column : column + BLOCK] = jnp.sum(
            gate.astype(WIDE), axis=0, keepdims=True
        )
    parts.leave("gate")
    up = parts.weights["up"].ready()
    total = parts.ref("total")
    for start in range(0, total.shape[1], BLOCK):
        at = slice(start, start + BLOCK)
        total[:, at] += product_nt(gate_ref[...], up[at])
    unit, scale = statistics(parts.ref("sum_one")[...])
    grad, gain, bias = norm_back(total[...], unit, scale, small_ref[1:2])
    total[...] = grad
    low = grad.astype(LOW)
    attended_ref[...] = low
    vector_ref[3:4] = jnp.sum(low.astype(WIDE), axis=0, keepdims=True)
    vector_ref[4:5] = gain
    vector_ref[5:6] = bias
    parts.leave("attended")
    if "grad_one" in parts.outs:
        parts.ref("grad_one")[...] = grad
        parts.leave("grad_one")


def attend_back_part(parts):
    micro_step = parts.pick[1]
    attended_ref, mixed_ref, mixture, total = parts.refs("attended", "mixed", "mixture", "total")
    vector_ref = vector_rows(parts)
    cos_ref, sin_ref, column_ref, row_ref = parts.refs("cosine", "sine", "column", "row")
    cosine, sine = cos_ref[micro_step], sin_ref[micro_step]
    allowed = jnp.concatenate([column_ref[micro_step]] * 2, axis=1) == row_ref[micro_step]
    width = mixture.shape[1]
    if "grad_one" in parts.loads:
        total[...] = parts.ref("grad_one")[...]
    out = parts.weights["out"].ready()
    for start in range(0, width, BLOCK):
        at = slice(start, start + BLOCK)
        mixture[:, at] = product_nt(attended_ref[...], out[at]).astype(LOW)
    q_ref, k_ref, v_ref = parts.refs("q", "k", "v")
    for start in range(0, width, 2 * HEAD):
        at = slice(start, start + 2 * HEAD)
        queries, keys, values = q_ref[:, at], k_ref[:, at], v_ref[:, at]
        scaled = queries * LOW(score_scale)
        grad_mixture = mixture[:, at]
        grads = []
        for head in range(2):
            held = lane_ids() // HEAD == head
            attention = probabilities(scaled, keys, allowed, held)
            own = jnp.where(held, grad_mixture, jnp.zeros_like(grad_mixture))
            grad_attention = product_nt(own, values)
            grad_values = product_tn(attention.astype(LOW), own)
            along = jnp.sum(grad_attention * attention, axis=1, keepdims=True)
            grad_scores = (attention * (grad_attention - along)).astype(LOW)
            grads.append((product(grad_scores, keys), product_tn(grad_scores, queries), grad_values))
        first_head = lane_ids() < HEAD
        for part in range(2):
            value = jnp.where(first_head, grads[0][part], grads[1][part]) * score_scale
            mixed_ref[part, :, at] = turned(value, cosine, -sine).astype(LOW)
        mixed_ref[2, :, at] = (grads[0][2] + grads[1][2]).astype(LOW)
    parts.leave("mixed")
    for part in range(3):
        vector_ref[part : part + 1] = jnp.sum(
            mixed_ref[part].astype(WIDE), axis=0, keepdims=True
        )
    qkv = parts.weights["qkv"].ready()
    for start in range(0, width, BLOCK):
        at = slice(start, start + BLOCK)
        value = total[:, at]
        for part in range(3):
            value = value + product_nt(mixed_ref[part], qkv[at, part * width : (part + 1) * width])
        total[:, at] = value
    if "grad_low" in parts.outs:
        parts.ref("grad_low")[...] = total[...].astype(LOW)
        parts.leave("grad_low")
        parts.ref("grad_source")[...] = total[...]
    else:
        late, early, own, source_ref = parts.refs("late", "early", "own", "grad_source")

        @pl.when(parts.pick[0] == 1)
        def _():
            source_ref[:ROWS] = total[...]
            source_ref[ROWS:] = own[...]

        @pl.when(parts.pick[0] == 0)
        def _():
            source_ref[:ROWS] = early[...]
            source_ref[ROWS:] = late[...]

    parts.leave("grad_source")


class Layer:
    def __init__(self, places, layout):
        self.places = places
        self.layout = dict(zip(("cosine", "sine", "column", "row"), layout))

    def attend_set(self, source):
        rows = source.shape
        return (
            {"x": source, **self.layout, "qkv_bias": self.qkv_bias, "small": self.small},
            {"qkv": self.qkv, "out": self.out},
            {
                "q": (rows, LOW),
                "k": (rows, LOW),
                "v": (rows, LOW),
                "mixture": (rows, LOW),
                "sum_one": (rows, WIDE),
                "norm": (rows, LOW),
            },
            {},
        )

    def up_set(self):
        rows = (ROWS, self.up.columns)
        return (
            {"up_bias": self.up_bias},
            {"up": self.up},
            {"active": (rows, LOW), "slope": (rows, LOW)},
            {},
        )

    def down_set(self, projection, earlier):
        rows = (ROWS, self.down.columns)
        loads = {"small": self.small}
        outs = {"sum_two": (rows, WIDE), "result": (rows, LOW)}
        if projection is not None:
            loads["projection"] = projection
            outs["embedded"] = ((ROWS, PROJ), LOW)
        if earlier:
            loads |= dict(zip(("early", "late", "own"), earlier))
            outs["activations"] = ((MICRO * ROWS, self.down.columns), LOW)
        return loads, {"down": self.down}, outs, {}

    def run(self, name, bodies, sets, pick, more=None, cost=NO_COST):
        loads, weights, outs, scratch = dict(more or {}), {}, {}, {}
        order = list(loads)
        for one in sets:
            order += [key for key in (*one[0], *one[1]) if key not in order]
            loads, weights = loads | one[0], weights | one[1]
            outs, scratch = outs | one[2], scratch | one[3]
        return run_parts(
            name, bodies, pick, self.places, loads, weights, outs, scratch, order, cost
        )

    def attend(self, source, pick):
        return self.run("attend", [attend_part], [self.attend_set(source)], pick)

    def rise(self, norm, pick):
        return self.run("up", [up_part], [self.up_set()], pick, {"norm": norm})

    def fall(self, active, norm, pick):
        return self.run(
            "down", [down_part], [self.down_set(None, ())], pick, {"active": active, "norm": norm}
        )

    def forward(self, source, pick, projection, earlier):
        return self.run(
            "forward",
            [attend_part, up_part, down_part],
            [self.attend_set(source), self.up_set(), self.down_set(projection, earlier)],
            pick,
            cost=FULL_COST,
        )

    def norm_back_set(self, state, loss_grads, back_grad):
        rows = (ROWS, self.down.columns)
        outs = {"branch": (rows, LOW), "vectors": ((16, rows[1]), WIDE)}
        if loss_grads is not None:
            loads = dict(zip(("docs", "own_parts", "projection"), loss_grads))
            outs["grad_embedded"] = ((ROWS, PROJ), LOW)
        else:
            loads = {"back": back_grad}
        loads |= {"sum_two": state["sum_two"], "small": self.small}
        return loads, {}, outs, {"total": pltpu.VMEM(rows, WIDE)}

    def feed_back_set(self, state):
        rows, hidden = (ROWS, self.down.columns), self.up.columns
        return (
            {"slope": state["slope"], "small": self.small},
            {"down": self.down, "up": self.up},
            {
                "gate": ((ROWS, hidden), LOW),
                "attended": (rows, LOW),
                "vectors": ((16, rows[1]), WIDE),
            },
            {"total": pltpu.VMEM(rows, WIDE)},
        )

    def attend_back_set(self, state, earlier):
        rows = (ROWS, self.out.columns)
        outs = {"mixed": ((3, *rows), LOW), "vectors": ((16, rows[1]), WIDE)}
        loads = {"q": state["q"], "k": state["k"], "v": state["v"], **self.layout}
        if earlier:
            loads |= dict(zip(("late", "early", "own"), earlier))
            outs["grad_source"] = ((MICRO * ROWS, rows[1]), WIDE)
        else:
            outs |= {"grad_source": (rows, WIDE), "grad_low": (rows, LOW)}
        return (
            loads,
            {"out": self.out, "qkv": self.qkv},
            outs,
            {"mixture": pltpu.VMEM(rows, LOW), "total": pltpu.VMEM(rows, WIDE)},
        )

    def backward(self, state, loss_grads, back_grad, pick):
        return self.run(
            "backward",
            [norm_back_part, feed_back_part, attend_back_part],
            [
                self.norm_back_set(state, loss_grads, back_grad),
                self.feed_back_set(state),
                ({"sum_one": state["sum_one"]}, {}, {}, {}),
                self.attend_back_set(state, ()),
            ],
            pick,
            cost=FULL_COST,
        )

    def norm_back(self, state, back_grad, pick):
        loads, weights, outs, scratch = self.norm_back_set(state, None, back_grad)
        outs |= {"total": (state["sum_two"].shape, WIDE)}
        return self.run("norm_back", [norm_back_part], [(loads, weights, outs, {})], pick)

    def feed_back(self, state, branch, total, pick):
        loads, weights, outs, scratch = self.feed_back_set(state)
        outs |= {"grad_one": (total.shape, WIDE)}
        loads = {"branch": branch} | loads
        return self.run(
            "feed_back",
            [feed_back_part],
            [(loads, weights, outs, {}), ({"total": total, "sum_one": state["sum_one"]}, {}, {}, {})],
            pick,
            cost=FULL_COST,
        )

    def attend_back(self, state, attended, grad_one, earlier, pick):
        return self.run(
            "attend_back",
            [attend_back_part],
            [self.attend_back_set(state, earlier)],
            pick,
            {"attended": attended, "grad_one": grad_one},
            cost=FULL_COST,
        )


def grid_of(count):
    dims = []
    while count % 2 == 0:
        dims.append(2)
        count //= 2
    return ([count] if count > 1 else []) + dims


def coordinates(dims, number):
    at = []
    for size in reversed(dims):
        at.append(number % size)
        number = number // size
    return at[::-1]


def shifted(value, dims, dim, steps):
    count = math.prod(dims)
    stride = math.prod(dims[dim + 1 :])
    pairs = []
    for source in range(count):
        place = (source // stride) % dims[dim]
        pairs.append((source, source + ((place + steps) % dims[dim] - place) * stride))
    return lax.ppermute(value, "dp", pairs)


def after(value, *earlier):
    return lax.optimization_barrier((value, *earlier))[0]


def stage(sends, earlier, beside=None):
    values = [after(value, *earlier) for value, _ in sends]
    backwards = list(zip(values, sends))[::-1]
    arrived = [permuted(value) for value, (_, permuted) in backwards][::-1]
    made = beside(earlier, arrived) if beside else []
    return list(lax.optimization_barrier((*arrived, *made)))[: len(sends)]


def step_along(dims, dim, steps):
    return lambda value: shifted(value, dims, dim, steps)


def rows_kernel(top, places, *refs):
    pieces, out, sems = refs[:-2], refs[-2], refs[-1]
    copies = []
    for group in pieces:
        for inner in range(group.shape[0]):
            number = len(copies)
            copies.append(
                pltpu.make_async_copy(
                    group.at[inner, pl.ds(top, out.shape[1])],
                    out.at[places[number]],
                    sems.at[number],
                )
            )
    for copy in copies:
        copy.start()
    for copy in copies:
        copy.wait()


def placed_rows(groups, places, top, rows):
    count, columns = places.shape[0], groups[0].shape[2]
    return pl.pallas_call(
        partial(rows_kernel, top),
        out_shape=jax.ShapeDtypeStruct((count, rows, columns), groups[0].dtype),
        in_specs=[pl.BlockSpec(memory_space=pltpu.SMEM)]
        + [pl.BlockSpec(memory_space=pl.ANY)] * len(groups),
        out_specs=pl.BlockSpec(memory_space=pltpu.VMEM),
        scratch_shapes=[pltpu.SemaphoreType.DMA((count,))],
        name="place",
    )(places, *groups)


def block_owners(order, dims, at):
    owners = jnp.zeros((1,), jnp.int32)
    for dim in order:
        steps = jnp.arange(dims[dim], dtype=jnp.int32)
        own = ((at[dim] - steps) % dims[dim]) * math.prod(dims[dim + 1 :])
        owners = (own[:, None] + owners[None, :]).reshape(-1)
    return owners


class Gather:
    def __init__(self, chunks, dims):
        self.dims, self.chunks = dims, chunks
        self.held = [[value[None]] for value, _, _ in chunks]
        self.arrived, self.step = [], 0

    def groups(self, number):
        _, order, start = self.chunks[number]
        while self.step < start + len(order):
            self.advance()
        return self.held[number]

    def advance(self, *needed):
        sends, takers = [], []
        for number, (value, order, start) in enumerate(self.chunks):
            if start <= self.step < start + len(order):
                dim = order[self.step - start]
                for steps in range(1, self.dims[dim]):
                    for group in self.held[number]:
                        sends.append((group, step_along(self.dims, dim, steps)))
                        takers.append(number)
        self.arrived = stage(sends, [*self.arrived, *needed])
        for number in sorted(set(takers)):
            value, order, start = self.chunks[number]
            got = [one for one, taker in zip(self.arrived, takers) if taker == number]
            held = self.held[number] + got
            blocks = sum(group.shape[0] for group in held)
            last = self.step - start >= len(order) - 2
            if not last or (blocks * value.size < 1 << 20 and self.step - start < len(order) - 1):
                held = [jnp.concatenate(held)]
            self.held[number] = held
        self.step += 1


def scatter_rows_plain(left, right, dims, dp_index):
    count = math.prod(dims)
    at = [
        (dp_index // math.prod(dims[dim + 1 :])) % dims[dim] for dim in range(len(dims))
    ]
    samples, height = left.shape
    rows, columns = height // count, right.shape[1]
    split = left.reshape(samples, count // 2, 2, rows)
    for_other = lax.dynamic_index_in_dim(split, 1 - at[-1], 2, False).reshape(samples, -1)
    for_self = lax.dynamic_index_in_dim(split, at[-1], 2, False).reshape(samples, -1)
    sent = product_tn(for_other, right).astype(jnp.bfloat16)
    total = product_tn(for_self, right) + shifted(sent, dims, len(dims) - 1, 1).astype(jnp.float32)
    for dim in reversed(range(len(dims) - 1)):
        low = total.astype(jnp.bfloat16).reshape(-1, dims[dim], rows, columns)
        total = lax.dynamic_index_in_dim(low, at[dim], 1, False).astype(jnp.float32)
        for steps in range(1, dims[dim]):
            part = lax.dynamic_index_in_dim(low, (at[dim] + steps) % dims[dim], 1, False)
            total = total + shifted(part, dims, dim, steps).astype(jnp.float32)
    return total.reshape(rows, columns)


def fetch_chosen(pick_ref, pair, place, target, sem):
    for wanted, ref in ((1, pair[0]), (0, pair[1])):

        @pl.when(pick_ref[0] == wanted)
        def _(ref=ref):
            pltpu.make_async_copy(ref.at[place], target, sem).start()

    return pltpu.make_async_copy(pair[0].at[place], target, sem)


def grad_kernel(pick_ref, *refs, rows, slots, outer, stride, start, other_start, sends):
    lefts, rights, refs = (refs[0:2], refs[2:4]), (refs[4:6], refs[6:8]), refs[8:]
    if not sends:
        other_ref, *refs = refs
    out_refs, refs = refs[: 1 if sends else slots], refs[1 if sends else slots :]
    if sends:
        left, right, out, left_sems, right_sems, out_sems = refs
    else:
        left, right, other, out, left_sems, right_sems, other_sems, out_sems = refs
    chips, width = outer * slots, right.shape[1]
    samples = lefts[0][0].shape[0]
    side = 1 - pick_ref[1] if sends else pick_ref[1]
    thin = rows % 128 != 0
    block = min(2 * BLOCK, width) if thin else width
    blocks = width // block
    wide_part = rights[0][0].shape[-1]

    def left_copies(number):
        if thin:
            place, target = (slice(None), slice(None)), slice(None)
        else:
            chip = number if sends else chip_of(number)
            place = (slice(None), pl.ds(pl.multiple_of((2 * chip + side) * rows, rows), rows))
            target = slice(number * rows, (number + 1) * rows)
        return [
            fetch_chosen(
                pick_ref,
                lefts[half],
                place,
                left.at[half * samples : (half + 1) * samples, target],
                left_sems.at[number, half],
            )
            for half in range(2)
        ]

    def right_copies(number):
        begin = start + number * block
        columns = pl.ds(begin % wide_part, block)
        place = (slice(None), columns)
        if len(rights[0][0].shape) == 3:
            place = (begin // wide_part, *place)
        at = slice(number * block, (number + 1) * block)
        return [
            fetch_chosen(
                pick_ref,
                rights[half],
                place,
                right.at[half * samples : (half + 1) * samples, at],
                right_sems.at[number, half],
            )
            for half in range(2)
        ]

    def chip_of(number):
        inner = number % outer
        first_chip = inner // stride * stride * slots + inner % stride
        return first_chip + stride * lax.rem(pick_ref[2] + number // outer, slots)

    def other_copy(number):
        if thin:
            return pltpu.make_async_copy(
                other_ref.at[pl.ds(0, chips * rows), pl.ds(other_start + number * block, block)],
                other.at[:, number * block : (number + 1) * block],
                other_sems.at[number],
            )
        return pltpu.make_async_copy(
            other_ref.at[
                pl.ds(pl.multiple_of(chip_of(number) * rows, rows), rows), pl.ds(other_start, width)
            ],
            other.at[number * rows : (number + 1) * rows],
            other_sems.at[number],
        )

    def wait(copies):
        for copy in copies:
            copy.wait()

    leaving = []
    if thin:
        halves_of_left = left_copies(0)
        arriving = [right_copies(number) for number in range(blocks)]
        if not sends:
            others = [other_copy(number) for number in range(blocks)]
            for copy in others:
                copy.start()
        wait(halves_of_left)
        flipped = left[...].T
        turned = jnp.concatenate(
            [
                jnp.where(
                    side == 0,
                    flipped[2 * rows * chip : 2 * rows * chip + rows],
                    flipped[2 * rows * chip + rows : 2 * rows * (chip + 1)],
                )
                for chip in range(chips)
            ]
        )
        for number in range(blocks):
            at = slice(number * block, (number + 1) * block)
            wait(arriving[number])
            result = product(turned, right[:, at])
            if sends:
                out[:, at] = result.astype(LOW)
                leaving.append(
                    pltpu.make_async_copy(out.at[:, at], out_refs[0].at[:, at], out_sems.at[number])
                )
                leaving[-1].start()
                continue
            others[number].wait()
            out[:, at] = (result + other[:, at].astype(WIDE)).astype(LOW)
            for place in range(chips):
                leaving.append(
                    pltpu.make_async_copy(
                        out.at[pl.ds(pl.multiple_of(chip_of(place) * rows, rows), rows), at],
                        out_refs[place // outer].at[place % outer, :, at],
                        out_sems.at[number * chips + place],
                    )
                )
                leaving[-1].start()
    else:
        arriving = right_copies(0)
        pieces = [left_copies(number) for number in range(chips)]
        if not sends:
            others = [other_copy(number) for number in range(chips)]
            for copy in others:
                copy.start()
        wait(arriving)
        for number in range(chips):
            at = slice(number * rows, (number + 1) * rows)
            wait(pieces[number])
            result = product_tn(left[:, at], right[...])
            if sends:
                out[at] = result.astype(LOW)
                target = out_refs[0].at[at]
            else:
                others[number].wait()
                out[at] = (result + other[at].astype(WIDE)).astype(LOW)
                target = out_refs[number // outer].at[number % outer]
            leaving.append(pltpu.make_async_copy(out.at[at], target, out_sems.at[number]))
            leaving[-1].start()
    wait(leaving)


def fold_kernel(pick_ref, held_ref, other_ref, out_ref, *send_refs, slots, stride):
    for slot in range(slots):
        place = lax.rem(pick_ref[0] + slot, slots)
        for number in range(out_ref.shape[0]):
            index = number // stride * stride * slots + number % stride + place * stride
            value = held_ref[index].astype(WIDE) + other_ref[index].astype(WIDE)
            if slot == 0:
                out_ref[number] = value
                continue
            send_refs[slot - 1][number] = value.astype(LOW)


def slots_of(value, slots, stride):
    return value.reshape(-1, slots, stride, *value.shape[1:])


class Scatter:
    def __init__(self, name, lefts, rights, dims, at, dim, first):
        self.name, self.lefts, self.rights, self.dims, self.at = name, lefts, rights, dims, at
        self.count = math.prod(dims)
        self.height = lefts[0][0].shape[1]
        self.rows = self.height // self.count
        sample = rights[0][0]
        self.columns = sample.shape[-1] * (3 if sample.ndim == 3 else 1)
        self.slots, self.stride = dims[dim], math.prod(dims[dim + 1 : -1])
        self.place = at[dim]
        self.pick = jnp.stack([first, at[-1], self.place])

    def product(self, start, width, other, other_start, cost, earlier=()):
        samples = self.lefts[0][0].shape[0]
        half, rows, slots = self.height // 2, self.rows, self.slots
        chips = self.count // 2
        outer = chips // slots
        sends = other is None
        thin = rows % 128 != 0
        blocks = width // min(2 * BLOCK, width) if thin else 1
        pieces = 1 if thin else chips
        anywhere = pl.BlockSpec(memory_space=pl.ANY)
        args = [*self.lefts[0], *self.lefts[1], *self.rights[0], *self.rights[1]]
        args += [] if sends else [other]
        out_sems = blocks * (1 if sends else chips) if thin else chips
        other_scratch = [] if sends else [pltpu.VMEM((half, width), LOW)]
        other_sems = [] if sends else [pltpu.SemaphoreType.DMA((blocks if thin else chips,))]
        outs = [(half, width)] if sends else [(outer, rows, width)] * slots
        scratch = [
            pltpu.VMEM((2 * samples, self.height if thin else half), LOW),
            pltpu.VMEM((2 * samples, width), LOW),
            *other_scratch,
            pltpu.VMEM((half, width), LOW),
        ]
        return pl.pallas_call(
            partial(
                grad_kernel,
                rows=rows,
                slots=slots,
                outer=outer,
                stride=self.stride,
                start=start,
                other_start=other_start,
                sends=sends,
            ),
            in_specs=[pl.BlockSpec(memory_space=pltpu.SMEM)] + [anywhere] * len(args),
            out_specs=[anywhere] * len(outs),
            out_shape=[jax.ShapeDtypeStruct(out, LOW) for out in outs],
            scratch_shapes=[
                *scratch,
                pltpu.SemaphoreType.DMA((pieces, 2)),
                pltpu.SemaphoreType.DMA((blocks, 2)),
                *other_sems,
                pltpu.SemaphoreType.DMA((out_sems,)),
            ],
            compiler_params=pltpu.CompilerParams(vmem_limit_bytes=VMEM_LIMIT),
            cost_estimate=cost,
            name=self.name + ("_send" if sends else "_keep"),
        )(after(self.pick, *earlier), *(in_hbm(array) for array in args))

    def make(self, cost, earlier=(), start=0, width=None):
        self.sent = self.product(start, width or self.columns, None, 0, cost, earlier)[0]
        self.other_from = start
        return self.sent

    def keep(self, start, width, cost, earlier=()):
        return self.product(start, width, self.other, start - self.other_from, cost, earlier)


def own_kernel(where_ref, vectors_ref, *out_refs, spans):
    width = vectors_ref.shape[1]
    for (first_row, rows, length), out_ref in zip(spans, out_refs):
        start = where_ref[0] * length
        if rows > 1 and width % length == 0:
            line = vectors_ref[pl.ds(first_row + start // width, 1)]
        else:
            line = jnp.concatenate(
                [vectors_ref[first_row + row : first_row + row + 1] for row in range(rows)], axis=1
            )
        turns = lax.rem(line.shape[1] - lax.rem(start, line.shape[1]), line.shape[1])
        line = pltpu.roll(jnp.broadcast_to(line, (8, line.shape[1])), turns, 1)
        out_ref[...] = line[0:1, :length]


def own_parts(vectors, spans, dp_index):
    return pl.pallas_call(
        partial(own_kernel, spans=spans),
        in_specs=[
            pl.BlockSpec(memory_space=pltpu.SMEM),
            pl.BlockSpec(memory_space=pltpu.VMEM),
        ],
        out_specs=[pl.BlockSpec(memory_space=pltpu.VMEM)] * len(spans),
        out_shape=[jax.ShapeDtypeStruct((1, length), WIDE) for _, _, length in spans],
        name="own_parts",
    )(dp_index[None], vectors)


class Whole:
    def __init__(self, value):
        self.value = value

    def outgoing(self, dim):
        return self.value

    def take(self, arrived):
        self.value = self.value + arrived


class Halved:
    def __init__(self, value, dims, at):
        self.value, self.dims, self.at = value, dims, at

    def outgoing(self, dim):
        split = self.value.reshape(-1, self.dims[dim], *self.value.shape[1:])
        self.kept = lax.dynamic_index_in_dim(split, self.at[dim], 1, False)
        return lax.dynamic_index_in_dim(split, 1 - self.at[dim], 1, False)

    def take(self, arrived):
        self.value = self.kept + arrived


def folded(held, moved, slots, stride, place):
    outer, rows, columns = held.shape
    if rows % 16 == 0 and len(moved) == 1:
        whole = pl.BlockSpec(memory_space=pltpu.VMEM)
        shape = (outer // slots, rows, columns)
        total, *sends = pl.pallas_call(
            partial(fold_kernel, slots=slots, stride=stride),
            out_shape=[jax.ShapeDtypeStruct(shape, WIDE)]
            + [jax.ShapeDtypeStruct(shape, LOW)] * (slots - 1),
            in_specs=[pl.BlockSpec(memory_space=pltpu.SMEM), whole, whole],
            out_specs=[whole] * slots,
            compiler_params=pltpu.CompilerParams(vmem_limit_bytes=24 << 20),
            cost_estimate=NO_COST,
            name="fold",
        )(place[None], held, moved[0])
        return total, sends
    total = held.astype(WIDE)
    for piece in moved:
        total = total + piece.astype(WIDE)
    split = slots_of(total, slots, stride)
    blocks = [
        lax.dynamic_index_in_dim(split, (place + steps) % slots, 1, False).reshape(-1, rows, columns)
        for steps in range(slots)
    ]
    return blocks[0], [block.astype(LOW) for block in blocks[1:]]


def travels(pieces, chunks, order, dims, at, cores, riders, during):
    held, sends, sums = {}, {}, {}
    arrived, riding = [], []
    ways = list(reversed(range(len(dims))))
    for step in range(chunks + len(order) - 1):
        if step < chunks:
            held[step], *sends[step] = pieces[step]
        if step in riders:
            riding += [(rider, step) for rider in riders[step]()]
        outgoing, takers = [], []
        for phase, dim in enumerate(order):
            number = step - phase
            if 0 <= number < chunks:
                outgoing += [
                    (value, step_along(dims, dim, k)) for k, value in enumerate(sends[number], start=1)
                ]
                takers += [number] * len(sends[number])
        exchanging = cores.get(step, lambda: [])()
        outgoing += [(weight.sent, step_along(dims, ways[0], 1)) for weight in exchanging]
        along = [(rider, ways[step - start]) for rider, start in riding if step - start < len(ways)]
        outgoing += [(rider.outgoing(dim), step_along(dims, dim, 1)) for rider, dim in along]

        def beside(earlier, arriving):
            for weight, half in zip(exchanging, arriving[len(takers) :]):
                weight.other = half
            return during[step](earlier) if step < len(during) else []

        arrived = stage(outgoing, arrived, beside)
        for (rider, _), part in zip(along, arrived[len(takers) + len(exchanging) :]):
            rider.take(part)
        arrived = arrived[: len(takers)]
        for phase, dim in enumerate(order):
            number = step - phase
            if not 0 <= number < chunks:
                continue
            moved = [value for value, taker in zip(arrived, takers) if taker == number]
            left = order[phase + 1 :]
            if left:
                stride = math.prod(dims[other] for other in left if other > left[0])
                held[number], sends[number] = folded(
                    held[number], moved, dims[left[0]], stride, at[left[0]]
                )
            else:
                total = held[number].astype(WIDE)
                for piece in moved:
                    total = total + piece.astype(WIDE)
                sums[number] = total.reshape(total.shape[-2:])
    return [sums[number] for number in range(chunks)]


def spread(value, count):
    return lax.all_to_all(
        jnp.broadcast_to(value[None], (count, *value.shape)), "dp", 0, 0, tiled=True
    )


def summed(parts):
    return jnp.sum(lax.all_to_all(parts, "dp", 0, 0, tiled=True).astype(jnp.float32), axis=0)


def halves(value):
    high = value.astype(jnp.bfloat16)
    return high, (value - high.astype(jnp.float32)).astype(jnp.bfloat16)


def exact_product(left_side, right_side):
    high, low = halves(right_side)
    return product(left_side, high) + product(left_side, low)


def product_by_ones(left_side, right_side):
    high, low = halves(left_side)
    return product(high, right_side) + product(low, right_side)


def prefix_masks(length):
    places = lax.broadcasted_iota(jnp.int32, (1, length), 1)
    return [places < width for width in PREFIXES]


def similar_parts(documents, queries_t):
    docs_f32 = documents.astype(jnp.float32)
    squares = docs_f32 * docs_f32
    query_squares = queries_t * queries_t
    queries_low = queries_t.astype(jnp.bfloat16)
    parts = []
    for width, mask in zip(PREFIXES, prefix_masks(PROJ)):
        cut = jnp.where(mask, docs_f32, 0.0)
        doc_scale = lax.rsqrt(
            jnp.sum(jnp.where(mask, squares, 0.0), axis=1, keepdims=True) + unit_eps
        )
        query_scale = lax.rsqrt(
            jnp.sum(query_squares[:width], axis=0, keepdims=True) + unit_eps
        )
        cut = cut.astype(jnp.bfloat16)
        similar = product(cut, queries_low) * doc_scale * query_scale
        parts.append((cut, doc_scale, query_scale, similar))
    return parts


def members_of(ends_ref, micro_step, by_row):
    shape = (DOC_ROWS, 8) if by_row else (8, DOC_ROWS)
    rows = lax.broadcasted_iota(jnp.int32, shape, 0 if by_row else 1)
    docs = lax.broadcasted_iota(jnp.int32, shape, 1 if by_row else 0)
    inside = jnp.zeros(shape, jnp.float32)
    for number in range(DOCS_DEV):
        begin = ends_ref[micro_step, number - 1] if number else 0
        held = (docs == number) & (rows >= begin) & (rows < ends_ref[micro_step, number])
        inside = jnp.where(held, 1.0, inside)
    return inside.astype(jnp.bfloat16)


def query_of_token(tokens, by_token):
    shape = (tokens, 128) if by_token else (128, tokens)
    token = lax.broadcasted_iota(jnp.int32, shape, 0 if by_token else 1)
    query = lax.broadcasted_iota(jnp.int32, shape, 1 if by_token else 0)
    held = (token >= query * QLEN) & (token < query * QLEN + QLEN)
    return jnp.where(held, 1.0, 0.0).astype(jnp.bfloat16)


def score_kernel(ends_ref, queries_ref, docs_ref, out_ref, *, micro_step):
    tokens = queries_ref.shape[0] * queries_ref.shape[1]
    queries_t = queries_ref[...].astype(WIDE).reshape(tokens, PROJ).T
    members = members_of(ends_ref, micro_step, False)
    by_query = query_of_token(tokens, True)
    for number, (_, _, _, similar) in enumerate(similar_parts(docs_ref[:DOC_ROWS], queries_t)):
        masses = exact_product(members, jnp.exp(sharpness * similar))
        held = lax.broadcasted_iota(jnp.int32, masses.shape, 0) < DOCS_DEV
        logs = jnp.log(jnp.where(held, masses, 1.0))
        out_ref[0, number] = product_by_ones(logs, by_query) / sharpness


def loss_kernel(
    ends_ref, where_ref, queries_ref, docs_ref, tables_ref, times_ref, first_ref,
    loss_ref, grad_queries_ref, grad_docs_ref, table, *, micro_step
):
    step = pl.program_id(0)
    devices, width = queries_ref.shape[:2]
    tokens = devices * width
    queries_t = queries_ref[...].astype(WIDE).reshape(tokens, PROJ).T
    queries_low = queries_t.astype(LOW)
    members = members_of(ends_ref, micro_step, False)
    members_by_row = members_of(ends_ref, micro_step, True)
    spread_out = query_of_token(tokens, False)
    places = lax.broadcasted_iota(jnp.int32, (PROJ, 1), 0)
    grad_queries = jnp.zeros((PROJ, tokens), WIDE)
    grad_docs = jnp.zeros((DOC_ROWS, PROJ), WIDE)
    losses = jnp.zeros((1, 128), WIDE)
    times, first = times_ref[0], first_ref[0]
    own_rows = pl.ds(pl.multiple_of(where_ref[0] * 8, 8), 8)
    own_times, own_first = times_ref[0, own_rows], first_ref[0, own_rows]
    table[...] = jnp.zeros_like(table)
    for number, (cut, doc_scale, query_scale, similar) in enumerate(
        similar_parts(docs_ref[:DOC_ROWS], queries_t)
    ):
        for device in range(table.shape[0] // 8):
            table[8 * device : 8 * device + DOCS_DEV] = tables_ref[device, 0, number]
        scores = table[...]
        top = jnp.max(jnp.where(times > 0, scores, -1e30), axis=0, keepdims=True)
        top = jnp.where(top > -1e29, top, 0.0)
        normal = top + jnp.log(
            jnp.maximum(
                jnp.sum(times * jnp.exp(jnp.minimum(scores - top, 0.0)), axis=0, keepdims=True),
                1e-30,
            )
        )
        losses = losses + normal - jnp.sum(first * scores, axis=0, keepdims=True)
        own = table[own_rows]
        grad_score = own_times * jnp.exp(jnp.where(own_times > 0, own - normal, 0.0)) - own_first
        weights = jnp.exp(sharpness * similar)
        masses = exact_product(members, weights)
        by_token = product_by_ones(grad_score, spread_out)
        held = lax.broadcasted_iota(jnp.int32, masses.shape, 0) < DOCS_DEV
        by_token = jnp.where(held, by_token / jnp.where(held, masses, 1.0), 0.0)
        grad_similar = weights * exact_product(members_by_row, by_token)
        along = grad_similar * similar
        pulled = (grad_similar * doc_scale * query_scale).astype(LOW)
        mask = lax.broadcasted_iota(jnp.int32, (1, PROJ), 1) < PREFIXES[number]
        grad_docs = (
            grad_docs
            + jnp.where(mask, product_nt(pulled, queries_low), 0.0)
            - cut.astype(WIDE) * (doc_scale * doc_scale * jnp.sum(along, axis=1, keepdims=True))
        )
        toward = product_tn(cut, pulled)
        back = queries_t * (query_scale * query_scale * jnp.sum(along, axis=0, keepdims=True))
        grad_queries = grad_queries + toward - jnp.where(places < PREFIXES[number], back, 0.0)
    loss_ref[0] = losses
    grad_queries_ref[...] = grad_queries.T.reshape(devices, width, PROJ).astype(LOW)

    @pl.when(step == 0)
    def _():
        grad_docs_ref[...] = grad_docs

    @pl.when(step > 0)
    def _():
        grad_docs_ref[...] += grad_docs


class Loss:
    def __init__(self, micro_step, ends, pair_rows, dp_index, count):
        self.micro_step, self.ends, self.dp_index, self.count = micro_step, ends, dp_index, count
        self.group = math.gcd(count, 16)
        self.steps = count // self.group
        place = jnp.arange(8 * count, dtype=jnp.int32)
        doc_ids = jnp.where(place % 8 < DOCS_DEV, place // 8 * DOCS_DEV + place % 8, -1)
        picked = (pair_rows[None, :, :] == doc_ids[:, None, None]).astype(WIDE)
        self.times, self.first = [
            jnp.pad(
                jnp.swapaxes(value.reshape(8 * count, self.steps, -1), 0, 1),
                [(0, 0), (0, 0), (0, 128 - self.group * QRY_DEV)],
            )
            for value in (jnp.sum(picked, axis=2), picked[..., 0])
        ]
        self.params = dict(
            grid=(self.steps,), compiler_params=pltpu.CompilerParams(vmem_limit_bytes=40 << 20)
        )
        self.queries_spec = pl.BlockSpec((self.group, QRY_DEV * QLEN, PROJ), lambda i: (i, 0, 0))
        self.smem = pl.BlockSpec(memory_space=pltpu.SMEM)

    def scores(self, embedded):
        self.embedded = embedded
        self.queries = spread(embedded[DOC_ROWS:], self.count)
        return pl.pallas_call(
            partial(score_kernel, micro_step=self.micro_step),
            out_shape=jax.ShapeDtypeStruct((self.steps, 3, 8, 128), WIDE),
            in_specs=[
                self.smem,
                self.queries_spec,
                pl.BlockSpec((ROWS, PROJ), lambda i: (0, 0)),
            ],
            out_specs=pl.BlockSpec((1, 3, 8, 128), lambda i: (i, 0, 0, 0)),
            name="scores",
            cost_estimate=NO_COST,
            **self.params,
        )(self.ends, self.queries, embedded)[:, :, :DOCS_DEV]

    def grads(self, tables, *earlier):
        losses, grad_queries, grad_docs = pl.pallas_call(
            partial(loss_kernel, micro_step=self.micro_step),
            out_shape=(
                jax.ShapeDtypeStruct((self.steps, 1, 128), WIDE),
                jax.ShapeDtypeStruct(self.queries.shape, LOW),
                jax.ShapeDtypeStruct((DOC_ROWS, PROJ), WIDE),
            ),
            in_specs=[
                self.smem,
                self.smem,
                self.queries_spec,
                pl.BlockSpec((ROWS, PROJ), lambda i: (0, 0)),
                pl.BlockSpec((self.count, 1, 3, DOCS_DEV, 128), lambda i: (0, i, 0, 0, 0)),
                pl.BlockSpec((1, 8 * self.count, 128), lambda i: (i, 0, 0)),
                pl.BlockSpec((1, 8 * self.count, 128), lambda i: (i, 0, 0)),
            ],
            out_specs=(
                pl.BlockSpec((1, 1, 128), lambda i: (i, 0, 0)),
                self.queries_spec,
                pl.BlockSpec((DOC_ROWS, PROJ), lambda i: (0, 0)),
            ),
            scratch_shapes=[pltpu.VMEM((8 * self.count, 128), WIDE)],
            name="losses",
            cost_estimate=NO_COST,
            **self.params,
        )(
            self.ends,
            self.dp_index[None],
            self.queries,
            after(self.embedded, *earlier),
            tables,
            self.times,
            self.first,
        )
        losses = losses[:, 0, : self.group * QRY_DEV].reshape(self.count * QRY_DEV)
        own = lax.dynamic_slice_in_dim(losses, self.dp_index * QRY_DEV, QRY_DEV, 0)
        return own, grad_queries, grad_docs


def shards(
    tokens,
    qkv_weight,
    qkv_bias,
    out_weight,
    out_bias,
    norm1_gain,
    norm1_bias,
    up_weight,
    up_bias,
    down_weight,
    down_bias,
    norm2_gain,
    norm2_bias,
    proj_weight,
    doc_lengths,
    pair_docs,
):
    section_index = lax.axis_index("section")
    dp_index = lax.axis_index("dp")
    count = lax.axis_size("dp")
    dims = grid_of(count)
    at = coordinates(dims, dp_index)
    is_first = section_index == 0
    first = is_first.astype(jnp.int32)
    width, hidden = tokens.shape[1], up_weight.shape[2]
    own_height = width // count
    by_hand = own_height % 16 == 0

    segments, positions = [
        jnp.stack(value)
        for value in zip(*(doc_layout(doc_lengths[micro_step]) for micro_step in range(MICRO)))
    ]
    by_row = jnp.broadcast_to(segments[:, :, None], (MICRO, ROWS, ROWS // 2))
    layout = (*rotary(positions), by_row, segments[:, None, :])
    picks = [jnp.stack([first, jnp.int32(micro_step)]) for micro_step in range(MICRO)]
    own_rows = [tokens[micro_step * ROWS : (micro_step + 1) * ROWS] for micro_step in range(MICRO)]
    ends = jnp.cumsum(doc_lengths, axis=1)
    pair_rows = pair_docs.reshape(count, MICRO, QRY_DEV, CANDS)
    losses_of = [
        Loss(
            micro_step,
            ends,
            pair_rows[:, micro_step].reshape(count * QRY_DEV, CANDS),
            dp_index,
            count,
        )
        for micro_step in range(MICRO)
    ]

    vectors = (
        qkv_bias,
        out_bias,
        norm1_gain,
        norm1_bias,
        up_bias,
        down_bias,
        norm2_gain,
        norm2_bias,
    )
    lengths = [value.shape[1] for value in vectors]
    short = sum(lengths)
    shards_of = [out_weight[0], qkv_weight[0], up_weight[0], down_weight[0]]

    fetched = (width, width, hidden // 4, width // 2)

    def small_parameters(layer, rows, projection):
        cuts, start = [], 0
        for length in lengths:
            cuts.append(rows[:, start : start + length].astype(WIDE).reshape(-1))
            start += length
        qkv_b, out_b, gain_one, bias_one, up_b, down_b, gain_two, bias_two = cuts
        layer.qkv_bias = qkv_b.reshape(3, width)
        layer.up_bias = up_b[None]
        layer.small = jnp.concatenate(
            [
                jnp.stack([out_b, gain_one, bias_one, down_b, gain_two, bias_two]),
                jnp.zeros((2, width), WIDE),
            ]
        )
        return projection.reshape(width, -1)

    if by_hand:
        line = jnp.concatenate([*vectors, jnp.zeros((1, width - short), LOW)], axis=1)
        proj_lines = proj_weight.reshape(-1, width)
        filler = jnp.zeros((15 - proj_lines.shape[0], width), LOW)
        order = list(range(len(dims)))
        chunks = [(jnp.concatenate([shards_of[0], line, proj_lines, filler]), order, 0)]
        cuts_of = ([1], [1, 2], [2, 2], [2, 2])
        for number in (1, 2, 3):
            parts, shard = cuts_of[number], shards_of[number]
            unit, start = shard.shape[1] // sum(parts), 0
            for part in parts:
                value = lax.slice_in_dim(shard, start, start + part * unit, axis=1)
                chunks.append((value, order, len(chunks)))
                start += part * unit
        gather = Gather(chunks, dims)
        layer = Layer(block_owners(order, dims, at), layout)

        def whole(number, first_chunk):
            parts, start = [], 0
            unit = shards_of[number].shape[1] // sum(cuts_of[number])
            for offset, part in enumerate(cuts_of[number]):
                parts.append((start, part * unit, gather.groups(first_chunk + offset)))
                start += part * unit
            return Weight(count, shards_of[number].shape[0], start, fetched[number], parts)

        layer.out = whole(0, 0)
        block = placed_rows(layer.out.arrays, layer.places, own_height, 16)
        projection = small_parameters(
            layer, block[:, 0], block[:, 1 : 1 + proj_lines.shape[0]]
        )
        layer.qkv = whole(1, 1)
        states = [layer.attend(rows, pick) for rows, pick in zip(own_rows, picks)]
        gather.advance()
        gather.advance(states[0]["norm"])
        layer.up = whole(2, 3)
        for state, pick in zip(states, picks):
            state |= layer.rise(state["norm"], pick)
        gather.advance(states[1]["norm"])
        gather.advance(*(state["active"] for state in states))
        layer.down = whole(3, 5)
    else:
        layer = Layer(jnp.zeros((1,), jnp.int32), layout)
        wholes = [
            lax.all_gather(value, "dp", axis=0, tiled=True)[None] for value in shards_of
        ]
        layer.out, layer.qkv, layer.up, layer.down = [
            Weight(1, *value.shape[1:], columns, [(0, value.shape[2], [value])])
            for value, columns in zip(wholes, fetched)
        ]
        together = spread(jnp.concatenate([*vectors, proj_weight.reshape(1, -1)], axis=1)[0], count)
        projection = small_parameters(layer, together[:, :short], together[:, short:])
        states = [layer.attend(rows, pick) for rows, pick in zip(own_rows, picks)]
        for state, pick in zip(states, picks):
            state |= layer.rise(state["norm"], pick)

    arrived = []
    for state, pick in zip(states, picks):
        active = after(state["active"], *(one["result"] for one in states if "result" in one))
        state |= layer.fall(active, state["norm"], pick)
        arrived.append(from_behind(state["result"], "section", 1))
    own_scores = []
    for micro_step in range(MICRO):
        last = micro_step == MICRO - 1
        states.append(
            layer.forward(
                arrived[micro_step],
                picks[micro_step],
                projection,
                [state["result"] for state in states] if last else (),
            )
        )
        own_scores.append(losses_of[micro_step].scores(states[-1]["embedded"]))
    activations = states[-1]["activations"][None]

    tables = spread(jnp.stack(own_scores), count)
    own_losses, loss_grads = [None] * MICRO, [None] * MICRO
    earlier = []
    for micro_step in reversed(range(MICRO)):
        own_losses[micro_step], grad_queries, grad_docs = losses_of[micro_step].grads(
            tables[:, micro_step], *earlier
        )
        earlier = [grad_queries]
        loss_grads[micro_step] = (
            grad_docs,
            lax.all_to_all(grad_queries, "dp", 0, 0, tiled=True),
            projection,
        )
    own_losses = jnp.concatenate(own_losses)
    query_losses = jnp.where(is_first, from_behind(own_losses, "section", -1), own_losses)
    loss_grads[0] = (after(loss_grads[0][0], query_losses), *loss_grads[0][1:])

    back, back_grads = [], []
    for micro_step in reversed(range(MICRO)):
        back.append(
            layer.backward(states[MICRO + micro_step], loss_grads[micro_step], None, picks[micro_step])
        )
        back_grads.append(from_behind(back[-1]["grad_low"], "section", -1))
    back.append(layer.backward(states[1], None, back_grads[0], picks[1]))
    back_grad = after(back_grads[1], back[-1]["mixed"])
    grads = layer.norm_back(states[0], back_grad, picks[0])
    vectors_of = [one["vectors"] for one in (*back, grads)]

    def pairs(values):
        return [values[1], values[3]], [values[0], values[2]]

    lefts = [
        pairs([state[name] for state in states]) for name in ("active", "norm", "mixture")
    ] + [pairs([*own_rows, *arrived])]

    def rights_of(name):
        return pairs([grads[name], *(back[number][name] for number in (2, 1, 0))])

    def feed_back(*earlier):
        grads.update(
            layer.feed_back(states[0], after(grads["branch"], *earlier), grads["total"], picks[0])
        )

    def attend_back(*earlier):
        grads.update(
            layer.attend_back(
                states[0],
                after(grads["attended"], *earlier),
                grads["grad_one"],
                [one["grad_source"] for one in back],
                picks[0],
            )
        )

    if by_hand:
        last_dim = len(dims) - 2
        weights = {}

        def weight_of(name, number, right):
            weights[name] = Scatter(
                name, lefts[number], rights_of(right), dims, at, last_dim, first
            )
            return weights[name]

        half = width // 2
        downs = [weight_of("down", 0, "branch") for _ in range(2)]
        for number, (weight, earlier) in enumerate(zip(downs, ([], [downs[0]]))):
            weight.make(NO_COST, [one.sent for one in earlier], number * half, half)
            weight.other = shifted(weight.sent, dims, len(dims) - 1, 1)
        pieces = {0: downs[0].keep(0, half, NO_COST, [downs[1].sent])}

        def first_stage(earlier):
            feed_back(*pieces[0])
            vectors_of.append(grads["vectors"])
            sent = weight_of("up", 1, "gate").make(SOME_COST)
            pieces[1] = downs[1].keep(half, half, SOME_COST, [sent])
            return pieces[1]

        def second_stage(earlier):
            attend_back(*earlier)
            vectors_of.append(grads["vectors"])
            pieces[2] = weights["up"].keep(0, hidden // 2, SOME_COST, [grads["mixed"]])
            return pieces[2]

        def third_stage(earlier):
            sent = weight_of("qkv", 3, "mixed").make(FULL_COST, earlier)
            sent = weight_of("out", 2, "attended").make(FULL_COST, [sent])
            pieces[3] = weights["up"].keep(hidden // 2, hidden // 2, FULL_COST, [sent])
            return pieces[3]

        def fourth_stage(earlier):
            pieces[4] = weights["qkv"].keep(0, 2 * width, FULL_COST, earlier)
            pieces[5] = weights["qkv"].keep(2 * width, width, FULL_COST, pieces[4])
            return pieces[5]

        def fifth_stage(earlier):
            pieces[6] = weights["out"].keep(0, width, FULL_COST, earlier)
            return pieces[6]

        def projection_grad():
            total = product_tn(
                jnp.concatenate([state["result"] for state in states[:1:-1]]),
                jnp.concatenate([one["grad_embedded"] for one in back[:MICRO]]),
            ) * section_index.astype(WIDE)
            parts = jnp.swapaxes(total.reshape(2, count, -1, total.shape[1]), 0, 1)
            riding.append(Halved(parts, dims, at))
            return riding[-1]

        def vector_grads():
            riding.append(Whole(sum(vectors_of)))
            return riding[-1]

        riding = []
        sums = travels(
            pieces,
            7,
            list(reversed(range(last_dim + 1))),
            dims,
            at,
            {
                1: lambda: [weights["up"]],
                3: lambda: [weights["qkv"], weights["out"]],
            },
            {4: lambda: [projection_grad(), vector_grads()]},
            [first_stage, second_stage, third_stage, fourth_stage, fifth_stage],
        )
        proj_own, own_vectors = riding[0].value[0], riding[1].value
        grad_down, grad_up, grad_qkv = (
            jnp.concatenate(group, axis=1)[None] for group in (sums[0:2], sums[2:4], sums[4:6])
        )
        grad_out = sums[6][None]
    else:
        feed_back()
        vectors_of.append(grads["vectors"])
        attend_back()
        weight_grads = []
        for number, name in enumerate(("branch", "gate", "attended", "mixed")):
            left = jnp.concatenate([jnp.where(is_first, *pair) for pair in lefts[number]])
            right = [jnp.where(is_first, *pair) for pair in rights_of(name)]
            if number == 3:
                right = [jnp.swapaxes(value, 0, 1).reshape(ROWS, -1) for value in right]
            weight_grads.append(
                scatter_rows_plain(left, jnp.concatenate(right), dims, dp_index)[None]
            )
        grad_down, grad_up, grad_out, grad_qkv = weight_grads
        own_vectors = lax.psum(sum([*vectors_of, grads["vectors"]]), "dp")
        proj_total = product_tn(
            jnp.concatenate([state["result"] for state in states[:1:-1]]),
            jnp.concatenate([one["grad_embedded"] for one in back[:MICRO]]),
        ) * section_index.astype(WIDE)
        proj_own = summed(jnp.swapaxes(proj_total.reshape(2, count, -1, PROJ), 0, 1))
    grad_inputs = grads["grad_source"]
    proj_grad = jnp.where(is_first, from_behind(proj_own[0], "section", -1), proj_own[1])
    grad_qkv_b, grad_out_b, grad_gain1, grad_bias1, grad_up_b, grad_down_b, grad_gain2, grad_bias2 = (
        own_parts(
            own_vectors,
            [
                (first_row, rows, rows * width // count)
                for first_row, rows in (
                    (0, 3), (3, 1), (4, 1), (5, 1), (6, hidden // width), (10, 1), (11, 1), (12, 1)
                )
            ],
            dp_index,
        )
    )
    return (
        query_losses,
        activations,
        grad_inputs[None],
        grad_qkv,
        grad_qkv_b,
        grad_out,
        grad_out_b,
        grad_gain1,
        grad_bias1,
        grad_up,
        grad_up_b,
        grad_down,
        grad_down_b,
        grad_gain2,
        grad_bias2,
        proj_grad,
    )


def solution(mesh):
    in_specs = (
        P("dp", None),
        P("section", "dp", None),
        P("section", "dp"),
        P("section", "dp", None),
        P("section", "dp"),
        P("section", "dp"),
        P("section", "dp"),
        P("section", "dp", None),
        P("section", "dp"),
        P("section", "dp", None),
        P("section", "dp"),
        P("section", "dp"),
        P("section", "dp"),
        P("dp", None),
        P("dp", None),
        P(),
    )
    out_specs = (
        P("dp"),
        P("section", "dp", None),
        P("section", "dp", None),
        P("section", "dp", None),
        P("section", "dp"),
        P("section", "dp", None),
        P("section", "dp"),
        P("section", "dp"),
        P("section", "dp"),
        P("section", "dp", None),
        P("section", "dp"),
        P("section", "dp", None),
        P("section", "dp"),
        P("section", "dp"),
        P("section", "dp"),
        P(("section", "dp"), None),
    )
    return jax.shard_map(shards, mesh=mesh, in_specs=in_specs, out_specs=out_specs, check_vma=False)
```

```python
from functools import partial
import math

import jax
import jax.numpy as jnp
from jax import lax
from jax.experimental import pallas as pl
from jax.experimental.pallas import tpu as pltpu
from jax.sharding import PartitionSpec as P

HEAD = 64
PROJ = 128
QLEN = 32
DOC_ROWS = 192
QRY_DEV = 2
DOCS_DEV = 3
MICRO = 2
CANDS = 8
ROWS = 256
PREFIXES = (PROJ // 2, 3 * PROJ // 4, PROJ)


norm_eps = 1e-05
unit_eps = 1e-06
sharpness = 20.0
score_scale = 0.125
masked_score = -1000000000.0


def from_behind(value, axis, steps):
    count = lax.axis_size(axis)
    first, last = (max(0, -steps), min(count, count - steps))
    return lax.ppermute(value, axis, [(source, source + steps) for source in range(first, last)])


def product(left_side, right_side):
    return jnp.dot(left_side, right_side, preferred_element_type=jnp.float32)


def product_tn(left_side, right_side):
    return lax.dot_general(
        left_side, right_side, (((0,), (0,)), ((), ())), preferred_element_type=jnp.float32
    )


def product_nt(left_side, right_side):
    return lax.dot_general(
        left_side, right_side, (((1,), (1,)), ((), ())), preferred_element_type=jnp.float32
    )


def doc_layout(doc_lens):
    row_ids = jnp.arange(ROWS, dtype=jnp.int32)
    ends_at = jnp.cumsum(doc_lens)
    starts_at = ends_at - doc_lens
    doc_of = jnp.sum((row_ids[:, None] >= ends_at[None, :]).astype(jnp.int32), axis=1)
    doc_index = jnp.arange(DOCS_DEV, dtype=jnp.int32)
    begins = jnp.sum(
        jnp.where(doc_of[:, None] == doc_index[None, :], starts_at[None, :], 0), axis=1
    )
    in_docs = row_ids < DOC_ROWS
    query_rows = jnp.maximum(row_ids - DOC_ROWS, 0)
    segment = jnp.where(in_docs, doc_of, DOCS_DEV + query_rows // QLEN)
    position = jnp.where(in_docs, row_ids - begins, query_rows % QLEN)
    return (segment, position)


def rotary(position):
    step_ids = jnp.arange(HEAD // 2, dtype=jnp.int32).astype(jnp.float32)
    frequency = jnp.exp(step_ids * (-2.0 * math.log(10000.0) / HEAD))
    angles = position.astype(jnp.float32)[..., None] * frequency
    cosine, sine = jnp.cos(angles), jnp.sin(angles)
    return (
        jnp.concatenate([cosine] * 4, axis=-1),
        jnp.concatenate([-sine, sine] * 2, axis=-1),
    )


def lane_ids():
    return lax.broadcasted_iota(jnp.int32, (1, 2 * HEAD), 1)


def turned(value, cosine, sine):
    in_first = lane_ids() % HEAD < HEAD // 2
    ahead = pltpu.roll(value, 2 * HEAD - HEAD // 2, 1)
    behind = pltpu.roll(value, HEAD // 2, 1)
    return value * cosine + jnp.where(in_first, ahead, behind) * sine


def statistics(values):
    center = values - jnp.mean(values, axis=1, keepdims=True)
    spread = jnp.mean(center * center, axis=1, keepdims=True)
    scale = lax.rsqrt(spread + norm_eps)
    return center * scale, scale


def norm_back(grad, unit, scale, gain):
    inner = grad * gain
    along = jnp.mean(inner * unit, axis=1, keepdims=True)
    grad_in = scale * (inner - jnp.mean(inner, axis=1, keepdims=True) - unit * along)
    return grad_in, jnp.sum(grad * unit, axis=0, keepdims=True), jnp.sum(grad, axis=0, keepdims=True)


def gelu_parts(value):
    bell = jnp.exp(-0.5 * value * value)
    part = 1.0 / (1.0 + (0.3275911 * math.sqrt(0.5)) * jnp.abs(value))
    tail = 0.5 * 1.061405429 * part - 0.5 * 1.453152027
    tail = tail * part + 0.5 * 1.421413741
    tail = tail * part - 0.5 * 0.284496736
    tail = tail * part + 0.5 * 0.254829592
    tail = tail * part * bell
    below = jnp.where(value >= 0, 1.0 - tail, tail)
    return value * below, below + value * bell * (1.0 / math.sqrt(2.0 * math.pi))


def probabilities(queries, keys, allowed, held):
    scores = product_nt(jnp.where(held, queries, jnp.zeros_like(queries)), keys)
    scores = jnp.where(allowed, scores, masked_score)
    scores = jnp.exp(scores - jnp.max(scores, axis=1, keepdims=True))
    return scores * (1.0 / jnp.sum(scores, axis=1, keepdims=True))


LOW, WIDE = jnp.bfloat16, jnp.float32
VMEM_LIMIT = 46 << 20


def in_hbm(array):
    if array.size < 1 << 17:
        return array
    return pltpu.with_memory_space_constraint(array, pltpu.HBM)


BLOCK = 512
NO_COST = pl.CostEstimate(flops=1, bytes_accessed=1, transcendentals=0)
FULL_COST = pl.CostEstimate(flops=40 * 10**9, bytes_accessed=10**8, transcendentals=0)


class Weight:
    def __init__(self, count, rows, columns, width, parts):
        self.count, self.rows, self.columns, self.width = count, rows, columns, width
        self.height = self.count * rows
        self.arrays = [group for _, _, groups in parts for group in groups]
        self.plan = [
            (start, width, [group.shape[0] for group in groups]) for start, width, groups in parts
        ]

    def scratch(self):
        return [
            pltpu.VMEM((self.height, self.columns), LOW),
            pltpu.SemaphoreType.DMA((self.columns // self.width, self.count)),
        ]


class Fetch:
    def __init__(self, weight, places_ref, refs, buffer, sems):
        self.weight, self.places_ref = weight, places_ref
        self.refs, self.buffer, self.sems = refs, buffer, sems
        self.waited = set()

    def copies(self, number):
        weight, begin = self.weight, number * self.weight.width
        passed = 0
        for start, width, lengths in weight.plan:
            if start <= begin < start + width:
                break
            passed += len(lengths)
        columns = pl.ds(begin - start, weight.width)
        block = 0
        for group, length in enumerate(lengths):
            for inner in range(length):
                place = pl.multiple_of(self.places_ref[block] * weight.rows, weight.rows)
                yield pltpu.make_async_copy(
                    self.refs[passed + group].at[inner, pl.ds(0, weight.rows), columns],
                    self.buffer.at[pl.ds(place, weight.rows), pl.ds(begin, weight.width)],
                    self.sems.at[number, block],
                )
                block += 1

    def start(self):
        for number in range(self.weight.columns // self.weight.width):
            for copy in self.copies(number):
                copy.start()

    def ready(self, until=None):
        until = self.weight.columns if until is None else until
        for number in range(-(-until // self.weight.width)):
            if number not in self.waited:
                self.waited.add(number)
                for copy in self.copies(number):
                    copy.wait()
        return self.buffer


class Parts:
    def __init__(self, refs, loads, weights, outs, scratch):
        self.pick, self.places, *refs = refs
        loaded, refs = refs[: len(loads)], refs[len(loads) :]
        fetched = {}
        for name, weight in weights.items():
            fetched[name], refs = refs[: len(weight.arrays)], refs[len(weight.arrays) :]
        stored, refs = refs[: len(outs)], refs[len(outs) :]
        self.buffers, refs = dict(zip(loads, refs)), refs[len(loads) :]
        self.weights = {}
        for name, weight in weights.items():
            buffer, sems, *refs = refs
            self.weights[name] = Fetch(weight, self.places, fetched[name], buffer, sems)
        self.outs, refs = dict(zip(outs, refs)), refs[len(outs) :]
        self.scratch, refs = dict(zip(scratch, refs)), refs[len(scratch) :]
        load_sems, out_sems = refs
        self.loads = {
            name: pltpu.make_async_copy(ref, self.buffers[name], load_sems.at[number])
            for number, (name, ref) in enumerate(zip(loads, loaded))
        }
        self.stores = {
            name: pltpu.make_async_copy(self.outs[name], ref, out_sems.at[number])
            for number, (name, ref) in enumerate(zip(outs, stored))
        }
        self.waited, self.begun = set(), set()

    def start(self, order):
        for name in order:
            (self.loads[name] if name in self.loads else self.weights[name]).start()

    def ref(self, name):
        if name in self.outs:
            return self.outs[name]
        if name in self.scratch:
            return self.scratch[name]
        if name not in self.waited:
            self.waited.add(name)
            self.loads[name].wait()
        return self.buffers[name]

    def refs(self, *names):
        return [self.ref(name) for name in names]

    def leave(self, *names):
        for name in names:
            self.stores[name].start()

    def finish(self):
        for name in self.stores:
            self.stores[name].wait()


def run_parts(name, bodies, pick, places, loads, weights, outs, scratch, order, cost):
    def kernel(*refs):
        parts = Parts(refs, list(loads), weights, list(outs), list(scratch))
        parts.start(order)
        for body in bodies:
            body(parts)
        if "vectors" in outs:
            parts.leave("vectors")
        parts.finish()

    arrays = [*loads.values(), *(array for weight in weights.values() for array in weight.arrays)]
    scratch_shapes = [pltpu.VMEM(array.shape, array.dtype) for array in loads.values()]
    scratch_shapes += [entry for weight in weights.values() for entry in weight.scratch()]
    scratch_shapes += [pltpu.VMEM(*out) for out in outs.values()] + list(scratch.values())
    results = pl.pallas_call(
        kernel,
        in_specs=[pl.BlockSpec(memory_space=pltpu.SMEM)] * 2
        + [pl.BlockSpec(memory_space=pl.ANY)] * len(arrays),
        out_specs=[pl.BlockSpec(memory_space=pltpu.HBM)] * len(outs),
        out_shape=[pltpu.HBM(*out) for out in outs.values()],
        scratch_shapes=scratch_shapes
        + [pltpu.SemaphoreType.DMA((len(loads),)), pltpu.SemaphoreType.DMA((len(outs),))],
        compiler_params=pltpu.CompilerParams(vmem_limit_bytes=VMEM_LIMIT),
        cost_estimate=cost,
        name=name,
    )(pick, places, *(in_hbm(array) for array in arrays))
    return dict(zip(outs, results))


def attend_part(parts):
    micro_step = parts.pick[1]
    source = parts.ref("x")
    cos_ref, sin_ref, column_ref, row_ref, bias_ref = parts.refs(
        "cosine", "sine", "column", "row", "qkv_bias"
    )
    cosine, sine = cos_ref[micro_step], sin_ref[micro_step]
    outs = parts.refs("q", "k", "v")
    width = source.shape[1]
    for part, ref in enumerate(outs):
        qkv = parts.weights["qkv"].ready((part + 1) * width)
        for start in range(0, width, BLOCK):
            at = slice(part * width + start, part * width + start + BLOCK)
            value = product(source[...], qkv[:, at])
            value = value + bias_ref[part : part + 1, start : start + BLOCK]
            for pair in range(0, BLOCK, 2 * HEAD):
                two = value[:, pair : pair + 2 * HEAD]
                if part < 2:
                    two = turned(two, cosine, sine)
                ref[:, start + pair : start + pair + 2 * HEAD] = two.astype(LOW)
    parts.leave("q", "k", "v")
    allowed = jnp.concatenate([column_ref[micro_step]] * 2, axis=1) == row_ref[micro_step]
    q_ref, k_ref, v_ref = outs
    mixture_ref, sum_ref, norm_ref, small_ref = parts.refs("mixture", "sum_one", "norm", "small")
    for start in range(0, width, 2 * HEAD):
        at = slice(start, start + 2 * HEAD)
        queries = q_ref[:, at] * LOW(score_scale)
        keys, values = k_ref[:, at], v_ref[:, at]
        mixed = []
        for head in range(2):
            held = lane_ids() // HEAD == head
            attention = probabilities(queries, keys, allowed, held)
            mixed.append(product(attention.astype(LOW), values))
        mixture_ref[:, at] = jnp.where(lane_ids() < HEAD, mixed[0], mixed[1]).astype(LOW)
    out = parts.weights["out"].ready()
    for start in range(0, width, BLOCK):
        at = slice(start, start + BLOCK)
        sum_ref[:, at] = (
            source[:, at].astype(WIDE)
            + small_ref[0:1, at]
            + product(mixture_ref[...], out[:, at])
        )
    unit, _ = statistics(sum_ref[...])
    norm_ref[...] = (unit * small_ref[1:2] + small_ref[2:3]).astype(LOW)
    parts.leave("mixture", "sum_one", "norm")


def up_part(parts):
    norm_ref, bias_ref, active_ref, slope_ref = parts.refs("norm", "up_bias", "active", "slope")
    for start in range(0, active_ref.shape[1], BLOCK):
        up = parts.weights["up"].ready(start + BLOCK)
        at = slice(start, start + BLOCK)
        active, slope = gelu_parts(product(norm_ref[...], up[:, at]) + bias_ref[:, at])
        active_ref[:, at] = active.astype(LOW)
        slope_ref[:, at] = slope.astype(LOW)
    parts.leave("active", "slope")


def down_part(parts):
    active_ref, norm_ref, small_ref = parts.refs("active", "norm", "small")
    sum_ref, result_ref = parts.refs("sum_two", "result")
    for start in range(0, sum_ref.shape[1], BLOCK):
        at = slice(start, start + BLOCK)
        down = parts.weights["down"].ready(start + BLOCK)
        sum_ref[:, at] = (
            norm_ref[:, at].astype(WIDE)
            + small_ref[3:4, at]
            + product(active_ref[...], down[:, at])
        )
    unit, _ = statistics(sum_ref[...])
    result = (unit * small_ref[4:5] + small_ref[5:6]).astype(LOW)
    result_ref[...] = result
    parts.leave("result", "sum_two")
    if "embedded" in parts.outs:
        parts.ref("embedded")[...] = product(result, parts.ref("projection")[...]).astype(LOW)
        parts.leave("embedded")
    if "activations" in parts.outs:
        early, late, own, both = parts.refs("early", "late", "own", "activations")

        @pl.when(parts.pick[0] == 1)
        def _():
            both[:ROWS] = early[...]
            both[ROWS:] = late[...]

        @pl.when(parts.pick[0] == 0)
        def _():
            both[:ROWS] = own[...]
            both[ROWS:] = result

        parts.leave("activations")


def vector_rows(parts):
    vector_ref = parts.ref("vectors")
    if "vectors" not in parts.begun:
        parts.begun.add("vectors")
        vector_ref[...] = jnp.zeros_like(vector_ref)
    return vector_ref


def norm_back_part(parts):
    if "docs" in parts.loads:
        own = jnp.sum(parts.ref("own_parts")[...].astype(WIDE), axis=0)
        embedded = jnp.concatenate([parts.ref("docs")[...], own], axis=0).astype(LOW)
        parts.ref("grad_embedded")[...] = embedded
        parts.leave("grad_embedded")
        upstream = product_nt(embedded, parts.ref("projection")[...])
        upstream = upstream * (1 - parts.pick[0]).astype(WIDE)
    else:
        upstream = parts.ref("back")[...].astype(WIDE)
    branch_ref, total, small_ref = parts.refs("branch", "total", "small")
    vector_ref = vector_rows(parts)
    unit, scale = statistics(parts.ref("sum_two")[...])
    grad, gain, bias = norm_back(upstream, unit, scale, small_ref[4:5])
    low = grad.astype(LOW)
    branch_ref[...] = low
    total[...] = grad
    vector_ref[10:11] = jnp.sum(low.astype(WIDE), axis=0, keepdims=True)
    vector_ref[11:12] = gain
    vector_ref[12:13] = bias
    parts.leave("branch")
    if "total" in parts.outs:
        parts.leave("total")


def feed_back_part(parts):
    branch_ref, gate_ref, attended_ref = parts.refs("branch", "gate", "attended")
    small_ref, slope_ref = parts.refs("small", "slope")
    vector_ref = vector_rows(parts)
    width = attended_ref.shape[1]
    down = parts.weights["down"].ready()
    for start in range(0, gate_ref.shape[1], BLOCK):
        at = slice(start, start + BLOCK)
        gate = product_nt(branch_ref[...], down[at]) * slope_ref[:, at].astype(WIDE)
        gate = gate.astype(LOW)
        gate_ref[:, at] = gate
        row, column = 6 + start // width, start % width
        vector_ref[row : row + 1, column : column + BLOCK] = jnp.sum(
            gate.astype(WIDE), axis=0, keepdims=True
        )
    parts.leave("gate")
    up = parts.weights["up"].ready()
    total = parts.ref("total")
    for start in range(0, total.shape[1], BLOCK):
        at = slice(start, start + BLOCK)
        total[:, at] += product_nt(gate_ref[...], up[at])
    unit, scale = statistics(parts.ref("sum_one")[...])
    grad, gain, bias = norm_back(total[...], unit, scale, small_ref[1:2])
    total[...] = grad
    low = grad.astype(LOW)
    attended_ref[...] = low
    vector_ref[3:4] = jnp.sum(low.astype(WIDE), axis=0, keepdims=True)
    vector_ref[4:5] = gain
    vector_ref[5:6] = bias
    parts.leave("attended")
    if "grad_one" in parts.outs:
        parts.ref("grad_one")[...] = grad
        parts.leave("grad_one")


def attend_back_part(parts):
    micro_step = parts.pick[1]
    attended_ref, mixed_ref, mixture, total = parts.refs("attended", "mixed", "mixture", "total")
    vector_ref = vector_rows(parts)
    cos_ref, sin_ref, column_ref, row_ref = parts.refs("cosine", "sine", "column", "row")
    cosine, sine = cos_ref[micro_step], sin_ref[micro_step]
    allowed = jnp.concatenate([column_ref[micro_step]] * 2, axis=1) == row_ref[micro_step]
    width = mixture.shape[1]
    if "grad_one" in parts.loads:
        total[...] = parts.ref("grad_one")[...]
    out = parts.weights["out"].ready()
    for start in range(0, width, BLOCK):
        at = slice(start, start + BLOCK)
        mixture[:, at] = product_nt(attended_ref[...], out[at]).astype(LOW)
    q_ref, k_ref, v_ref = parts.refs("q", "k", "v")
    for start in range(0, width, 2 * HEAD):
        at = slice(start, start + 2 * HEAD)
        queries, keys, values = q_ref[:, at], k_ref[:, at], v_ref[:, at]
        scaled = queries * LOW(score_scale)
        grad_mixture = mixture[:, at]
        grads = []
        for head in range(2):
            held = lane_ids() // HEAD == head
            attention = probabilities(scaled, keys, allowed, held)
            own = jnp.where(held, grad_mixture, jnp.zeros_like(grad_mixture))
            grad_attention = product_nt(own, values)
            grad_values = product_tn(attention.astype(LOW), own)
            along = jnp.sum(grad_attention * attention, axis=1, keepdims=True)
            grad_scores = (attention * (grad_attention - along)).astype(LOW)
            grads.append((product(grad_scores, keys), product_tn(grad_scores, queries), grad_values))
        first_head = lane_ids() < HEAD
        for part in range(2):
            value = jnp.where(first_head, grads[0][part], grads[1][part]) * score_scale
            mixed_ref[part, :, at] = turned(value, cosine, -sine).astype(LOW)
        mixed_ref[2, :, at] = (grads[0][2] + grads[1][2]).astype(LOW)
    parts.leave("mixed")
    for part in range(3):
        vector_ref[part : part + 1] = jnp.sum(
            mixed_ref[part].astype(WIDE), axis=0, keepdims=True
        )
    qkv = parts.weights["qkv"].ready()
    for start in range(0, width, BLOCK):
        at = slice(start, start + BLOCK)
        value = total[:, at]
        for part in range(3):
            value = value + product_nt(mixed_ref[part], qkv[at, part * width : (part + 1) * width])
        total[:, at] = value
    if "grad_low" in parts.outs:
        parts.ref("grad_low")[...] = total[...].astype(LOW)
        parts.leave("grad_low")
        parts.ref("grad_source")[...] = total[...]
    else:
        late, early, own, source_ref = parts.refs("late", "early", "own", "grad_source")

        @pl.when(parts.pick[0] == 1)
        def _():
            source_ref[:ROWS] = total[...]
            source_ref[ROWS:] = own[...]

        @pl.when(parts.pick[0] == 0)
        def _():
            source_ref[:ROWS] = early[...]
            source_ref[ROWS:] = late[...]

    parts.leave("grad_source")


class Layer:
    def __init__(self, places, layout):
        self.places = places
        self.layout = dict(zip(("cosine", "sine", "column", "row"), layout))

    def attend_set(self, source):
        rows = source.shape
        return (
            {"x": source, **self.layout, "qkv_bias": self.qkv_bias, "small": self.small},
            {"qkv": self.qkv, "out": self.out},
            {
                "q": (rows, LOW),
                "k": (rows, LOW),
                "v": (rows, LOW),
                "mixture": (rows, LOW),
                "sum_one": (rows, WIDE),
                "norm": (rows, LOW),
            },
            {},
        )

    def up_set(self):
        rows = (ROWS, self.up.columns)
        return (
            {"up_bias": self.up_bias},
            {"up": self.up},
            {"active": (rows, LOW), "slope": (rows, LOW)},
            {},
        )

    def down_set(self, projection, earlier):
        rows = (ROWS, self.down.columns)
        loads = {"small": self.small}
        outs = {"sum_two": (rows, WIDE), "result": (rows, LOW)}
        if projection is not None:
            loads["projection"] = projection
            outs["embedded"] = ((ROWS, PROJ), LOW)
        if earlier:
            loads |= dict(zip(("early", "late", "own"), earlier))
            outs["activations"] = ((MICRO * ROWS, self.down.columns), LOW)
        return loads, {"down": self.down}, outs, {}

    def run(self, name, bodies, sets, pick, more=None, cost=NO_COST):
        loads, weights, outs, scratch = dict(more or {}), {}, {}, {}
        order = list(loads)
        for one in sets:
            order += [key for key in (*one[0], *one[1]) if key not in order]
            loads, weights = loads | one[0], weights | one[1]
            outs, scratch = outs | one[2], scratch | one[3]
        return run_parts(
            name, bodies, pick, self.places, loads, weights, outs, scratch, order, cost
        )

    def attend(self, source, pick):
        return self.run("attend", [attend_part], [self.attend_set(source)], pick)

    def rise(self, norm, pick):
        return self.run("up", [up_part], [self.up_set()], pick, {"norm": norm})

    def fall(self, active, norm, pick):
        return self.run(
            "down", [down_part], [self.down_set(None, ())], pick, {"active": active, "norm": norm}
        )

    def forward(self, source, pick, projection, earlier):
        return self.run(
            "forward",
            [attend_part, up_part, down_part],
            [self.attend_set(source), self.up_set(), self.down_set(projection, earlier)],
            pick,
            cost=FULL_COST,
        )

    def norm_back_set(self, state, loss_grads, back_grad):
        rows = (ROWS, self.down.columns)
        outs = {"branch": (rows, LOW), "vectors": ((16, rows[1]), WIDE)}
        if loss_grads is not None:
            loads = dict(zip(("docs", "own_parts", "projection"), loss_grads))
            outs["grad_embedded"] = ((ROWS, PROJ), LOW)
        else:
            loads = {"back": back_grad}
        loads |= {"sum_two": state["sum_two"], "small": self.small}
        return loads, {}, outs, {"total": pltpu.VMEM(rows, WIDE)}

    def feed_back_set(self, state):
        rows, hidden = (ROWS, self.down.columns), self.up.columns
        return (
            {"slope": state["slope"], "small": self.small},
            {"down": self.down, "up": self.up},
            {
                "gate": ((ROWS, hidden), LOW),
                "attended": (rows, LOW),
                "vectors": ((16, rows[1]), WIDE),
            },
            {"total": pltpu.VMEM(rows, WIDE)},
        )

    def attend_back_set(self, state, earlier):
        rows = (ROWS, self.out.columns)
        outs = {"mixed": ((3, *rows), LOW), "vectors": ((16, rows[1]), WIDE)}
        loads = {"q": state["q"], "k": state["k"], "v": state["v"], **self.layout}
        if earlier:
            loads |= dict(zip(("late", "early", "own"), earlier))
            outs["grad_source"] = ((MICRO * ROWS, rows[1]), WIDE)
        else:
            outs |= {"grad_source": (rows, WIDE), "grad_low": (rows, LOW)}
        return (
            loads,
            {"out": self.out, "qkv": self.qkv},
            outs,
            {"mixture": pltpu.VMEM(rows, LOW), "total": pltpu.VMEM(rows, WIDE)},
        )

    def backward(self, state, loss_grads, back_grad, pick):
        return self.run(
            "backward",
            [norm_back_part, feed_back_part, attend_back_part],
            [
                self.norm_back_set(state, loss_grads, back_grad),
                self.feed_back_set(state),
                ({"sum_one": state["sum_one"]}, {}, {}, {}),
                self.attend_back_set(state, ()),
            ],
            pick,
            cost=FULL_COST,
        )

    def norm_back(self, state, back_grad, pick):
        loads, weights, outs, scratch = self.norm_back_set(state, None, back_grad)
        outs |= {"total": (state["sum_two"].shape, WIDE)}
        return self.run("norm_back", [norm_back_part], [(loads, weights, outs, {})], pick)

    def feed_back(self, state, branch, total, pick):
        loads, weights, outs, scratch = self.feed_back_set(state)
        outs |= {"grad_one": (total.shape, WIDE)}
        loads = {"branch": branch} | loads
        return self.run(
            "feed_back",
            [feed_back_part],
            [(loads, weights, outs, {}), ({"total": total, "sum_one": state["sum_one"]}, {}, {}, {})],
            pick,
        )

    def attend_back(self, state, attended, grad_one, earlier, pick):
        return self.run(
            "attend_back",
            [attend_back_part],
            [self.attend_back_set(state, earlier)],
            pick,
            {"attended": attended, "grad_one": grad_one},
        )


def grid_of(count):
    dims = []
    while count % 2 == 0:
        dims.append(2)
        count //= 2
    return ([count] if count > 1 else []) + dims


def coordinates(dims, number):
    at = []
    for size in reversed(dims):
        at.append(number % size)
        number = number // size
    return at[::-1]


def shifted(value, dims, dim, steps):
    count = math.prod(dims)
    stride = math.prod(dims[dim + 1 :])
    pairs = []
    for source in range(count):
        place = (source // stride) % dims[dim]
        pairs.append((source, source + ((place + steps) % dims[dim] - place) * stride))
    return lax.ppermute(value, "dp", pairs)


def after(value, *earlier):
    return lax.optimization_barrier((value, *earlier))[0]


def stage(sends, earlier, beside=None):
    values = [after(value, *earlier) for value, _ in sends]
    backwards = list(zip(values, sends))[::-1]
    arrived = [permuted(value) for value, (_, permuted) in backwards][::-1]
    made = beside(earlier, arrived) if beside else []
    return list(lax.optimization_barrier((*arrived, *made)))[: len(sends)]


def step_along(dims, dim, steps):
    return lambda value: shifted(value, dims, dim, steps)


def rows_kernel(top, places, *refs):
    pieces, out, sems = refs[:-2], refs[-2], refs[-1]
    copies = []
    for group in pieces:
        for inner in range(group.shape[0]):
            number = len(copies)
            copies.append(
                pltpu.make_async_copy(
                    group.at[inner, pl.ds(top, out.shape[1])],
                    out.at[places[number]],
                    sems.at[number],
                )
            )
    for copy in copies:
        copy.start()
    for copy in copies:
        copy.wait()


def placed_rows(groups, places, top, rows):
    count, columns = places.shape[0], groups[0].shape[2]
    return pl.pallas_call(
        partial(rows_kernel, top),
        out_shape=jax.ShapeDtypeStruct((count, rows, columns), groups[0].dtype),
        in_specs=[pl.BlockSpec(memory_space=pltpu.SMEM)]
        + [pl.BlockSpec(memory_space=pl.ANY)] * len(groups),
        out_specs=pl.BlockSpec(memory_space=pltpu.VMEM),
        scratch_shapes=[pltpu.SemaphoreType.DMA((count,))],
        name="place",
    )(places, *groups)


def block_owners(order, dims, at):
    owners = jnp.zeros((1,), jnp.int32)
    for dim in order:
        steps = jnp.arange(dims[dim], dtype=jnp.int32)
        own = ((at[dim] - steps) % dims[dim]) * math.prod(dims[dim + 1 :])
        owners = (own[:, None] + owners[None, :]).reshape(-1)
    return owners


class Gather:
    def __init__(self, chunks, dims):
        self.dims, self.chunks = dims, chunks
        self.held = [[value[None]] for value, _, _ in chunks]
        self.arrived, self.step = [], 0

    def groups(self, number):
        _, order, start = self.chunks[number]
        while self.step < start + len(order):
            self.advance()
        return self.held[number]

    def advance(self, beside=None):
        sends, takers = [], []
        for number, (value, order, start) in enumerate(self.chunks):
            if start <= self.step < start + len(order):
                dim = order[self.step - start]
                for steps in range(1, self.dims[dim]):
                    for group in self.held[number]:
                        sends.append((group, step_along(self.dims, dim, steps)))
                        takers.append(number)
        self.arrived = stage(sends, self.arrived, beside)
        for number in sorted(set(takers)):
            value, order, start = self.chunks[number]
            got = [one for one, taker in zip(self.arrived, takers) if taker == number]
            held = self.held[number] + got
            blocks = sum(group.shape[0] for group in held)
            last = self.step - start >= len(order) - 2
            if not last or (blocks * value.size < 1 << 20 and self.step - start < len(order) - 1):
                held = [jnp.concatenate(held)]
            self.held[number] = held
        self.step += 1


def scatter_rows_plain(left, right, dims, dp_index):
    count = math.prod(dims)
    at = [
        (dp_index // math.prod(dims[dim + 1 :])) % dims[dim] for dim in range(len(dims))
    ]
    samples, height = left.shape
    rows, columns = height // count, right.shape[1]
    split = left.reshape(samples, count // 2, 2, rows)
    for_other = lax.dynamic_index_in_dim(split, 1 - at[-1], 2, False).reshape(samples, -1)
    for_self = lax.dynamic_index_in_dim(split, at[-1], 2, False).reshape(samples, -1)
    sent = product_tn(for_other, right).astype(jnp.bfloat16)
    total = product_tn(for_self, right) + shifted(sent, dims, len(dims) - 1, 1).astype(jnp.float32)
    for dim in reversed(range(len(dims) - 1)):
        low = total.astype(jnp.bfloat16).reshape(-1, dims[dim], rows, columns)
        total = lax.dynamic_index_in_dim(low, at[dim], 1, False).astype(jnp.float32)
        for steps in range(1, dims[dim]):
            part = lax.dynamic_index_in_dim(low, (at[dim] + steps) % dims[dim], 1, False)
            total = total + shifted(part, dims, dim, steps).astype(jnp.float32)
    return total.reshape(rows, columns)


def fetch_chosen(pick_ref, pair, place, target, sem):
    for wanted, ref in ((1, pair[0]), (0, pair[1])):

        @pl.when(pick_ref[0] == wanted)
        def _(ref=ref):
            pltpu.make_async_copy(ref.at[place], target, sem).start()

    return pltpu.make_async_copy(pair[0].at[place], target, sem)


def grad_kernel(pick_ref, *refs, rows, slots, outer, stride, start, other_start, sends):
    lefts, rights, refs = (refs[0:2], refs[2:4]), (refs[4:6], refs[6:8]), refs[8:]
    if not sends:
        other_ref, *refs = refs
    out_refs, refs = refs[: 1 if sends else slots], refs[1 if sends else slots :]
    if sends:
        left, right, out, left_sems, right_sems, out_sems = refs
    else:
        left, right, other, out, left_sems, right_sems, other_sems, out_sems = refs
    chips, width = outer * slots, right.shape[1]
    samples = lefts[0][0].shape[0]
    side = 1 - pick_ref[1] if sends else pick_ref[1]
    thin = rows % 128 != 0
    block = min(2 * BLOCK, width) if thin else width
    blocks = width // block
    wide_part = rights[0][0].shape[-1]

    def left_copies(number):
        if thin:
            place, target = (slice(None), slice(None)), slice(None)
        else:
            chip = number if sends else chip_of(number)
            place = (slice(None), pl.ds(pl.multiple_of((2 * chip + side) * rows, rows), rows))
            target = slice(number * rows, (number + 1) * rows)
        return [
            fetch_chosen(
                pick_ref,
                lefts[half],
                place,
                left.at[half * samples : (half + 1) * samples, target],
                left_sems.at[number, half],
            )
            for half in range(2)
        ]

    def right_copies(number):
        begin = start + number * block
        columns = pl.ds(begin % wide_part, block)
        place = (slice(None), columns)
        if len(rights[0][0].shape) == 3:
            place = (begin // wide_part, *place)
        at = slice(number * block, (number + 1) * block)
        return [
            fetch_chosen(
                pick_ref,
                rights[half],
                place,
                right.at[half * samples : (half + 1) * samples, at],
                right_sems.at[number, half],
            )
            for half in range(2)
        ]

    def chip_of(number):
        inner = number % outer
        first_chip = inner // stride * stride * slots + inner % stride
        return first_chip + stride * lax.rem(pick_ref[2] + number // outer, slots)

    def other_copy(number):
        if thin:
            return pltpu.make_async_copy(
                other_ref.at[pl.ds(0, chips * rows), pl.ds(other_start + number * block, block)],
                other.at[:, number * block : (number + 1) * block],
                other_sems.at[number],
            )
        return pltpu.make_async_copy(
            other_ref.at[
                pl.ds(pl.multiple_of(chip_of(number) * rows, rows), rows), pl.ds(other_start, width)
            ],
            other.at[number * rows : (number + 1) * rows],
            other_sems.at[number],
        )

    def wait(copies):
        for copy in copies:
            copy.wait()

    leaving = []
    if thin:
        halves_of_left = left_copies(0)
        arriving = [right_copies(number) for number in range(blocks)]
        if not sends:
            others = [other_copy(number) for number in range(blocks)]
            for copy in others:
                copy.start()
        wait(halves_of_left)
        flipped = left[...].T
        turned = jnp.concatenate(
            [
                jnp.where(
                    side == 0,
                    flipped[2 * rows * chip : 2 * rows * chip + rows],
                    flipped[2 * rows * chip + rows : 2 * rows * (chip + 1)],
                )
                for chip in range(chips)
            ]
        )
        for number in range(blocks):
            at = slice(number * block, (number + 1) * block)
            wait(arriving[number])
            result = product(turned, right[:, at])
            if sends:
                out[:, at] = result.astype(LOW)
                leaving.append(
                    pltpu.make_async_copy(out.at[:, at], out_refs[0].at[:, at], out_sems.at[number])
                )
                leaving[-1].start()
                continue
            others[number].wait()
            out[:, at] = (result + other[:, at].astype(WIDE)).astype(LOW)
            for place in range(chips):
                leaving.append(
                    pltpu.make_async_copy(
                        out.at[pl.ds(pl.multiple_of(chip_of(place) * rows, rows), rows), at],
                        out_refs[place // outer].at[place % outer, :, at],
                        out_sems.at[number * chips + place],
                    )
                )
                leaving[-1].start()
    else:
        arriving = right_copies(0)
        pieces = [left_copies(number) for number in range(chips)]
        if not sends:
            others = [other_copy(number) for number in range(chips)]
            for copy in others:
                copy.start()
        wait(arriving)
        for number in range(chips):
            at = slice(number * rows, (number + 1) * rows)
            wait(pieces[number])
            result = product_tn(left[:, at], right[...])
            if sends:
                out[at] = result.astype(LOW)
                target = out_refs[0].at[at]
            else:
                others[number].wait()
                out[at] = (result + other[at].astype(WIDE)).astype(LOW)
                target = out_refs[number // outer].at[number % outer]
            leaving.append(pltpu.make_async_copy(out.at[at], target, out_sems.at[number]))
            leaving[-1].start()
    wait(leaving)


def fold_kernel(pick_ref, held_ref, other_ref, out_ref, *send_refs, slots, stride):
    for slot in range(slots):
        place = lax.rem(pick_ref[0] + slot, slots)
        for number in range(out_ref.shape[0]):
            index = number // stride * stride * slots + number % stride + place * stride
            value = held_ref[index].astype(WIDE) + other_ref[index].astype(WIDE)
            if slot == 0:
                out_ref[number] = value
                continue
            send_refs[slot - 1][number] = value.astype(LOW)


def slots_of(value, slots, stride):
    return value.reshape(-1, slots, stride, *value.shape[1:])


class Scatter:
    def __init__(self, name, lefts, rights, dims, at, dim, first):
        self.name, self.lefts, self.rights, self.dims, self.at = name, lefts, rights, dims, at
        self.count = math.prod(dims)
        self.height = lefts[0][0].shape[1]
        self.rows = self.height // self.count
        sample = rights[0][0]
        self.columns = sample.shape[-1] * (3 if sample.ndim == 3 else 1)
        self.slots, self.stride = dims[dim], math.prod(dims[dim + 1 : -1])
        self.place = at[dim]
        self.pick = jnp.stack([first, at[-1], self.place])

    def product(self, start, width, other, other_start, cost, earlier=()):
        samples = self.lefts[0][0].shape[0]
        half, rows, slots = self.height // 2, self.rows, self.slots
        chips = self.count // 2
        outer = chips // slots
        sends = other is None
        thin = rows % 128 != 0
        blocks = width // min(2 * BLOCK, width) if thin else 1
        pieces = 1 if thin else chips
        anywhere = pl.BlockSpec(memory_space=pl.ANY)
        args = [*self.lefts[0], *self.lefts[1], *self.rights[0], *self.rights[1]]
        args += [] if sends else [other]
        out_sems = blocks * (1 if sends else chips) if thin else chips
        other_scratch = [] if sends else [pltpu.VMEM((half, width), LOW)]
        other_sems = [] if sends else [pltpu.SemaphoreType.DMA((blocks if thin else chips,))]
        outs = [(half, width)] if sends else [(outer, rows, width)] * slots
        scratch = [
            pltpu.VMEM((2 * samples, self.height if thin else half), LOW),
            pltpu.VMEM((2 * samples, width), LOW),
            *other_scratch,
            pltpu.VMEM((half, width), LOW),
        ]
        return pl.pallas_call(
            partial(
                grad_kernel,
                rows=rows,
                slots=slots,
                outer=outer,
                stride=self.stride,
                start=start,
                other_start=other_start,
                sends=sends,
            ),
            in_specs=[pl.BlockSpec(memory_space=pltpu.SMEM)] + [anywhere] * len(args),
            out_specs=[anywhere] * len(outs),
            out_shape=[jax.ShapeDtypeStruct(out, LOW) for out in outs],
            scratch_shapes=[
                *scratch,
                pltpu.SemaphoreType.DMA((pieces, 2)),
                pltpu.SemaphoreType.DMA((blocks, 2)),
                *other_sems,
                pltpu.SemaphoreType.DMA((out_sems,)),
            ],
            compiler_params=pltpu.CompilerParams(vmem_limit_bytes=VMEM_LIMIT),
            cost_estimate=cost,
            name=self.name + ("_send" if sends else "_keep"),
        )(after(self.pick, *earlier), *(in_hbm(array) for array in args))

    def make(self, cost, earlier=(), start=0, width=None):
        self.sent = self.product(start, width or self.columns, None, 0, cost, earlier)[0]
        self.other_from = start
        return self.sent

    def keep(self, start, width, cost, earlier=()):
        return self.product(start, width, self.other, start - self.other_from, cost, earlier)


def own_kernel(where_ref, vectors_ref, *out_refs, spans):
    width = vectors_ref.shape[1]
    for (first_row, rows, length), out_ref in zip(spans, out_refs):
        start = where_ref[0] * length
        if rows > 1 and width % length == 0:
            line = vectors_ref[pl.ds(first_row + start // width, 1)]
        else:
            line = jnp.concatenate(
                [vectors_ref[first_row + row : first_row + row + 1] for row in range(rows)], axis=1
            )
        turns = lax.rem(line.shape[1] - lax.rem(start, line.shape[1]), line.shape[1])
        line = pltpu.roll(jnp.broadcast_to(line, (8, line.shape[1])), turns, 1)
        out_ref[...] = line[0:1, :length]


def own_parts(vectors, spans, dp_index):
    return pl.pallas_call(
        partial(own_kernel, spans=spans),
        in_specs=[
            pl.BlockSpec(memory_space=pltpu.SMEM),
            pl.BlockSpec(memory_space=pltpu.VMEM),
        ],
        out_specs=[pl.BlockSpec(memory_space=pltpu.VMEM)] * len(spans),
        out_shape=[jax.ShapeDtypeStruct((1, length), WIDE) for _, _, length in spans],
        name="own_parts",
    )(dp_index[None], vectors)


class Whole:
    def __init__(self, value):
        self.value = value

    def outgoing(self, dim):
        return self.value

    def take(self, arrived):
        self.value = self.value + arrived


class Halved:
    def __init__(self, value, dims, at):
        self.value, self.dims, self.at = value, dims, at

    def outgoing(self, dim):
        split = self.value.reshape(-1, self.dims[dim], *self.value.shape[1:])
        self.kept = lax.dynamic_index_in_dim(split, self.at[dim], 1, False)
        return lax.dynamic_index_in_dim(split, 1 - self.at[dim], 1, False)

    def take(self, arrived):
        self.value = self.kept + arrived


def folded(held, moved, slots, stride, place):
    outer, rows, columns = held.shape
    if rows % 16 == 0 and len(moved) == 1:
        whole = pl.BlockSpec(memory_space=pltpu.VMEM)
        shape = (outer // slots, rows, columns)
        total, *sends = pl.pallas_call(
            partial(fold_kernel, slots=slots, stride=stride),
            out_shape=[jax.ShapeDtypeStruct(shape, WIDE)]
            + [jax.ShapeDtypeStruct(shape, LOW)] * (slots - 1),
            in_specs=[pl.BlockSpec(memory_space=pltpu.SMEM), whole, whole],
            out_specs=[whole] * slots,
            compiler_params=pltpu.CompilerParams(vmem_limit_bytes=24 << 20),
            cost_estimate=NO_COST,
            name="fold",
        )(place[None], held, moved[0])
        return total, sends
    total = held.astype(WIDE)
    for piece in moved:
        total = total + piece.astype(WIDE)
    split = slots_of(total, slots, stride)
    blocks = [
        lax.dynamic_index_in_dim(split, (place + steps) % slots, 1, False).reshape(-1, rows, columns)
        for steps in range(slots)
    ]
    return blocks[0], [block.astype(LOW) for block in blocks[1:]]


def travels(pieces, chunks, order, dims, at, cores, riders, during):
    held, sends, sums = {}, {}, {}
    arrived, riding = [], []
    ways = list(reversed(range(len(dims))))
    for step in range(chunks + len(order) - 1):
        if step < chunks:
            held[step], *sends[step] = pieces[step]
        if step in riders:
            riding += [(rider, step) for rider in riders[step]()]
        outgoing, takers = [], []
        for phase, dim in enumerate(order):
            number = step - phase
            if 0 <= number < chunks:
                outgoing += [
                    (value, step_along(dims, dim, k)) for k, value in enumerate(sends[number], start=1)
                ]
                takers += [number] * len(sends[number])
        exchanging = cores.get(step, lambda: [])()
        outgoing += [(weight.sent, step_along(dims, ways[0], 1)) for weight in exchanging]
        along = [(rider, ways[step - start]) for rider, start in riding if step - start < len(ways)]
        outgoing += [(rider.outgoing(dim), step_along(dims, dim, 1)) for rider, dim in along]

        def beside(earlier, arriving):
            for weight, half in zip(exchanging, arriving[len(takers) :]):
                weight.other = half
            return during[step](earlier) if step < len(during) else []

        arrived = stage(outgoing, arrived, beside)
        for (rider, _), part in zip(along, arrived[len(takers) + len(exchanging) :]):
            rider.take(part)
        arrived = arrived[: len(takers)]
        for phase, dim in enumerate(order):
            number = step - phase
            if not 0 <= number < chunks:
                continue
            moved = [value for value, taker in zip(arrived, takers) if taker == number]
            left = order[phase + 1 :]
            if left:
                stride = math.prod(dims[other] for other in left if other > left[0])
                held[number], sends[number] = folded(
                    held[number], moved, dims[left[0]], stride, at[left[0]]
                )
            else:
                total = held[number].astype(WIDE)
                for piece in moved:
                    total = total + piece.astype(WIDE)
                sums[number] = total.reshape(total.shape[-2:])
    return [sums[number] for number in range(chunks)]


def spread(value, count):
    return lax.all_to_all(
        jnp.broadcast_to(value[None], (count, *value.shape)), "dp", 0, 0, tiled=True
    )


def summed(parts):
    return jnp.sum(lax.all_to_all(parts, "dp", 0, 0, tiled=True).astype(jnp.float32), axis=0)


def halves(value):
    high = value.astype(jnp.bfloat16)
    return high, (value - high.astype(jnp.float32)).astype(jnp.bfloat16)


def exact_product(left_side, right_side):
    high, low = halves(right_side)
    return product(left_side, high) + product(left_side, low)


def product_by_ones(left_side, right_side):
    high, low = halves(left_side)
    return product(high, right_side) + product(low, right_side)


def prefix_masks(length):
    places = lax.broadcasted_iota(jnp.int32, (1, length), 1)
    return [places < width for width in PREFIXES]


def similar_parts(documents, queries_t):
    docs_f32 = documents.astype(jnp.float32)
    squares = docs_f32 * docs_f32
    query_squares = queries_t * queries_t
    queries_low = queries_t.astype(jnp.bfloat16)
    parts = []
    for width, mask in zip(PREFIXES, prefix_masks(PROJ)):
        cut = jnp.where(mask, docs_f32, 0.0)
        doc_scale = lax.rsqrt(
            jnp.sum(jnp.where(mask, squares, 0.0), axis=1, keepdims=True) + unit_eps
        )
        query_scale = lax.rsqrt(
            jnp.sum(query_squares[:width], axis=0, keepdims=True) + unit_eps
        )
        cut = cut.astype(jnp.bfloat16)
        similar = product(cut, queries_low) * doc_scale * query_scale
        parts.append((cut, doc_scale, query_scale, similar))
    return parts


def members_of(ends_ref, micro_step, by_row):
    shape = (DOC_ROWS, 8) if by_row else (8, DOC_ROWS)
    rows = lax.broadcasted_iota(jnp.int32, shape, 0 if by_row else 1)
    docs = lax.broadcasted_iota(jnp.int32, shape, 1 if by_row else 0)
    inside = jnp.zeros(shape, jnp.float32)
    for number in range(DOCS_DEV):
        begin = ends_ref[micro_step, number - 1] if number else 0
        held = (docs == number) & (rows >= begin) & (rows < ends_ref[micro_step, number])
        inside = jnp.where(held, 1.0, inside)
    return inside.astype(jnp.bfloat16)


def query_of_token(tokens, by_token):
    shape = (tokens, 128) if by_token else (128, tokens)
    token = lax.broadcasted_iota(jnp.int32, shape, 0 if by_token else 1)
    query = lax.broadcasted_iota(jnp.int32, shape, 1 if by_token else 0)
    held = (token >= query * QLEN) & (token < query * QLEN + QLEN)
    return jnp.where(held, 1.0, 0.0).astype(jnp.bfloat16)


def score_kernel(ends_ref, queries_ref, docs_ref, out_ref, *, micro_step):
    tokens = queries_ref.shape[0] * queries_ref.shape[1]
    queries_t = queries_ref[...].astype(WIDE).reshape(tokens, PROJ).T
    members = members_of(ends_ref, micro_step, False)
    by_query = query_of_token(tokens, True)
    for number, (_, _, _, similar) in enumerate(similar_parts(docs_ref[:DOC_ROWS], queries_t)):
        masses = exact_product(members, jnp.exp(sharpness * similar))
        held = lax.broadcasted_iota(jnp.int32, masses.shape, 0) < DOCS_DEV
        logs = jnp.log(jnp.where(held, masses, 1.0))
        out_ref[0, number] = product_by_ones(logs, by_query) / sharpness


def loss_kernel(
    ends_ref, where_ref, queries_ref, docs_ref, tables_ref, times_ref, first_ref,
    loss_ref, grad_queries_ref, grad_docs_ref, table, *, micro_step
):
    step = pl.program_id(0)
    devices, width = queries_ref.shape[:2]
    tokens = devices * width
    queries_t = queries_ref[...].astype(WIDE).reshape(tokens, PROJ).T
    queries_low = queries_t.astype(LOW)
    members = members_of(ends_ref, micro_step, False)
    members_by_row = members_of(ends_ref, micro_step, True)
    spread_out = query_of_token(tokens, False)
    places = lax.broadcasted_iota(jnp.int32, (PROJ, 1), 0)
    grad_queries = jnp.zeros((PROJ, tokens), WIDE)
    grad_docs = jnp.zeros((DOC_ROWS, PROJ), WIDE)
    losses = jnp.zeros((1, 128), WIDE)
    times, first = times_ref[0], first_ref[0]
    own_rows = pl.ds(pl.multiple_of(where_ref[0] * 8, 8), 8)
    own_times, own_first = times_ref[0, own_rows], first_ref[0, own_rows]
    table[...] = jnp.zeros_like(table)
    for number, (cut, doc_scale, query_scale, similar) in enumerate(
        similar_parts(docs_ref[:DOC_ROWS], queries_t)
    ):
        for device in range(table.shape[0] // 8):
            table[8 * device : 8 * device + DOCS_DEV] = tables_ref[device, 0, number]
        scores = table[...]
        top = jnp.max(jnp.where(times > 0, scores, -1e30), axis=0, keepdims=True)
        top = jnp.where(top > -1e29, top, 0.0)
        normal = top + jnp.log(
            jnp.maximum(
                jnp.sum(times * jnp.exp(jnp.minimum(scores - top, 0.0)), axis=0, keepdims=True),
                1e-30,
            )
        )
        losses = losses + normal - jnp.sum(first * scores, axis=0, keepdims=True)
        own = table[own_rows]
        grad_score = own_times * jnp.exp(jnp.where(own_times > 0, own - normal, 0.0)) - own_first
        weights = jnp.exp(sharpness * similar)
        masses = exact_product(members, weights)
        by_token = product_by_ones(grad_score, spread_out)
        held = lax.broadcasted_iota(jnp.int32, masses.shape, 0) < DOCS_DEV
        by_token = jnp.where(held, by_token / jnp.where(held, masses, 1.0), 0.0)
        grad_similar = weights * exact_product(members_by_row, by_token)
        along = grad_similar * similar
        pulled = (grad_similar * doc_scale * query_scale).astype(LOW)
        mask = lax.broadcasted_iota(jnp.int32, (1, PROJ), 1) < PREFIXES[number]
        grad_docs = (
            grad_docs
            + jnp.where(mask, product_nt(pulled, queries_low), 0.0)
            - cut.astype(WIDE) * (doc_scale * doc_scale * jnp.sum(along, axis=1, keepdims=True))
        )
        toward = product_tn(cut, pulled)
        back = queries_t * (query_scale * query_scale * jnp.sum(along, axis=0, keepdims=True))
        grad_queries = grad_queries + toward - jnp.where(places < PREFIXES[number], back, 0.0)
    loss_ref[0] = losses
    grad_queries_ref[...] = grad_queries.T.reshape(devices, width, PROJ).astype(LOW)

    @pl.when(step == 0)
    def _():
        grad_docs_ref[...] = grad_docs

    @pl.when(step > 0)
    def _():
        grad_docs_ref[...] += grad_docs


class Loss:
    def __init__(self, micro_step, ends, pair_rows, dp_index, count):
        self.micro_step, self.ends, self.dp_index, self.count = micro_step, ends, dp_index, count
        self.group = math.gcd(count, 16)
        self.steps = count // self.group
        place = jnp.arange(8 * count, dtype=jnp.int32)
        doc_ids = jnp.where(place % 8 < DOCS_DEV, place // 8 * DOCS_DEV + place % 8, -1)
        picked = (pair_rows[None, :, :] == doc_ids[:, None, None]).astype(WIDE)
        self.times, self.first = [
            jnp.pad(
                jnp.swapaxes(value.reshape(8 * count, self.steps, -1), 0, 1),
                [(0, 0), (0, 0), (0, 128 - self.group * QRY_DEV)],
            )
            for value in (jnp.sum(picked, axis=2), picked[..., 0])
        ]
        self.params = dict(
            grid=(self.steps,), compiler_params=pltpu.CompilerParams(vmem_limit_bytes=40 << 20)
        )
        self.queries_spec = pl.BlockSpec((self.group, QRY_DEV * QLEN, PROJ), lambda i: (i, 0, 0))
        self.smem = pl.BlockSpec(memory_space=pltpu.SMEM)

    def scores(self, embedded):
        self.embedded = embedded
        self.queries = spread(embedded[DOC_ROWS:], self.count)
        return pl.pallas_call(
            partial(score_kernel, micro_step=self.micro_step),
            out_shape=jax.ShapeDtypeStruct((self.steps, 3, 8, 128), WIDE),
            in_specs=[
                self.smem,
                self.queries_spec,
                pl.BlockSpec((ROWS, PROJ), lambda i: (0, 0)),
            ],
            out_specs=pl.BlockSpec((1, 3, 8, 128), lambda i: (i, 0, 0, 0)),
            name="scores",
            cost_estimate=NO_COST,
            **self.params,
        )(self.ends, self.queries, embedded)[:, :, :DOCS_DEV]

    def grads(self, tables, *earlier):
        losses, grad_queries, grad_docs = pl.pallas_call(
            partial(loss_kernel, micro_step=self.micro_step),
            out_shape=(
                jax.ShapeDtypeStruct((self.steps, 1, 128), WIDE),
                jax.ShapeDtypeStruct(self.queries.shape, LOW),
                jax.ShapeDtypeStruct((DOC_ROWS, PROJ), WIDE),
            ),
            in_specs=[
                self.smem,
                self.smem,
                self.queries_spec,
                pl.BlockSpec((ROWS, PROJ), lambda i: (0, 0)),
                pl.BlockSpec((self.count, 1, 3, DOCS_DEV, 128), lambda i: (0, i, 0, 0, 0)),
                pl.BlockSpec((1, 8 * self.count, 128), lambda i: (i, 0, 0)),
                pl.BlockSpec((1, 8 * self.count, 128), lambda i: (i, 0, 0)),
            ],
            out_specs=(
                pl.BlockSpec((1, 1, 128), lambda i: (i, 0, 0)),
                self.queries_spec,
                pl.BlockSpec((DOC_ROWS, PROJ), lambda i: (0, 0)),
            ),
            scratch_shapes=[pltpu.VMEM((8 * self.count, 128), WIDE)],
            name="losses",
            cost_estimate=NO_COST,
            **self.params,
        )(
            self.ends,
            self.dp_index[None],
            self.queries,
            after(self.embedded, *earlier),
            tables,
            self.times,
            self.first,
        )
        losses = losses[:, 0, : self.group * QRY_DEV].reshape(self.count * QRY_DEV)
        own = lax.dynamic_slice_in_dim(losses, self.dp_index * QRY_DEV, QRY_DEV, 0)
        return own, grad_queries, grad_docs


def shards(
    tokens,
    qkv_weight,
    qkv_bias,
    out_weight,
    out_bias,
    norm1_gain,
    norm1_bias,
    up_weight,
    up_bias,
    down_weight,
    down_bias,
    norm2_gain,
    norm2_bias,
    proj_weight,
    doc_lengths,
    pair_docs,
):
    section_index = lax.axis_index("section")
    dp_index = lax.axis_index("dp")
    count = lax.axis_size("dp")
    dims = grid_of(count)
    at = coordinates(dims, dp_index)
    is_first = section_index == 0
    first = is_first.astype(jnp.int32)
    width, hidden = tokens.shape[1], up_weight.shape[2]
    own_height = width // count
    by_hand = own_height % 16 == 0

    segments, positions = [
        jnp.stack(value)
        for value in zip(*(doc_layout(doc_lengths[micro_step]) for micro_step in range(MICRO)))
    ]
    by_row = jnp.broadcast_to(segments[:, :, None], (MICRO, ROWS, ROWS // 2))
    layout = (*rotary(positions), by_row, segments[:, None, :])
    picks = [jnp.stack([first, jnp.int32(micro_step)]) for micro_step in range(MICRO)]
    own_rows = [tokens[micro_step * ROWS : (micro_step + 1) * ROWS] for micro_step in range(MICRO)]
    ends = jnp.cumsum(doc_lengths, axis=1)
    pair_rows = pair_docs.reshape(count, MICRO, QRY_DEV, CANDS)
    losses_of = [
        Loss(
            micro_step,
            ends,
            pair_rows[:, micro_step].reshape(count * QRY_DEV, CANDS),
            dp_index,
            count,
        )
        for micro_step in range(MICRO)
    ]

    vectors = (
        qkv_bias,
        out_bias,
        norm1_gain,
        norm1_bias,
        up_bias,
        down_bias,
        norm2_gain,
        norm2_bias,
    )
    lengths = [value.shape[1] for value in vectors]
    short = sum(lengths)
    shards_of = [out_weight[0], qkv_weight[0], up_weight[0], down_weight[0]]

    fetched = (width, width, hidden // 4, width // 2)

    def small_parameters(layer, rows, projection):
        cuts, start = [], 0
        for length in lengths:
            cuts.append(rows[:, start : start + length].astype(WIDE).reshape(-1))
            start += length
        qkv_b, out_b, gain_one, bias_one, up_b, down_b, gain_two, bias_two = cuts
        layer.qkv_bias = qkv_b.reshape(3, width)
        layer.up_bias = up_b[None]
        layer.small = jnp.concatenate(
            [
                jnp.stack([out_b, gain_one, bias_one, down_b, gain_two, bias_two]),
                jnp.zeros((2, width), WIDE),
            ]
        )
        return projection.reshape(width, -1)

    if by_hand:
        line = jnp.concatenate([*vectors, jnp.zeros((1, width - short), LOW)], axis=1)
        proj_lines = proj_weight.reshape(-1, width)
        filler = jnp.zeros((15 - proj_lines.shape[0], width), LOW)
        order = list(range(len(dims)))
        chunks = [(jnp.concatenate([shards_of[0], line, proj_lines, filler]), order, 0)]
        cuts_of = ([1], [1, 2], [2, 2], [2, 2])
        for number in (1, 2, 3):
            parts, shard = cuts_of[number], shards_of[number]
            unit, start = shard.shape[1] // sum(parts), 0
            for part in parts:
                value = lax.slice_in_dim(shard, start, start + part * unit, axis=1)
                chunks.append((value, order, len(chunks)))
                start += part * unit
        gather = Gather(chunks, dims)
        layer = Layer(block_owners(order, dims, at), layout)

        def whole(number, first_chunk):
            parts, start = [], 0
            unit = shards_of[number].shape[1] // sum(cuts_of[number])
            for offset, part in enumerate(cuts_of[number]):
                parts.append((start, part * unit, gather.groups(first_chunk + offset)))
                start += part * unit
            return Weight(count, shards_of[number].shape[0], start, fetched[number], parts)

        layer.out = whole(0, 0)
        block = placed_rows(layer.out.arrays, layer.places, own_height, 16)
        projection = small_parameters(
            layer, block[:, 0], block[:, 1 : 1 + proj_lines.shape[0]]
        )
        layer.qkv = whole(1, 1)
        states = []

        def attend_beside(micro_step):
            def beside(earlier, arriving):
                rows = after(own_rows[micro_step], *earlier)
                states.append(layer.attend(rows, picks[micro_step]))
                return [states[-1]["norm"]]

            return beside

        def up_beside(earlier, arriving):
            for state, pick in zip(states, picks):
                state |= layer.rise(after(state["norm"], *earlier), pick)
            return [state["active"] for state in states]

        gather.advance(attend_beside(0))
        gather.advance(attend_beside(1))
        layer.up = whole(2, 3)
        gather.advance(up_beside)
        gather.advance()
        layer.down = whole(3, 5)
    else:
        layer = Layer(jnp.zeros((1,), jnp.int32), layout)
        wholes = [
            lax.all_gather(value, "dp", axis=0, tiled=True)[None] for value in shards_of
        ]
        layer.out, layer.qkv, layer.up, layer.down = [
            Weight(1, *value.shape[1:], columns, [(0, value.shape[2], [value])])
            for value, columns in zip(wholes, fetched)
        ]
        together = spread(jnp.concatenate([*vectors, proj_weight.reshape(1, -1)], axis=1)[0], count)
        projection = small_parameters(layer, together[:, :short], together[:, short:])
        states = [layer.attend(rows, pick) for rows, pick in zip(own_rows, picks)]
        for state, pick in zip(states, picks):
            state |= layer.rise(state["norm"], pick)

    arrived = []
    for state, pick in zip(states, picks):
        active = after(state["active"], *(one["result"] for one in states if "result" in one))
        state |= layer.fall(active, state["norm"], pick)
        arrived.append(from_behind(state["result"], "section", 1))
    own_scores = []
    for micro_step in range(MICRO):
        last = micro_step == MICRO - 1
        states.append(
            layer.forward(
                arrived[micro_step],
                picks[micro_step],
                projection,
                [state["result"] for state in states] if last else (),
            )
        )
        own_scores.append(losses_of[micro_step].scores(states[-1]["embedded"]))
    activations = states[-1]["activations"][None]

    tables = spread(jnp.stack(own_scores), count)
    own_losses, loss_grads = [None] * MICRO, [None] * MICRO
    earlier = []
    for micro_step in reversed(range(MICRO)):
        own_losses[micro_step], grad_queries, grad_docs = losses_of[micro_step].grads(
            tables[:, micro_step], *earlier
        )
        earlier = [grad_queries]
        loss_grads[micro_step] = (
            grad_docs,
            lax.all_to_all(grad_queries, "dp", 0, 0, tiled=True),
            projection,
        )
    own_losses = jnp.concatenate(own_losses)
    query_losses = jnp.where(is_first, from_behind(own_losses, "section", -1), own_losses)
    loss_grads[0] = (after(loss_grads[0][0], query_losses), *loss_grads[0][1:])

    back, back_grads = [], []
    for micro_step in reversed(range(MICRO)):
        back.append(
            layer.backward(states[MICRO + micro_step], loss_grads[micro_step], None, picks[micro_step])
        )
        back_grads.append(from_behind(back[-1]["grad_low"], "section", -1))
    back.append(layer.backward(states[1], None, back_grads[0], picks[1]))
    back_grad = after(back_grads[1], back[-1]["mixed"])
    grads = layer.norm_back(states[0], back_grad, picks[0])
    vectors_of = [one["vectors"] for one in (*back, grads)]

    def pairs(values):
        return [values[1], values[3]], [values[0], values[2]]

    lefts = [
        pairs([state[name] for state in states]) for name in ("active", "norm", "mixture")
    ] + [pairs([*own_rows, *arrived])]

    def rights_of(name):
        return pairs([grads[name], *(back[number][name] for number in (2, 1, 0))])

    def feed_back(*earlier):
        grads.update(
            layer.feed_back(states[0], after(grads["branch"], *earlier), grads["total"], picks[0])
        )

    def attend_back(*earlier):
        grads.update(
            layer.attend_back(
                states[0],
                after(grads["attended"], *earlier),
                grads["grad_one"],
                [one["grad_source"] for one in back],
                picks[0],
            )
        )

    if by_hand:
        last_dim = len(dims) - 2
        weights = {}

        def weight_of(name, number, right):
            weights[name] = Scatter(
                name, lefts[number], rights_of(right), dims, at, last_dim, first
            )
            return weights[name]

        half = width // 2
        downs = [weight_of("down", 0, "branch") for _ in range(2)]
        for number, (weight, earlier) in enumerate(zip(downs, ([], [downs[0]]))):
            weight.make(NO_COST, [one.sent for one in earlier], number * half, half)
            weight.other = shifted(weight.sent, dims, len(dims) - 1, 1)
        pieces = {0: downs[0].keep(0, half, NO_COST, [downs[1].sent])}

        def first_stage(earlier):
            feed_back(*pieces[0])
            vectors_of.append(grads["vectors"])
            sent = weight_of("up", 1, "gate").make(NO_COST)
            pieces[1] = downs[1].keep(half, half, NO_COST, [sent])
            return pieces[1]

        def second_stage(earlier):
            attend_back(*earlier)
            vectors_of.append(grads["vectors"])
            pieces[2] = weights["up"].keep(0, hidden // 2, NO_COST, [grads["mixed"]])
            return pieces[2]

        def third_stage(earlier):
            sent = weight_of("qkv", 3, "mixed").make(NO_COST, earlier)
            sent = weight_of("out", 2, "attended").make(NO_COST, [sent])
            pieces[3] = weights["up"].keep(hidden // 2, hidden // 2, NO_COST, [sent])
            return pieces[3]

        def fourth_stage(earlier):
            pieces[4] = weights["qkv"].keep(0, 2 * width, NO_COST, earlier)
            pieces[5] = weights["qkv"].keep(2 * width, width, NO_COST, pieces[4])
            return pieces[5]

        def fifth_stage(earlier):
            pieces[6] = weights["out"].keep(0, width, NO_COST, earlier)
            return pieces[6]

        def projection_grad():
            total = product_tn(
                jnp.concatenate([state["result"] for state in states[:1:-1]]),
                jnp.concatenate([one["grad_embedded"] for one in back[:MICRO]]),
            ) * section_index.astype(WIDE)
            parts = jnp.swapaxes(total.reshape(2, count, -1, total.shape[1]), 0, 1)
            riding.append(Halved(parts, dims, at))
            return riding[-1]

        def vector_grads():
            riding.append(Whole(sum(vectors_of)))
            return riding[-1]

        riding = []
        sums = travels(
            pieces,
            7,
            list(reversed(range(last_dim + 1))),
            dims,
            at,
            {
                1: lambda: [weights["up"]],
                3: lambda: [weights["qkv"], weights["out"]],
            },
            {4: lambda: [projection_grad(), vector_grads()]},
            [first_stage, second_stage, third_stage, fourth_stage, fifth_stage],
        )
        proj_own, own_vectors = riding[0].value[0], riding[1].value
        grad_down, grad_up, grad_qkv = (
            jnp.concatenate(group, axis=1)[None] for group in (sums[0:2], sums[2:4], sums[4:6])
        )
        grad_out = sums[6][None]
    else:
        feed_back()
        vectors_of.append(grads["vectors"])
        attend_back()
        weight_grads = []
        for number, name in enumerate(("branch", "gate", "attended", "mixed")):
            left = jnp.concatenate([jnp.where(is_first, *pair) for pair in lefts[number]])
            right = [jnp.where(is_first, *pair) for pair in rights_of(name)]
            if number == 3:
                right = [jnp.swapaxes(value, 0, 1).reshape(ROWS, -1) for value in right]
            weight_grads.append(
                scatter_rows_plain(left, jnp.concatenate(right), dims, dp_index)[None]
            )
        grad_down, grad_up, grad_out, grad_qkv = weight_grads
        own_vectors = lax.psum(sum([*vectors_of, grads["vectors"]]), "dp")
        proj_total = product_tn(
            jnp.concatenate([state["result"] for state in states[:1:-1]]),
            jnp.concatenate([one["grad_embedded"] for one in back[:MICRO]]),
        ) * section_index.astype(WIDE)
        proj_own = summed(jnp.swapaxes(proj_total.reshape(2, count, -1, PROJ), 0, 1))
    grad_inputs = grads["grad_source"]
    proj_grad = jnp.where(is_first, from_behind(proj_own[0], "section", -1), proj_own[1])
    grad_qkv_b, grad_out_b, grad_gain1, grad_bias1, grad_up_b, grad_down_b, grad_gain2, grad_bias2 = (
        own_parts(
            own_vectors,
            [
                (first_row, rows, rows * width // count)
                for first_row, rows in (
                    (0, 3), (3, 1), (4, 1), (5, 1), (6, hidden // width), (10, 1), (11, 1), (12, 1)
                )
            ],
            dp_index,
        )
    )
    return (
        query_losses,
        activations,
        grad_inputs[None],
        grad_qkv,
        grad_qkv_b,
        grad_out,
        grad_out_b,
        grad_gain1,
        grad_bias1,
        grad_up,
        grad_up_b,
        grad_down,
        grad_down_b,
        grad_gain2,
        grad_bias2,
        proj_grad,
    )


def solution(mesh):
    in_specs = (
        P("dp", None),
        P("section", "dp", None),
        P("section", "dp"),
        P("section", "dp", None),
        P("section", "dp"),
        P("section", "dp"),
        P("section", "dp"),
        P("section", "dp", None),
        P("section", "dp"),
        P("section", "dp", None),
        P("section", "dp"),
        P("section", "dp"),
        P("section", "dp"),
        P("dp", None),
        P("dp", None),
        P(),
    )
    out_specs = (
        P("dp"),
        P("section", "dp", None),
        P("section", "dp", None),
        P("section", "dp", None),
        P("section", "dp"),
        P("section", "dp", None),
        P("section", "dp"),
        P("section", "dp"),
        P("section", "dp"),
        P("section", "dp", None),
        P("section", "dp"),
        P("section", "dp", None),
        P("section", "dp"),
        P("section", "dp"),
        P("section", "dp"),
        P(("section", "dp"), None),
    )
    return jax.shard_map(shards, mesh=mesh, in_specs=in_specs, out_specs=out_specs, check_vma=False)
```

```python
from functools import partial
import math

import jax
import jax.numpy as jnp
from jax import lax
from jax.experimental import pallas as pl
from jax.experimental.pallas import tpu as pltpu
from jax.sharding import PartitionSpec as P

HEAD = 64
PROJ = 128
QLEN = 32
DOC_ROWS = 192
QRY_DEV = 2
DOCS_DEV = 3
MICRO = 2
CANDS = 8
ROWS = 256
PREFIXES = (PROJ // 2, 3 * PROJ // 4, PROJ)


norm_eps = 1e-05
unit_eps = 1e-06
sharpness = 20.0
score_scale = 0.125
masked_score = -1000000000.0


def from_behind(value, axis, steps):
    count = lax.axis_size(axis)
    first, last = (max(0, -steps), min(count, count - steps))
    return lax.ppermute(value, axis, [(source, source + steps) for source in range(first, last)])


def product(left_side, right_side):
    return jnp.dot(left_side, right_side, preferred_element_type=jnp.float32)


def product_tn(left_side, right_side):
    return lax.dot_general(
        left_side, right_side, (((0,), (0,)), ((), ())), preferred_element_type=jnp.float32
    )


def product_nt(left_side, right_side):
    return lax.dot_general(
        left_side, right_side, (((1,), (1,)), ((), ())), preferred_element_type=jnp.float32
    )


def doc_layout(doc_lens):
    row_ids = jnp.arange(ROWS, dtype=jnp.int32)
    ends_at = jnp.cumsum(doc_lens)
    starts_at = ends_at - doc_lens
    doc_of = jnp.sum((row_ids[:, None] >= ends_at[None, :]).astype(jnp.int32), axis=1)
    doc_index = jnp.arange(DOCS_DEV, dtype=jnp.int32)
    begins = jnp.sum(
        jnp.where(doc_of[:, None] == doc_index[None, :], starts_at[None, :], 0), axis=1
    )
    in_docs = row_ids < DOC_ROWS
    query_rows = jnp.maximum(row_ids - DOC_ROWS, 0)
    segment = jnp.where(in_docs, doc_of, DOCS_DEV + query_rows // QLEN)
    position = jnp.where(in_docs, row_ids - begins, query_rows % QLEN)
    return (segment, position)


def rotary(position):
    step_ids = jnp.arange(HEAD // 2, dtype=jnp.int32).astype(jnp.float32)
    frequency = jnp.exp(step_ids * (-2.0 * math.log(10000.0) / HEAD))
    angles = position.astype(jnp.float32)[..., None] * frequency
    cosine, sine = jnp.cos(angles), jnp.sin(angles)
    return (
        jnp.concatenate([cosine] * 4, axis=-1),
        jnp.concatenate([-sine, sine] * 2, axis=-1),
    )


def lane_ids():
    return lax.broadcasted_iota(jnp.int32, (1, 2 * HEAD), 1)


def turned(value, cosine, sine):
    in_first = lane_ids() % HEAD < HEAD // 2
    ahead = pltpu.roll(value, 2 * HEAD - HEAD // 2, 1)
    behind = pltpu.roll(value, HEAD // 2, 1)
    return value * cosine + jnp.where(in_first, ahead, behind) * sine


def statistics(values):
    center = values - jnp.mean(values, axis=1, keepdims=True)
    spread = jnp.mean(center * center, axis=1, keepdims=True)
    scale = lax.rsqrt(spread + norm_eps)
    return center * scale, scale


def norm_back(grad, unit, scale, gain):
    inner = grad * gain
    along = jnp.mean(inner * unit, axis=1, keepdims=True)
    grad_in = scale * (inner - jnp.mean(inner, axis=1, keepdims=True) - unit * along)
    return grad_in, jnp.sum(grad * unit, axis=0, keepdims=True), jnp.sum(grad, axis=0, keepdims=True)


def gelu_parts(value):
    bell = jnp.exp(-0.5 * value * value)
    part = 1.0 / (1.0 + (0.3275911 * math.sqrt(0.5)) * jnp.abs(value))
    tail = 0.5 * 1.061405429 * part - 0.5 * 1.453152027
    tail = tail * part + 0.5 * 1.421413741
    tail = tail * part - 0.5 * 0.284496736
    tail = tail * part + 0.5 * 0.254829592
    tail = tail * part * bell
    below = jnp.where(value >= 0, 1.0 - tail, tail)
    return value * below, below + value * bell * (1.0 / math.sqrt(2.0 * math.pi))


def probabilities(queries, keys, allowed, held):
    scores = product_nt(jnp.where(held, queries, jnp.zeros_like(queries)), keys)
    scores = jnp.where(allowed, scores, masked_score)
    scores = jnp.exp(scores - jnp.max(scores, axis=1, keepdims=True))
    return scores * (1.0 / jnp.sum(scores, axis=1, keepdims=True))


LOW, WIDE = jnp.bfloat16, jnp.float32
VMEM_LIMIT = 46 << 20


def in_hbm(array):
    if array.size < 1 << 17:
        return array
    return pltpu.with_memory_space_constraint(array, pltpu.HBM)


BLOCK = 512
NO_COST = pl.CostEstimate(flops=1, bytes_accessed=1, transcendentals=0)
FULL_COST = pl.CostEstimate(flops=40 * 10**9, bytes_accessed=10**8, transcendentals=0)


class Weight:
    def __init__(self, count, rows, columns, width, parts):
        self.count, self.rows, self.columns, self.width = count, rows, columns, width
        self.height = self.count * rows
        self.arrays = [group for _, _, groups in parts for group in groups]
        self.plan = [
            (start, width, [group.shape[0] for group in groups]) for start, width, groups in parts
        ]

    def scratch(self):
        return [
            pltpu.VMEM((self.height, self.columns), LOW),
            pltpu.SemaphoreType.DMA((self.columns // self.width, self.count)),
        ]


class Fetch:
    def __init__(self, weight, places_ref, refs, buffer, sems):
        self.weight, self.places_ref = weight, places_ref
        self.refs, self.buffer, self.sems = refs, buffer, sems
        self.waited = set()

    def copies(self, number):
        weight, begin = self.weight, number * self.weight.width
        passed = 0
        for start, width, lengths in weight.plan:
            if start <= begin < start + width:
                break
            passed += len(lengths)
        columns = pl.ds(begin - start, weight.width)
        block = 0
        for group, length in enumerate(lengths):
            for inner in range(length):
                place = pl.multiple_of(self.places_ref[block] * weight.rows, weight.rows)
                yield pltpu.make_async_copy(
                    self.refs[passed + group].at[inner, pl.ds(0, weight.rows), columns],
                    self.buffer.at[pl.ds(place, weight.rows), pl.ds(begin, weight.width)],
                    self.sems.at[number, block],
                )
                block += 1

    def start(self):
        for number in range(self.weight.columns // self.weight.width):
            for copy in self.copies(number):
                copy.start()

    def ready(self, until=None):
        until = self.weight.columns if until is None else until
        for number in range(-(-until // self.weight.width)):
            if number not in self.waited:
                self.waited.add(number)
                for copy in self.copies(number):
                    copy.wait()
        return self.buffer


class Parts:
    def __init__(self, refs, loads, weights, outs, scratch):
        self.pick, self.places, *refs = refs
        loaded, refs = refs[: len(loads)], refs[len(loads) :]
        fetched = {}
        for name, weight in weights.items():
            fetched[name], refs = refs[: len(weight.arrays)], refs[len(weight.arrays) :]
        stored, refs = refs[: len(outs)], refs[len(outs) :]
        self.buffers, refs = dict(zip(loads, refs)), refs[len(loads) :]
        self.weights = {}
        for name, weight in weights.items():
            buffer, sems, *refs = refs
            self.weights[name] = Fetch(weight, self.places, fetched[name], buffer, sems)
        self.outs, refs = dict(zip(outs, refs)), refs[len(outs) :]
        self.scratch, refs = dict(zip(scratch, refs)), refs[len(scratch) :]
        load_sems, out_sems = refs
        self.loads = {
            name: pltpu.make_async_copy(ref, self.buffers[name], load_sems.at[number])
            for number, (name, ref) in enumerate(zip(loads, loaded))
        }
        self.stores = {
            name: pltpu.make_async_copy(self.outs[name], ref, out_sems.at[number])
            for number, (name, ref) in enumerate(zip(outs, stored))
        }
        self.waited, self.begun = set(), set()

    def start(self, order):
        for name in order:
            (self.loads[name] if name in self.loads else self.weights[name]).start()

    def ref(self, name):
        if name in self.outs:
            return self.outs[name]
        if name in self.scratch:
            return self.scratch[name]
        if name not in self.waited:
            self.waited.add(name)
            self.loads[name].wait()
        return self.buffers[name]

    def refs(self, *names):
        return [self.ref(name) for name in names]

    def leave(self, *names):
        for name in names:
            self.stores[name].start()

    def finish(self):
        for name in self.stores:
            self.stores[name].wait()


def run_parts(name, bodies, pick, places, loads, weights, outs, scratch, order, cost):
    def kernel(*refs):
        parts = Parts(refs, list(loads), weights, list(outs), list(scratch))
        parts.start(order)
        for body in bodies:
            body(parts)
        if "vectors" in outs:
            parts.leave("vectors")
        parts.finish()

    arrays = [*loads.values(), *(array for weight in weights.values() for array in weight.arrays)]
    scratch_shapes = [pltpu.VMEM(array.shape, array.dtype) for array in loads.values()]
    scratch_shapes += [entry for weight in weights.values() for entry in weight.scratch()]
    scratch_shapes += [pltpu.VMEM(*out) for out in outs.values()] + list(scratch.values())
    results = pl.pallas_call(
        kernel,
        in_specs=[pl.BlockSpec(memory_space=pltpu.SMEM)] * 2
        + [pl.BlockSpec(memory_space=pl.ANY)] * len(arrays),
        out_specs=[pl.BlockSpec(memory_space=pltpu.HBM)] * len(outs),
        out_shape=[pltpu.HBM(*out) for out in outs.values()],
        scratch_shapes=scratch_shapes
        + [pltpu.SemaphoreType.DMA((len(loads),)), pltpu.SemaphoreType.DMA((len(outs),))],
        compiler_params=pltpu.CompilerParams(vmem_limit_bytes=VMEM_LIMIT),
        cost_estimate=cost,
        name=name,
    )(pick, places, *(in_hbm(array) for array in arrays))
    return dict(zip(outs, results))


def attend_part(parts):
    micro_step = parts.pick[1]
    source = parts.ref("x")
    cos_ref, sin_ref, column_ref, row_ref, bias_ref = parts.refs(
        "cosine", "sine", "column", "row", "qkv_bias"
    )
    cosine, sine = cos_ref[micro_step], sin_ref[micro_step]
    outs = parts.refs("q", "k", "v")
    width = source.shape[1]
    for part, ref in enumerate(outs):
        qkv = parts.weights["qkv"].ready((part + 1) * width)
        for start in range(0, width, BLOCK):
            at = slice(part * width + start, part * width + start + BLOCK)
            value = product(source[...], qkv[:, at])
            value = value + bias_ref[part : part + 1, start : start + BLOCK]
            for pair in range(0, BLOCK, 2 * HEAD):
                two = value[:, pair : pair + 2 * HEAD]
                if part < 2:
                    two = turned(two, cosine, sine)
                ref[:, start + pair : start + pair + 2 * HEAD] = two.astype(LOW)
    parts.leave("q", "k", "v")
    allowed = jnp.concatenate([column_ref[micro_step]] * 2, axis=1) == row_ref[micro_step]
    q_ref, k_ref, v_ref = outs
    mixture_ref, sum_ref, norm_ref, small_ref = parts.refs("mixture", "sum_one", "norm", "small")
    for start in range(0, width, 2 * HEAD):
        at = slice(start, start + 2 * HEAD)
        queries = q_ref[:, at] * LOW(score_scale)
        keys, values = k_ref[:, at], v_ref[:, at]
        mixed = []
        for head in range(2):
            held = lane_ids() // HEAD == head
            attention = probabilities(queries, keys, allowed, held)
            mixed.append(product(attention.astype(LOW), values))
        mixture_ref[:, at] = jnp.where(lane_ids() < HEAD, mixed[0], mixed[1]).astype(LOW)
    out = parts.weights["out"].ready()
    for start in range(0, width, BLOCK):
        at = slice(start, start + BLOCK)
        sum_ref[:, at] = (
            source[:, at].astype(WIDE)
            + small_ref[0:1, at]
            + product(mixture_ref[...], out[:, at])
        )
    unit, _ = statistics(sum_ref[...])
    norm_ref[...] = (unit * small_ref[1:2] + small_ref[2:3]).astype(LOW)
    parts.leave("mixture", "sum_one", "norm")


def up_part(parts):
    norm_ref, bias_ref, active_ref, slope_ref = parts.refs("norm", "up_bias", "active", "slope")
    for start in range(0, active_ref.shape[1], BLOCK):
        up = parts.weights["up"].ready(start + BLOCK)
        at = slice(start, start + BLOCK)
        active, slope = gelu_parts(product(norm_ref[...], up[:, at]) + bias_ref[:, at])
        active_ref[:, at] = active.astype(LOW)
        slope_ref[:, at] = slope.astype(LOW)
    parts.leave("active", "slope")


def down_part(parts):
    active_ref, norm_ref, small_ref = parts.refs("active", "norm", "small")
    sum_ref, result_ref = parts.refs("sum_two", "result")
    for start in range(0, sum_ref.shape[1], BLOCK):
        at = slice(start, start + BLOCK)
        down = parts.weights["down"].ready(start + BLOCK)
        sum_ref[:, at] = (
            norm_ref[:, at].astype(WIDE)
            + small_ref[3:4, at]
            + product(active_ref[...], down[:, at])
        )
    unit, _ = statistics(sum_ref[...])
    result = (unit * small_ref[4:5] + small_ref[5:6]).astype(LOW)
    result_ref[...] = result
    parts.leave("result", "sum_two")
    if "embedded" in parts.outs:
        parts.ref("embedded")[...] = product(result, parts.ref("projection")[...]).astype(LOW)
        parts.leave("embedded")
    if "activations" in parts.outs:
        early, late, own, both = parts.refs("early", "late", "own", "activations")

        @pl.when(parts.pick[0] == 1)
        def _():
            both[:ROWS] = early[...]
            both[ROWS:] = late[...]

        @pl.when(parts.pick[0] == 0)
        def _():
            both[:ROWS] = own[...]
            both[ROWS:] = result

        parts.leave("activations")


def vector_rows(parts):
    vector_ref = parts.ref("vectors")
    if "vectors" not in parts.begun:
        parts.begun.add("vectors")
        vector_ref[...] = jnp.zeros_like(vector_ref)
    return vector_ref


def norm_back_part(parts):
    if "docs" in parts.loads:
        own = jnp.sum(parts.ref("own_parts")[...].astype(WIDE), axis=0)
        embedded = jnp.concatenate([parts.ref("docs")[...], own], axis=0).astype(LOW)
        parts.ref("grad_embedded")[...] = embedded
        parts.leave("grad_embedded")
        upstream = product_nt(embedded, parts.ref("projection")[...])
        upstream = upstream * (1 - parts.pick[0]).astype(WIDE)
    else:
        upstream = parts.ref("back")[...].astype(WIDE)
    branch_ref, total, small_ref = parts.refs("branch", "total", "small")
    vector_ref = vector_rows(parts)
    unit, scale = statistics(parts.ref("sum_two")[...])
    grad, gain, bias = norm_back(upstream, unit, scale, small_ref[4:5])
    low = grad.astype(LOW)
    branch_ref[...] = low
    total[...] = grad
    vector_ref[10:11] = jnp.sum(low.astype(WIDE), axis=0, keepdims=True)
    vector_ref[11:12] = gain
    vector_ref[12:13] = bias
    parts.leave("branch")
    if "total" in parts.outs:
        parts.leave("total")


def feed_back_part(parts):
    branch_ref, gate_ref, attended_ref = parts.refs("branch", "gate", "attended")
    small_ref, slope_ref = parts.refs("small", "slope")
    vector_ref = vector_rows(parts)
    width = attended_ref.shape[1]
    down = parts.weights["down"].ready()
    for start in range(0, gate_ref.shape[1], BLOCK):
        at = slice(start, start + BLOCK)
        gate = product_nt(branch_ref[...], down[at]) * slope_ref[:, at].astype(WIDE)
        gate = gate.astype(LOW)
        gate_ref[:, at] = gate
        row, column = 6 + start // width, start % width
        vector_ref[row : row + 1, column : column + BLOCK] = jnp.sum(
            gate.astype(WIDE), axis=0, keepdims=True
        )
    parts.leave("gate")
    up = parts.weights["up"].ready()
    total = parts.ref("total")
    for start in range(0, total.shape[1], BLOCK):
        at = slice(start, start + BLOCK)
        total[:, at] += product_nt(gate_ref[...], up[at])
    unit, scale = statistics(parts.ref("sum_one")[...])
    grad, gain, bias = norm_back(total[...], unit, scale, small_ref[1:2])
    total[...] = grad
    low = grad.astype(LOW)
    attended_ref[...] = low
    vector_ref[3:4] = jnp.sum(low.astype(WIDE), axis=0, keepdims=True)
    vector_ref[4:5] = gain
    vector_ref[5:6] = bias
    parts.leave("attended")
    if "grad_one" in parts.outs:
        parts.ref("grad_one")[...] = grad
        parts.leave("grad_one")


def attend_back_part(parts):
    micro_step = parts.pick[1]
    attended_ref, mixed_ref, mixture, total = parts.refs("attended", "mixed", "mixture", "total")
    vector_ref = vector_rows(parts)
    cos_ref, sin_ref, column_ref, row_ref = parts.refs("cosine", "sine", "column", "row")
    cosine, sine = cos_ref[micro_step], sin_ref[micro_step]
    allowed = jnp.concatenate([column_ref[micro_step]] * 2, axis=1) == row_ref[micro_step]
    width = mixture.shape[1]
    if "grad_one" in parts.loads:
        total[...] = parts.ref("grad_one")[...]
    out = parts.weights["out"].ready()
    for start in range(0, width, BLOCK):
        at = slice(start, start + BLOCK)
        mixture[:, at] = product_nt(attended_ref[...], out[at]).astype(LOW)
    q_ref, k_ref, v_ref = parts.refs("q", "k", "v")
    for start in range(0, width, 2 * HEAD):
        at = slice(start, start + 2 * HEAD)
        queries, keys, values = q_ref[:, at], k_ref[:, at], v_ref[:, at]
        scaled = queries * LOW(score_scale)
        grad_mixture = mixture[:, at]
        grads = []
        for head in range(2):
            held = lane_ids() // HEAD == head
            attention = probabilities(scaled, keys, allowed, held)
            own = jnp.where(held, grad_mixture, jnp.zeros_like(grad_mixture))
            grad_attention = product_nt(own, values)
            grad_values = product_tn(attention.astype(LOW), own)
            along = jnp.sum(grad_attention * attention, axis=1, keepdims=True)
            grad_scores = (attention * (grad_attention - along)).astype(LOW)
            grads.append((product(grad_scores, keys), product_tn(grad_scores, queries), grad_values))
        first_head = lane_ids() < HEAD
        for part in range(2):
            value = jnp.where(first_head, grads[0][part], grads[1][part]) * score_scale
            mixed_ref[part, :, at] = turned(value, cosine, -sine).astype(LOW)
        mixed_ref[2, :, at] = (grads[0][2] + grads[1][2]).astype(LOW)
    parts.leave("mixed")
    for part in range(3):
        vector_ref[part : part + 1] = jnp.sum(
            mixed_ref[part].astype(WIDE), axis=0, keepdims=True
        )
    qkv = parts.weights["qkv"].ready()
    for start in range(0, width, BLOCK):
        at = slice(start, start + BLOCK)
        value = total[:, at]
        for part in range(3):
            value = value + product_nt(mixed_ref[part], qkv[at, part * width : (part + 1) * width])
        total[:, at] = value
    if "grad_low" in parts.outs:
        parts.ref("grad_low")[...] = total[...].astype(LOW)
        parts.leave("grad_low")
        parts.ref("grad_source")[...] = total[...]
    else:
        late, early, own, source_ref = parts.refs("late", "early", "own", "grad_source")

        @pl.when(parts.pick[0] == 1)
        def _():
            source_ref[:ROWS] = total[...]
            source_ref[ROWS:] = own[...]

        @pl.when(parts.pick[0] == 0)
        def _():
            source_ref[:ROWS] = early[...]
            source_ref[ROWS:] = late[...]

    parts.leave("grad_source")


class Layer:
    def __init__(self, places, layout):
        self.places = places
        self.layout = dict(zip(("cosine", "sine", "column", "row"), layout))

    def attend_set(self, source):
        rows = source.shape
        return (
            {"x": source, **self.layout, "qkv_bias": self.qkv_bias, "small": self.small},
            {"qkv": self.qkv, "out": self.out},
            {
                "q": (rows, LOW),
                "k": (rows, LOW),
                "v": (rows, LOW),
                "mixture": (rows, LOW),
                "sum_one": (rows, WIDE),
                "norm": (rows, LOW),
            },
            {},
        )

    def up_set(self):
        rows = (ROWS, self.up.columns)
        return (
            {"up_bias": self.up_bias},
            {"up": self.up},
            {"active": (rows, LOW), "slope": (rows, LOW)},
            {},
        )

    def down_set(self, projection, earlier):
        rows = (ROWS, self.down.columns)
        loads = {"small": self.small}
        outs = {"sum_two": (rows, WIDE), "result": (rows, LOW)}
        if projection is not None:
            loads["projection"] = projection
            outs["embedded"] = ((ROWS, PROJ), LOW)
        if earlier:
            loads |= dict(zip(("early", "late", "own"), earlier))
            outs["activations"] = ((MICRO * ROWS, self.down.columns), LOW)
        return loads, {"down": self.down}, outs, {}

    def run(self, name, bodies, sets, pick, more=None, cost=NO_COST):
        loads, weights, outs, scratch = dict(more or {}), {}, {}, {}
        order = list(loads)
        for one in sets:
            order += [key for key in (*one[0], *one[1]) if key not in order]
            loads, weights = loads | one[0], weights | one[1]
            outs, scratch = outs | one[2], scratch | one[3]
        return run_parts(
            name, bodies, pick, self.places, loads, weights, outs, scratch, order, cost
        )

    def attend(self, source, pick):
        return self.run("attend", [attend_part], [self.attend_set(source)], pick)

    def rise(self, norm, pick):
        return self.run("up", [up_part], [self.up_set()], pick, {"norm": norm})

    def fall(self, active, norm, pick):
        return self.run(
            "down", [down_part], [self.down_set(None, ())], pick, {"active": active, "norm": norm}
        )

    def forward(self, source, pick, projection, earlier):
        return self.run(
            "forward",
            [attend_part, up_part, down_part],
            [self.attend_set(source), self.up_set(), self.down_set(projection, earlier)],
            pick,
            cost=FULL_COST,
        )

    def norm_back_set(self, state, loss_grads, back_grad):
        rows = (ROWS, self.down.columns)
        outs = {"branch": (rows, LOW), "vectors": ((16, rows[1]), WIDE)}
        if loss_grads is not None:
            loads = dict(zip(("docs", "own_parts", "projection"), loss_grads))
            outs["grad_embedded"] = ((ROWS, PROJ), LOW)
        else:
            loads = {"back": back_grad}
        loads |= {"sum_two": state["sum_two"], "small": self.small}
        return loads, {}, outs, {"total": pltpu.VMEM(rows, WIDE)}

    def feed_back_set(self, state):
        rows, hidden = (ROWS, self.down.columns), self.up.columns
        return (
            {"slope": state["slope"], "small": self.small},
            {"down": self.down, "up": self.up},
            {
                "gate": ((ROWS, hidden), LOW),
                "attended": (rows, LOW),
                "vectors": ((16, rows[1]), WIDE),
            },
            {"total": pltpu.VMEM(rows, WIDE)},
        )

    def attend_back_set(self, state, earlier):
        rows = (ROWS, self.out.columns)
        outs = {"mixed": ((3, *rows), LOW), "vectors": ((16, rows[1]), WIDE)}
        loads = {"q": state["q"], "k": state["k"], "v": state["v"], **self.layout}
        if earlier:
            loads |= dict(zip(("late", "early", "own"), earlier))
            outs["grad_source"] = ((MICRO * ROWS, rows[1]), WIDE)
        else:
            outs |= {"grad_source": (rows, WIDE), "grad_low": (rows, LOW)}
        return (
            loads,
            {"out": self.out, "qkv": self.qkv},
            outs,
            {"mixture": pltpu.VMEM(rows, LOW), "total": pltpu.VMEM(rows, WIDE)},
        )

    def backward(self, state, loss_grads, back_grad, pick):
        return self.run(
            "backward",
            [norm_back_part, feed_back_part, attend_back_part],
            [
                self.norm_back_set(state, loss_grads, back_grad),
                self.feed_back_set(state),
                ({"sum_one": state["sum_one"]}, {}, {}, {}),
                self.attend_back_set(state, ()),
            ],
            pick,
            cost=FULL_COST,
        )

    def norm_back(self, state, back_grad, pick):
        loads, weights, outs, scratch = self.norm_back_set(state, None, back_grad)
        outs |= {"total": (state["sum_two"].shape, WIDE)}
        return self.run("norm_back", [norm_back_part], [(loads, weights, outs, {})], pick)

    def feed_back(self, state, branch, total, pick):
        loads, weights, outs, scratch = self.feed_back_set(state)
        outs |= {"grad_one": (total.shape, WIDE)}
        loads = {"branch": branch} | loads
        return self.run(
            "feed_back",
            [feed_back_part],
            [(loads, weights, outs, {}), ({"total": total, "sum_one": state["sum_one"]}, {}, {}, {})],
            pick,
        )

    def attend_back(self, state, attended, grad_one, earlier, pick):
        return self.run(
            "attend_back",
            [attend_back_part],
            [self.attend_back_set(state, earlier)],
            pick,
            {"attended": attended, "grad_one": grad_one},
        )


def grid_of(count):
    dims = []
    while count % 2 == 0:
        dims.append(2)
        count //= 2
    return ([count] if count > 1 else []) + dims


def coordinates(dims, number):
    at = []
    for size in reversed(dims):
        at.append(number % size)
        number = number // size
    return at[::-1]


def shifted(value, dims, dim, steps):
    count = math.prod(dims)
    stride = math.prod(dims[dim + 1 :])
    pairs = []
    for source in range(count):
        place = (source // stride) % dims[dim]
        pairs.append((source, source + ((place + steps) % dims[dim] - place) * stride))
    return lax.ppermute(value, "dp", pairs)


def after(value, *earlier):
    return lax.optimization_barrier((value, *earlier))[0]


def stage(sends, earlier, beside=None):
    values = [after(value, *earlier) for value, _ in sends]
    backwards = list(zip(values, sends))[::-1]
    arrived = [permuted(value) for value, (_, permuted) in backwards][::-1]
    made = beside(earlier, arrived) if beside else []
    return list(lax.optimization_barrier((*arrived, *made)))[: len(sends)]


def step_along(dims, dim, steps):
    return lambda value: shifted(value, dims, dim, steps)


def rows_kernel(top, places, *refs):
    pieces, out, sems = refs[:-2], refs[-2], refs[-1]
    copies = []
    for group in pieces:
        for inner in range(group.shape[0]):
            number = len(copies)
            copies.append(
                pltpu.make_async_copy(
                    group.at[inner, pl.ds(top, out.shape[1])],
                    out.at[places[number]],
                    sems.at[number],
                )
            )
    for copy in copies:
        copy.start()
    for copy in copies:
        copy.wait()


def placed_rows(groups, places, top, rows):
    count, columns = places.shape[0], groups[0].shape[2]
    return pl.pallas_call(
        partial(rows_kernel, top),
        out_shape=jax.ShapeDtypeStruct((count, rows, columns), groups[0].dtype),
        in_specs=[pl.BlockSpec(memory_space=pltpu.SMEM)]
        + [pl.BlockSpec(memory_space=pl.ANY)] * len(groups),
        out_specs=pl.BlockSpec(memory_space=pltpu.VMEM),
        scratch_shapes=[pltpu.SemaphoreType.DMA((count,))],
        name="place",
    )(places, *groups)


def block_owners(order, dims, at):
    owners = jnp.zeros((1,), jnp.int32)
    for dim in order:
        steps = jnp.arange(dims[dim], dtype=jnp.int32)
        own = ((at[dim] - steps) % dims[dim]) * math.prod(dims[dim + 1 :])
        owners = (own[:, None] + owners[None, :]).reshape(-1)
    return owners


class Gather:
    def __init__(self, chunks, dims):
        self.dims, self.chunks = dims, chunks
        self.held = [[value[None]] for value, _, _ in chunks]
        self.arrived, self.step = [], 0

    def groups(self, number):
        _, order, start = self.chunks[number]
        while self.step < start + len(order):
            self.advance()
        return self.held[number]

    def advance(self, beside=None):
        sends, takers = [], []
        for number, (value, order, start) in enumerate(self.chunks):
            if start <= self.step < start + len(order):
                dim = order[self.step - start]
                for steps in range(1, self.dims[dim]):
                    for group in self.held[number]:
                        sends.append((group, step_along(self.dims, dim, steps)))
                        takers.append(number)
        self.arrived = stage(sends, self.arrived, beside)
        for number in sorted(set(takers)):
            value, order, start = self.chunks[number]
            got = [one for one, taker in zip(self.arrived, takers) if taker == number]
            held = self.held[number] + got
            blocks = sum(group.shape[0] for group in held)
            last = self.step - start >= len(order) - 2
            if not last or (blocks * value.size < 1 << 20 and self.step - start < len(order) - 1):
                held = [jnp.concatenate(held)]
            self.held[number] = held
        self.step += 1


def scatter_rows_plain(left, right, dims, dp_index):
    count = math.prod(dims)
    at = [
        (dp_index // math.prod(dims[dim + 1 :])) % dims[dim] for dim in range(len(dims))
    ]
    samples, height = left.shape
    rows, columns = height // count, right.shape[1]
    split = left.reshape(samples, count // 2, 2, rows)
    for_other = lax.dynamic_index_in_dim(split, 1 - at[-1], 2, False).reshape(samples, -1)
    for_self = lax.dynamic_index_in_dim(split, at[-1], 2, False).reshape(samples, -1)
    sent = product_tn(for_other, right).astype(jnp.bfloat16)
    total = product_tn(for_self, right) + shifted(sent, dims, len(dims) - 1, 1).astype(jnp.float32)
    for dim in reversed(range(len(dims) - 1)):
        low = total.astype(jnp.bfloat16).reshape(-1, dims[dim], rows, columns)
        total = lax.dynamic_index_in_dim(low, at[dim], 1, False).astype(jnp.float32)
        for steps in range(1, dims[dim]):
            part = lax.dynamic_index_in_dim(low, (at[dim] + steps) % dims[dim], 1, False)
            total = total + shifted(part, dims, dim, steps).astype(jnp.float32)
    return total.reshape(rows, columns)


def fetch_chosen(pick_ref, pair, place, target, sem):
    for wanted, ref in ((1, pair[0]), (0, pair[1])):

        @pl.when(pick_ref[0] == wanted)
        def _(ref=ref):
            pltpu.make_async_copy(ref.at[place], target, sem).start()

    return pltpu.make_async_copy(pair[0].at[place], target, sem)


def grad_kernel(pick_ref, *refs, rows, slots, outer, stride, start, other_start, sends):
    lefts, rights, refs = (refs[0:2], refs[2:4]), (refs[4:6], refs[6:8]), refs[8:]
    if not sends:
        other_ref, *refs = refs
    out_refs, refs = refs[: 1 if sends else slots], refs[1 if sends else slots :]
    if sends:
        left, right, out, left_sems, right_sems, out_sems = refs
    else:
        left, right, other, out, left_sems, right_sems, other_sems, out_sems = refs
    chips, width = outer * slots, right.shape[1]
    samples = lefts[0][0].shape[0]
    side = 1 - pick_ref[1] if sends else pick_ref[1]
    thin = rows % 128 != 0
    block = min(2 * BLOCK, width) if thin else width
    blocks = width // block
    wide_part = rights[0][0].shape[-1]

    def left_copies(number):
        if thin:
            place, target = (slice(None), slice(None)), slice(None)
        else:
            chip = number if sends else chip_of(number)
            place = (slice(None), pl.ds(pl.multiple_of((2 * chip + side) * rows, rows), rows))
            target = slice(number * rows, (number + 1) * rows)
        return [
            fetch_chosen(
                pick_ref,
                lefts[half],
                place,
                left.at[half * samples : (half + 1) * samples, target],
                left_sems.at[number, half],
            )
            for half in range(2)
        ]

    def right_copies(number):
        begin = start + number * block
        columns = pl.ds(begin % wide_part, block)
        place = (slice(None), columns)
        if len(rights[0][0].shape) == 3:
            place = (begin // wide_part, *place)
        at = slice(number * block, (number + 1) * block)
        return [
            fetch_chosen(
                pick_ref,
                rights[half],
                place,
                right.at[half * samples : (half + 1) * samples, at],
                right_sems.at[number, half],
            )
            for half in range(2)
        ]

    def chip_of(number):
        inner = number % outer
        first_chip = inner // stride * stride * slots + inner % stride
        return first_chip + stride * lax.rem(pick_ref[2] + number // outer, slots)

    def other_copy(number):
        if thin:
            return pltpu.make_async_copy(
                other_ref.at[pl.ds(0, chips * rows), pl.ds(other_start + number * block, block)],
                other.at[:, number * block : (number + 1) * block],
                other_sems.at[number],
            )
        return pltpu.make_async_copy(
            other_ref.at[
                pl.ds(pl.multiple_of(chip_of(number) * rows, rows), rows), pl.ds(other_start, width)
            ],
            other.at[number * rows : (number + 1) * rows],
            other_sems.at[number],
        )

    def wait(copies):
        for copy in copies:
            copy.wait()

    leaving = []
    if thin:
        halves_of_left = left_copies(0)
        arriving = [right_copies(number) for number in range(blocks)]
        if not sends:
            others = [other_copy(number) for number in range(blocks)]
            for copy in others:
                copy.start()
        wait(halves_of_left)
        flipped = left[...].T
        turned = jnp.concatenate(
            [
                jnp.where(
                    side == 0,
                    flipped[2 * rows * chip : 2 * rows * chip + rows],
                    flipped[2 * rows * chip + rows : 2 * rows * (chip + 1)],
                )
                for chip in range(chips)
            ]
        )
        for number in range(blocks):
            at = slice(number * block, (number + 1) * block)
            wait(arriving[number])
            result = product(turned, right[:, at])
            if sends:
                out[:, at] = result.astype(LOW)
                leaving.append(
                    pltpu.make_async_copy(out.at[:, at], out_refs[0].at[:, at], out_sems.at[number])
                )
                leaving[-1].start()
                continue
            others[number].wait()
            out[:, at] = (result + other[:, at].astype(WIDE)).astype(LOW)
            for place in range(chips):
                leaving.append(
                    pltpu.make_async_copy(
                        out.at[pl.ds(pl.multiple_of(chip_of(place) * rows, rows), rows), at],
                        out_refs[place // outer].at[place % outer, :, at],
                        out_sems.at[number * chips + place],
                    )
                )
                leaving[-1].start()
    else:
        arriving = right_copies(0)
        pieces = [left_copies(number) for number in range(chips)]
        if not sends:
            others = [other_copy(number) for number in range(chips)]
            for copy in others:
                copy.start()
        wait(arriving)
        for number in range(chips):
            at = slice(number * rows, (number + 1) * rows)
            wait(pieces[number])
            result = product_tn(left[:, at], right[...])
            if sends:
                out[at] = result.astype(LOW)
                target = out_refs[0].at[at]
            else:
                others[number].wait()
                out[at] = (result + other[at].astype(WIDE)).astype(LOW)
                target = out_refs[number // outer].at[number % outer]
            leaving.append(pltpu.make_async_copy(out.at[at], target, out_sems.at[number]))
            leaving[-1].start()
    wait(leaving)


def fold_kernel(pick_ref, held_ref, other_ref, out_ref, *send_refs, slots, stride):
    for slot in range(slots):
        place = lax.rem(pick_ref[0] + slot, slots)
        for number in range(out_ref.shape[0]):
            index = number // stride * stride * slots + number % stride + place * stride
            value = held_ref[index].astype(WIDE) + other_ref[index].astype(WIDE)
            if slot == 0:
                out_ref[number] = value
                continue
            send_refs[slot - 1][number] = value.astype(LOW)


def slots_of(value, slots, stride):
    return value.reshape(-1, slots, stride, *value.shape[1:])


class Scatter:
    def __init__(self, name, lefts, rights, dims, at, dim, first):
        self.name, self.lefts, self.rights, self.dims, self.at = name, lefts, rights, dims, at
        self.count = math.prod(dims)
        self.height = lefts[0][0].shape[1]
        self.rows = self.height // self.count
        sample = rights[0][0]
        self.columns = sample.shape[-1] * (3 if sample.ndim == 3 else 1)
        self.slots, self.stride = dims[dim], math.prod(dims[dim + 1 : -1])
        self.place = at[dim]
        self.pick = jnp.stack([first, at[-1], self.place])

    def product(self, start, width, other, other_start, cost, earlier=()):
        samples = self.lefts[0][0].shape[0]
        half, rows, slots = self.height // 2, self.rows, self.slots
        chips = self.count // 2
        outer = chips // slots
        sends = other is None
        thin = rows % 128 != 0
        blocks = width // min(2 * BLOCK, width) if thin else 1
        pieces = 1 if thin else chips
        anywhere = pl.BlockSpec(memory_space=pl.ANY)
        args = [*self.lefts[0], *self.lefts[1], *self.rights[0], *self.rights[1]]
        args += [] if sends else [other]
        out_sems = blocks * (1 if sends else chips) if thin else chips
        other_scratch = [] if sends else [pltpu.VMEM((half, width), LOW)]
        other_sems = [] if sends else [pltpu.SemaphoreType.DMA((blocks if thin else chips,))]
        outs = [(half, width)] if sends else [(outer, rows, width)] * slots
        scratch = [
            pltpu.VMEM((2 * samples, self.height if thin else half), LOW),
            pltpu.VMEM((2 * samples, width), LOW),
            *other_scratch,
            pltpu.VMEM((half, width), LOW),
        ]
        return pl.pallas_call(
            partial(
                grad_kernel,
                rows=rows,
                slots=slots,
                outer=outer,
                stride=self.stride,
                start=start,
                other_start=other_start,
                sends=sends,
            ),
            in_specs=[pl.BlockSpec(memory_space=pltpu.SMEM)] + [anywhere] * len(args),
            out_specs=[anywhere] * len(outs),
            out_shape=[jax.ShapeDtypeStruct(out, LOW) for out in outs],
            scratch_shapes=[
                *scratch,
                pltpu.SemaphoreType.DMA((pieces, 2)),
                pltpu.SemaphoreType.DMA((blocks, 2)),
                *other_sems,
                pltpu.SemaphoreType.DMA((out_sems,)),
            ],
            compiler_params=pltpu.CompilerParams(vmem_limit_bytes=VMEM_LIMIT),
            cost_estimate=cost,
            name=self.name + ("_send" if sends else "_keep"),
        )(after(self.pick, *earlier), *(in_hbm(array) for array in args))

    def make(self, cost, earlier=(), start=0, width=None):
        self.sent = self.product(start, width or self.columns, None, 0, cost, earlier)[0]
        self.other_from = start
        return self.sent

    def keep(self, start, width, cost, earlier=()):
        return self.product(start, width, self.other, start - self.other_from, cost, earlier)


def own_kernel(where_ref, vectors_ref, *out_refs, spans):
    width = vectors_ref.shape[1]
    for (first_row, rows, length), out_ref in zip(spans, out_refs):
        start = where_ref[0] * length
        if rows > 1 and width % length == 0:
            line = vectors_ref[pl.ds(first_row + start // width, 1)]
        else:
            line = jnp.concatenate(
                [vectors_ref[first_row + row : first_row + row + 1] for row in range(rows)], axis=1
            )
        turns = lax.rem(line.shape[1] - lax.rem(start, line.shape[1]), line.shape[1])
        line = pltpu.roll(jnp.broadcast_to(line, (8, line.shape[1])), turns, 1)
        out_ref[...] = line[0:1, :length]


def own_parts(vectors, spans, dp_index):
    return pl.pallas_call(
        partial(own_kernel, spans=spans),
        in_specs=[
            pl.BlockSpec(memory_space=pltpu.SMEM),
            pl.BlockSpec(memory_space=pltpu.VMEM),
        ],
        out_specs=[pl.BlockSpec(memory_space=pltpu.VMEM)] * len(spans),
        out_shape=[jax.ShapeDtypeStruct((1, length), WIDE) for _, _, length in spans],
        name="own_parts",
    )(dp_index[None], vectors)


class Whole:
    def __init__(self, value):
        self.value = value

    def outgoing(self, dim):
        return self.value

    def take(self, arrived):
        self.value = self.value + arrived


class Halved:
    def __init__(self, value, dims, at):
        self.value, self.dims, self.at = value, dims, at

    def outgoing(self, dim):
        split = self.value.reshape(-1, self.dims[dim], *self.value.shape[1:])
        self.kept = lax.dynamic_index_in_dim(split, self.at[dim], 1, False)
        return lax.dynamic_index_in_dim(split, 1 - self.at[dim], 1, False)

    def take(self, arrived):
        self.value = self.kept + arrived


def folded(held, moved, slots, stride, place):
    outer, rows, columns = held.shape
    if rows % 16 == 0 and len(moved) == 1:
        whole = pl.BlockSpec(memory_space=pltpu.VMEM)
        shape = (outer // slots, rows, columns)
        total, *sends = pl.pallas_call(
            partial(fold_kernel, slots=slots, stride=stride),
            out_shape=[jax.ShapeDtypeStruct(shape, WIDE)]
            + [jax.ShapeDtypeStruct(shape, LOW)] * (slots - 1),
            in_specs=[pl.BlockSpec(memory_space=pltpu.SMEM), whole, whole],
            out_specs=[whole] * slots,
            compiler_params=pltpu.CompilerParams(vmem_limit_bytes=24 << 20),
            cost_estimate=NO_COST,
            name="fold",
        )(place[None], held, moved[0])
        return total, sends
    total = held.astype(WIDE)
    for piece in moved:
        total = total + piece.astype(WIDE)
    split = slots_of(total, slots, stride)
    blocks = [
        lax.dynamic_index_in_dim(split, (place + steps) % slots, 1, False).reshape(-1, rows, columns)
        for steps in range(slots)
    ]
    return blocks[0], [block.astype(LOW) for block in blocks[1:]]


def travels(pieces, chunks, order, dims, at, cores, riders, during):
    held, sends, sums = {}, {}, {}
    arrived, riding = [], []
    ways = list(reversed(range(len(dims))))
    for step in range(chunks + len(order) - 1):
        if step < chunks:
            held[step], *sends[step] = pieces[step]
        if step in riders:
            riding += [(rider, step) for rider in riders[step]()]
        outgoing, takers = [], []
        for phase, dim in enumerate(order):
            number = step - phase
            if 0 <= number < chunks:
                outgoing += [
                    (value, step_along(dims, dim, k)) for k, value in enumerate(sends[number], start=1)
                ]
                takers += [number] * len(sends[number])
        exchanging = cores.get(step, lambda: [])()
        outgoing += [(weight.sent, step_along(dims, ways[0], 1)) for weight in exchanging]
        along = [(rider, ways[step - start]) for rider, start in riding if step - start < len(ways)]
        outgoing += [(rider.outgoing(dim), step_along(dims, dim, 1)) for rider, dim in along]

        def beside(earlier, arriving):
            for weight, half in zip(exchanging, arriving[len(takers) :]):
                weight.other = half
            return during[step](earlier) if step < len(during) else []

        arrived = stage(outgoing, arrived, beside)
        for (rider, _), part in zip(along, arrived[len(takers) + len(exchanging) :]):
            rider.take(part)
        arrived = arrived[: len(takers)]
        for phase, dim in enumerate(order):
            number = step - phase
            if not 0 <= number < chunks:
                continue
            moved = [value for value, taker in zip(arrived, takers) if taker == number]
            left = order[phase + 1 :]
            if left:
                stride = math.prod(dims[other] for other in left if other > left[0])
                held[number], sends[number] = folded(
                    held[number], moved, dims[left[0]], stride, at[left[0]]
                )
            else:
                total = held[number].astype(WIDE)
                for piece in moved:
                    total = total + piece.astype(WIDE)
                sums[number] = total.reshape(total.shape[-2:])
    return [sums[number] for number in range(chunks)]


def spread(value, count):
    return lax.all_to_all(
        jnp.broadcast_to(value[None], (count, *value.shape)), "dp", 0, 0, tiled=True
    )


def summed(parts):
    return jnp.sum(lax.all_to_all(parts, "dp", 0, 0, tiled=True).astype(jnp.float32), axis=0)


def halves(value):
    high = value.astype(jnp.bfloat16)
    return high, (value - high.astype(jnp.float32)).astype(jnp.bfloat16)


def exact_product(left_side, right_side):
    high, low = halves(right_side)
    return product(left_side, high) + product(left_side, low)


def product_by_ones(left_side, right_side):
    high, low = halves(left_side)
    return product(high, right_side) + product(low, right_side)


def prefix_masks(length):
    places = lax.broadcasted_iota(jnp.int32, (1, length), 1)
    return [places < width for width in PREFIXES]


def similar_parts(documents, queries_t):
    docs_f32 = documents.astype(jnp.float32)
    squares = docs_f32 * docs_f32
    query_squares = queries_t * queries_t
    queries_low = queries_t.astype(jnp.bfloat16)
    parts = []
    for width, mask in zip(PREFIXES, prefix_masks(PROJ)):
        cut = jnp.where(mask, docs_f32, 0.0)
        doc_scale = lax.rsqrt(
            jnp.sum(jnp.where(mask, squares, 0.0), axis=1, keepdims=True) + unit_eps
        )
        query_scale = lax.rsqrt(
            jnp.sum(query_squares[:width], axis=0, keepdims=True) + unit_eps
        )
        cut = cut.astype(jnp.bfloat16)
        similar = product(cut, queries_low) * doc_scale * query_scale
        parts.append((cut, doc_scale, query_scale, similar))
    return parts


def members_of(ends_ref, micro_step, by_row):
    shape = (DOC_ROWS, 8) if by_row else (8, DOC_ROWS)
    rows = lax.broadcasted_iota(jnp.int32, shape, 0 if by_row else 1)
    docs = lax.broadcasted_iota(jnp.int32, shape, 1 if by_row else 0)
    inside = jnp.zeros(shape, jnp.float32)
    for number in range(DOCS_DEV):
        begin = ends_ref[micro_step, number - 1] if number else 0
        held = (docs == number) & (rows >= begin) & (rows < ends_ref[micro_step, number])
        inside = jnp.where(held, 1.0, inside)
    return inside.astype(jnp.bfloat16)


def query_of_token(tokens, by_token):
    shape = (tokens, 128) if by_token else (128, tokens)
    token = lax.broadcasted_iota(jnp.int32, shape, 0 if by_token else 1)
    query = lax.broadcasted_iota(jnp.int32, shape, 1 if by_token else 0)
    held = (token >= query * QLEN) & (token < query * QLEN + QLEN)
    return jnp.where(held, 1.0, 0.0).astype(jnp.bfloat16)


def score_kernel(ends_ref, queries_ref, docs_ref, out_ref, *, micro_step):
    tokens = queries_ref.shape[0] * queries_ref.shape[1]
    queries_t = queries_ref[...].astype(WIDE).reshape(tokens, PROJ).T
    members = members_of(ends_ref, micro_step, False)
    by_query = query_of_token(tokens, True)
    for number, (_, _, _, similar) in enumerate(similar_parts(docs_ref[:DOC_ROWS], queries_t)):
        masses = exact_product(members, jnp.exp(sharpness * similar))
        held = lax.broadcasted_iota(jnp.int32, masses.shape, 0) < DOCS_DEV
        logs = jnp.log(jnp.where(held, masses, 1.0))
        out_ref[0, number] = product_by_ones(logs, by_query) / sharpness


def loss_kernel(
    ends_ref, where_ref, queries_ref, docs_ref, tables_ref, times_ref, first_ref,
    loss_ref, grad_queries_ref, grad_docs_ref, table, *, micro_step
):
    step = pl.program_id(0)
    devices, width = queries_ref.shape[:2]
    tokens = devices * width
    queries_t = queries_ref[...].astype(WIDE).reshape(tokens, PROJ).T
    queries_low = queries_t.astype(LOW)
    members = members_of(ends_ref, micro_step, False)
    members_by_row = members_of(ends_ref, micro_step, True)
    spread_out = query_of_token(tokens, False)
    places = lax.broadcasted_iota(jnp.int32, (PROJ, 1), 0)
    grad_queries = jnp.zeros((PROJ, tokens), WIDE)
    grad_docs = jnp.zeros((DOC_ROWS, PROJ), WIDE)
    losses = jnp.zeros((1, 128), WIDE)
    times, first = times_ref[0], first_ref[0]
    own_rows = pl.ds(pl.multiple_of(where_ref[0] * 8, 8), 8)
    own_times, own_first = times_ref[0, own_rows], first_ref[0, own_rows]
    table[...] = jnp.zeros_like(table)
    for number, (cut, doc_scale, query_scale, similar) in enumerate(
        similar_parts(docs_ref[:DOC_ROWS], queries_t)
    ):
        for device in range(table.shape[0] // 8):
            table[8 * device : 8 * device + DOCS_DEV] = tables_ref[device, 0, number]
        scores = table[...]
        top = jnp.max(jnp.where(times > 0, scores, -1e30), axis=0, keepdims=True)
        top = jnp.where(top > -1e29, top, 0.0)
        normal = top + jnp.log(
            jnp.maximum(
                jnp.sum(times * jnp.exp(jnp.minimum(scores - top, 0.0)), axis=0, keepdims=True),
                1e-30,
            )
        )
        losses = losses + normal - jnp.sum(first * scores, axis=0, keepdims=True)
        own = table[own_rows]
        grad_score = own_times * jnp.exp(jnp.where(own_times > 0, own - normal, 0.0)) - own_first
        weights = jnp.exp(sharpness * similar)
        masses = exact_product(members, weights)
        by_token = product_by_ones(grad_score, spread_out)
        held = lax.broadcasted_iota(jnp.int32, masses.shape, 0) < DOCS_DEV
        by_token = jnp.where(held, by_token / jnp.where(held, masses, 1.0), 0.0)
        grad_similar = weights * exact_product(members_by_row, by_token)
        along = grad_similar * similar
        pulled = (grad_similar * doc_scale * query_scale).astype(LOW)
        mask = lax.broadcasted_iota(jnp.int32, (1, PROJ), 1) < PREFIXES[number]
        grad_docs = (
            grad_docs
            + jnp.where(mask, product_nt(pulled, queries_low), 0.0)
            - cut.astype(WIDE) * (doc_scale * doc_scale * jnp.sum(along, axis=1, keepdims=True))
        )
        toward = product_tn(cut, pulled)
        back = queries_t * (query_scale * query_scale * jnp.sum(along, axis=0, keepdims=True))
        grad_queries = grad_queries + toward - jnp.where(places < PREFIXES[number], back, 0.0)
    loss_ref[0] = losses
    grad_queries_ref[...] = grad_queries.T.reshape(devices, width, PROJ).astype(LOW)

    @pl.when(step == 0)
    def _():
        grad_docs_ref[...] = grad_docs

    @pl.when(step > 0)
    def _():
        grad_docs_ref[...] += grad_docs


class Loss:
    def __init__(self, micro_step, ends, pair_rows, dp_index, count):
        self.micro_step, self.ends, self.dp_index, self.count = micro_step, ends, dp_index, count
        self.group = math.gcd(count, 16)
        self.steps = count // self.group
        place = jnp.arange(8 * count, dtype=jnp.int32)
        doc_ids = jnp.where(place % 8 < DOCS_DEV, place // 8 * DOCS_DEV + place % 8, -1)
        picked = (pair_rows[None, :, :] == doc_ids[:, None, None]).astype(WIDE)
        self.times, self.first = [
            jnp.pad(
                jnp.swapaxes(value.reshape(8 * count, self.steps, -1), 0, 1),
                [(0, 0), (0, 0), (0, 128 - self.group * QRY_DEV)],
            )
            for value in (jnp.sum(picked, axis=2), picked[..., 0])
        ]
        self.params = dict(
            grid=(self.steps,), compiler_params=pltpu.CompilerParams(vmem_limit_bytes=40 << 20)
        )
        self.queries_spec = pl.BlockSpec((self.group, QRY_DEV * QLEN, PROJ), lambda i: (i, 0, 0))
        self.smem = pl.BlockSpec(memory_space=pltpu.SMEM)

    def scores(self, embedded):
        self.embedded = embedded
        self.queries = spread(embedded[DOC_ROWS:], self.count)
        return pl.pallas_call(
            partial(score_kernel, micro_step=self.micro_step),
            out_shape=jax.ShapeDtypeStruct((self.steps, 3, 8, 128), WIDE),
            in_specs=[
                self.smem,
                self.queries_spec,
                pl.BlockSpec((ROWS, PROJ), lambda i: (0, 0)),
            ],
            out_specs=pl.BlockSpec((1, 3, 8, 128), lambda i: (i, 0, 0, 0)),
            name="scores",
            cost_estimate=NO_COST,
            **self.params,
        )(self.ends, self.queries, embedded)[:, :, :DOCS_DEV]

    def grads(self, tables, *earlier):
        losses, grad_queries, grad_docs = pl.pallas_call(
            partial(loss_kernel, micro_step=self.micro_step),
            out_shape=(
                jax.ShapeDtypeStruct((self.steps, 1, 128), WIDE),
                jax.ShapeDtypeStruct(self.queries.shape, LOW),
                jax.ShapeDtypeStruct((DOC_ROWS, PROJ), WIDE),
            ),
            in_specs=[
                self.smem,
                self.smem,
                self.queries_spec,
                pl.BlockSpec((ROWS, PROJ), lambda i: (0, 0)),
                pl.BlockSpec((self.count, 1, 3, DOCS_DEV, 128), lambda i: (0, i, 0, 0, 0)),
                pl.BlockSpec((1, 8 * self.count, 128), lambda i: (i, 0, 0)),
                pl.BlockSpec((1, 8 * self.count, 128), lambda i: (i, 0, 0)),
            ],
            out_specs=(
                pl.BlockSpec((1, 1, 128), lambda i: (i, 0, 0)),
                self.queries_spec,
                pl.BlockSpec((DOC_ROWS, PROJ), lambda i: (0, 0)),
            ),
            scratch_shapes=[pltpu.VMEM((8 * self.count, 128), WIDE)],
            name="losses",
            cost_estimate=NO_COST,
            **self.params,
        )(
            self.ends,
            self.dp_index[None],
            self.queries,
            after(self.embedded, *earlier),
            tables,
            self.times,
            self.first,
        )
        losses = losses[:, 0, : self.group * QRY_DEV].reshape(self.count * QRY_DEV)
        own = lax.dynamic_slice_in_dim(losses, self.dp_index * QRY_DEV, QRY_DEV, 0)
        return own, grad_queries, grad_docs


def shards(
    tokens,
    qkv_weight,
    qkv_bias,
    out_weight,
    out_bias,
    norm1_gain,
    norm1_bias,
    up_weight,
    up_bias,
    down_weight,
    down_bias,
    norm2_gain,
    norm2_bias,
    proj_weight,
    doc_lengths,
    pair_docs,
):
    section_index = lax.axis_index("section")
    dp_index = lax.axis_index("dp")
    count = lax.axis_size("dp")
    dims = grid_of(count)
    at = coordinates(dims, dp_index)
    is_first = section_index == 0
    first = is_first.astype(jnp.int32)
    width, hidden = tokens.shape[1], up_weight.shape[2]
    own_height = width // count
    by_hand = own_height % 16 == 0

    segments, positions = [
        jnp.stack(value)
        for value in zip(*(doc_layout(doc_lengths[micro_step]) for micro_step in range(MICRO)))
    ]
    by_row = jnp.broadcast_to(segments[:, :, None], (MICRO, ROWS, ROWS // 2))
    layout = (*rotary(positions), by_row, segments[:, None, :])
    picks = [jnp.stack([first, jnp.int32(micro_step)]) for micro_step in range(MICRO)]
    own_rows = [tokens[micro_step * ROWS : (micro_step + 1) * ROWS] for micro_step in range(MICRO)]
    ends = jnp.cumsum(doc_lengths, axis=1)
    pair_rows = pair_docs.reshape(count, MICRO, QRY_DEV, CANDS)
    losses_of = [
        Loss(
            micro_step,
            ends,
            pair_rows[:, micro_step].reshape(count * QRY_DEV, CANDS),
            dp_index,
            count,
        )
        for micro_step in range(MICRO)
    ]

    vectors = (
        qkv_bias,
        out_bias,
        norm1_gain,
        norm1_bias,
        up_bias,
        down_bias,
        norm2_gain,
        norm2_bias,
    )
    lengths = [value.shape[1] for value in vectors]
    short = sum(lengths)
    shards_of = [out_weight[0], qkv_weight[0], up_weight[0], down_weight[0]]

    fetched = (width, width, hidden // 4, width // 2)

    def small_parameters(layer, rows, projection):
        cuts, start = [], 0
        for length in lengths:
            cuts.append(rows[:, start : start + length].astype(WIDE).reshape(-1))
            start += length
        qkv_b, out_b, gain_one, bias_one, up_b, down_b, gain_two, bias_two = cuts
        layer.qkv_bias = qkv_b.reshape(3, width)
        layer.up_bias = up_b[None]
        layer.small = jnp.concatenate(
            [
                jnp.stack([out_b, gain_one, bias_one, down_b, gain_two, bias_two]),
                jnp.zeros((2, width), WIDE),
            ]
        )
        return projection.reshape(width, -1)

    if by_hand:
        line = jnp.concatenate([*vectors, jnp.zeros((1, width - short), LOW)], axis=1)
        proj_lines = proj_weight.reshape(-1, width)
        filler = jnp.zeros((15 - proj_lines.shape[0], width), LOW)
        order = list(range(len(dims)))
        chunks = [(jnp.concatenate([shards_of[0], line, proj_lines, filler]), order, 0)]
        cuts_of = ([1], [1, 2], [2, 2], [2, 2])
        for number in (1, 2, 3):
            parts, shard = cuts_of[number], shards_of[number]
            unit, start = shard.shape[1] // sum(parts), 0
            for part in parts:
                value = lax.slice_in_dim(shard, start, start + part * unit, axis=1)
                chunks.append((value, order, len(chunks)))
                start += part * unit
        gather = Gather(chunks, dims)
        layer = Layer(block_owners(order, dims, at), layout)

        def whole(number, first_chunk):
            parts, start = [], 0
            unit = shards_of[number].shape[1] // sum(cuts_of[number])
            for offset, part in enumerate(cuts_of[number]):
                parts.append((start, part * unit, gather.groups(first_chunk + offset)))
                start += part * unit
            return Weight(count, shards_of[number].shape[0], start, fetched[number], parts)

        layer.out = whole(0, 0)
        block = placed_rows(layer.out.arrays, layer.places, own_height, 16)
        projection = small_parameters(
            layer, block[:, 0], block[:, 1 : 1 + proj_lines.shape[0]]
        )
        layer.qkv = whole(1, 1)
        states = []

        def attend_beside(micro_step):
            def beside(earlier, arriving):
                rows = after(own_rows[micro_step], *earlier)
                states.append(layer.attend(rows, picks[micro_step]))
                return [states[-1]["norm"]]

            return beside

        def up_beside(earlier, arriving):
            for state, pick in zip(states, picks):
                state |= layer.rise(after(state["norm"], *earlier), pick)
            return [state["active"] for state in states]

        gather.advance(attend_beside(0))
        gather.advance(attend_beside(1))
        layer.up = whole(2, 3)
        gather.advance(up_beside)
        gather.advance()
        layer.down = whole(3, 5)
    else:
        layer = Layer(jnp.zeros((1,), jnp.int32), layout)
        wholes = [
            lax.all_gather(value, "dp", axis=0, tiled=True)[None] for value in shards_of
        ]
        layer.out, layer.qkv, layer.up, layer.down = [
            Weight(1, *value.shape[1:], columns, [(0, value.shape[2], [value])])
            for value, columns in zip(wholes, fetched)
        ]
        together = spread(jnp.concatenate([*vectors, proj_weight.reshape(1, -1)], axis=1)[0], count)
        projection = small_parameters(layer, together[:, :short], together[:, short:])
        states = [layer.attend(rows, pick) for rows, pick in zip(own_rows, picks)]
        for state, pick in zip(states, picks):
            state |= layer.rise(state["norm"], pick)

    arrived = []
    for state, pick in zip(states, picks):
        active = after(state["active"], *(one["result"] for one in states if "result" in one))
        state |= layer.fall(active, state["norm"], pick)
        arrived.append(from_behind(state["result"], "section", 1))
    own_scores = []
    for micro_step in range(MICRO):
        last = micro_step == MICRO - 1
        states.append(
            layer.forward(
                arrived[micro_step],
                picks[micro_step],
                projection,
                [state["result"] for state in states] if last else (),
            )
        )
        own_scores.append(losses_of[micro_step].scores(states[-1]["embedded"]))
    activations = states[-1]["activations"][None]

    tables = spread(jnp.stack(own_scores), count)
    own_losses, loss_grads = [None] * MICRO, [None] * MICRO
    earlier = []
    for micro_step in reversed(range(MICRO)):
        own_losses[micro_step], grad_queries, grad_docs = losses_of[micro_step].grads(
            tables[:, micro_step], *earlier
        )
        earlier = [grad_queries]
        loss_grads[micro_step] = (
            grad_docs,
            lax.all_to_all(grad_queries, "dp", 0, 0, tiled=True),
            projection,
        )
    own_losses = jnp.concatenate(own_losses)
    query_losses = jnp.where(is_first, from_behind(own_losses, "section", -1), own_losses)
    loss_grads[0] = (after(loss_grads[0][0], query_losses), *loss_grads[0][1:])

    back, back_grads = [], []
    for micro_step in reversed(range(MICRO)):
        back.append(
            layer.backward(states[MICRO + micro_step], loss_grads[micro_step], None, picks[micro_step])
        )
        back_grads.append(from_behind(back[-1]["grad_low"], "section", -1))
    back.append(layer.backward(states[1], None, back_grads[0], picks[1]))
    back_grad = after(back_grads[1], back[-1]["mixed"])
    grads = layer.norm_back(states[0], back_grad, picks[0])
    vectors_of = [one["vectors"] for one in (*back, grads)]

    def pairs(values):
        return [values[1], values[3]], [values[0], values[2]]

    lefts = [
        pairs([state[name] for state in states]) for name in ("active", "norm", "mixture")
    ] + [pairs([*own_rows, *arrived])]

    def rights_of(name):
        return pairs([grads[name], *(back[number][name] for number in (2, 1, 0))])

    def feed_back(*earlier):
        grads.update(
            layer.feed_back(states[0], after(grads["branch"], *earlier), grads["total"], picks[0])
        )

    def attend_back(*earlier):
        grads.update(
            layer.attend_back(
                states[0],
                after(grads["attended"], *earlier),
                grads["grad_one"],
                [one["grad_source"] for one in back],
                picks[0],
            )
        )

    if by_hand:
        last_dim = len(dims) - 2
        weights = {}

        def weight_of(name, number, right):
            weights[name] = Scatter(
                name, lefts[number], rights_of(right), dims, at, last_dim, first
            )
            return weights[name]

        half = width // 2
        downs = [weight_of("down", 0, "branch") for _ in range(2)]
        for number, (weight, earlier) in enumerate(zip(downs, ([], [downs[0]]))):
            weight.make(NO_COST, [one.sent for one in earlier], number * half, half)
            weight.other = shifted(weight.sent, dims, len(dims) - 1, 1)
        pieces = {0: downs[0].keep(0, half, NO_COST, [downs[1].sent])}

        def exchanged(weight, earlier):
            weight.make(NO_COST, earlier)
            weight.other = shifted(weight.sent, dims, len(dims) - 1, 1)
            return weight.sent

        def first_stage(earlier):
            feed_back(*pieces[0])
            vectors_of.append(grads["vectors"])
            pieces[1] = downs[1].keep(half, half, NO_COST, [grads["gate"]])
            return pieces[1]

        def second_stage(earlier):
            exchanged(weight_of("up", 1, "gate"), earlier)
            pieces[2] = weights["up"].keep(0, hidden // 2, NO_COST)
            return pieces[2]

        def third_stage(earlier):
            attend_back(*earlier)
            vectors_of.append(grads["vectors"])
            pieces[3] = weights["up"].keep(
                hidden // 2, hidden // 2, NO_COST, [grads["mixed"]]
            )
            return pieces[3]

        def fourth_stage(earlier):
            sent = exchanged(weight_of("qkv", 3, "mixed"), earlier)
            sent = weight_of("out", 2, "attended").make(NO_COST, [sent])
            pieces[4] = weights["qkv"].keep(0, 2 * width, NO_COST, [sent])
            return pieces[4]

        def fifth_stage(earlier):
            pieces[5] = weights["qkv"].keep(2 * width, width, NO_COST, earlier)
            pieces[6] = weights["out"].keep(0, width, NO_COST, pieces[5])
            return pieces[6]

        def projection_grad():
            total = product_tn(
                jnp.concatenate([state["result"] for state in states[:1:-1]]),
                jnp.concatenate([one["grad_embedded"] for one in back[:MICRO]]),
            ) * section_index.astype(WIDE)
            parts = jnp.swapaxes(total.reshape(2, count, -1, total.shape[1]), 0, 1)
            riding.append(Halved(parts, dims, at))
            return riding[-1]

        def vector_grads():
            riding.append(Whole(sum(vectors_of)))
            return riding[-1]

        riding = []
        sums = travels(
            pieces,
            7,
            list(reversed(range(last_dim + 1))),
            dims,
            at,
            {4: lambda: [weights["out"]]},
            {4: lambda: [projection_grad(), vector_grads()]},
            [first_stage, second_stage, third_stage, fourth_stage, fifth_stage],
        )
        proj_own, own_vectors = riding[0].value[0], riding[1].value
        grad_down, grad_up, grad_qkv = (
            jnp.concatenate(group, axis=1)[None] for group in (sums[0:2], sums[2:4], sums[4:6])
        )
        grad_out = sums[6][None]
    else:
        feed_back()
        vectors_of.append(grads["vectors"])
        attend_back()
        weight_grads = []
        for number, name in enumerate(("branch", "gate", "attended", "mixed")):
            left = jnp.concatenate([jnp.where(is_first, *pair) for pair in lefts[number]])
            right = [jnp.where(is_first, *pair) for pair in rights_of(name)]
            if number == 3:
                right = [jnp.swapaxes(value, 0, 1).reshape(ROWS, -1) for value in right]
            weight_grads.append(
                scatter_rows_plain(left, jnp.concatenate(right), dims, dp_index)[None]
            )
        grad_down, grad_up, grad_out, grad_qkv = weight_grads
        own_vectors = lax.psum(sum([*vectors_of, grads["vectors"]]), "dp")
        proj_total = product_tn(
            jnp.concatenate([state["result"] for state in states[:1:-1]]),
            jnp.concatenate([one["grad_embedded"] for one in back[:MICRO]]),
        ) * section_index.astype(WIDE)
        proj_own = summed(jnp.swapaxes(proj_total.reshape(2, count, -1, PROJ), 0, 1))
    grad_inputs = grads["grad_source"]
    proj_grad = jnp.where(is_first, from_behind(proj_own[0], "section", -1), proj_own[1])
    grad_qkv_b, grad_out_b, grad_gain1, grad_bias1, grad_up_b, grad_down_b, grad_gain2, grad_bias2 = (
        own_parts(
            own_vectors,
            [
                (first_row, rows, rows * width // count)
                for first_row, rows in (
                    (0, 3), (3, 1), (4, 1), (5, 1), (6, hidden // width), (10, 1), (11, 1), (12, 1)
                )
            ],
            dp_index,
        )
    )
    return (
        query_losses,
        activations,
        grad_inputs[None],
        grad_qkv,
        grad_qkv_b,
        grad_out,
        grad_out_b,
        grad_gain1,
        grad_bias1,
        grad_up,
        grad_up_b,
        grad_down,
        grad_down_b,
        grad_gain2,
        grad_bias2,
        proj_grad,
    )


def solution(mesh):
    in_specs = (
        P("dp", None),
        P("section", "dp", None),
        P("section", "dp"),
        P("section", "dp", None),
        P("section", "dp"),
        P("section", "dp"),
        P("section", "dp"),
        P("section", "dp", None),
        P("section", "dp"),
        P("section", "dp", None),
        P("section", "dp"),
        P("section", "dp"),
        P("section", "dp"),
        P("dp", None),
        P("dp", None),
        P(),
    )
    out_specs = (
        P("dp"),
        P("section", "dp", None),
        P("section", "dp", None),
        P("section", "dp", None),
        P("section", "dp"),
        P("section", "dp", None),
        P("section", "dp"),
        P("section", "dp"),
        P("section", "dp"),
        P("section", "dp", None),
        P("section", "dp"),
        P("section", "dp", None),
        P("section", "dp"),
        P("section", "dp"),
        P("section", "dp"),
        P(("section", "dp"), None),
    )
    return jax.shard_map(shards, mesh=mesh, in_specs=in_specs, out_specs=out_specs, check_vma=False)
```
